512 devices in a mesh: row: 4 (over x), col: 16 (over z_lo, y), layer: 8 (over z_hi, core).
Axes of the slice: x: 4, y: 4, z: 16 (z_hi: 4, z_lo: 4; z = z_hi * 4 + z_lo), core: 2. Of those that a mesh axis runs over, the one named last changes fastest.
Arguments:
- earlier_warming_amount: float32 [32, 512, 2048], P('layer', 'row', 'col'), may hold values from -2 to 2
- conductive_capability: float32 [32, 512, 2048], P('layer', 'row', 'col'), may hold values from 0.5 to 2
- thermal_mass_timewise: float32 [32, 512, 2048], P('layer', 'row', 'col'), may hold values from 0.5 to 2
- toggling_wattage_map: bfloat16 [512, 64, 4096], P(('row', 'col', 'layer')), may hold values from 0.049804688 to 1
- baseline_loss_wattage: bfloat16 [512, 64, 4096], P(('row', 'col', 'layer')), may hold values from 0.049804688 to 1
- receiving_panel: int32 [512, 64, 1], P(('row', 'col', 'layer')), may hold values from 0 to 63; in each aligned block of 64 rows (0 to 63, 64 to 127, ..., all dimensions but the last counted through in order) at most 4 rows name the same one
- subsquare_placement: int32 [512, 64], P(('row', 'col', 'layer')), may hold values from 0 to 3
- holder_chip_module: int32 [512, 64], P(('row', 'col', 'layer')), may hold values from 0 to 15, never falling along the last dimension, each value on 1 to 8 neighbouring positions
- module_tier_order: int32 [512, 16], P(('row', 'col', 'layer')), may hold values from 0 to 3
- warming_sensitivity: float32 [512, 16], P(('row', 'col', 'layer')), may hold values from 0.5 to 2
Outputs:
- new_temperature: float32 [32, 512, 2048], P('layer', 'row', 'col')
- supplied_wattage_density: float32 [32, 512, 2048], P('layer', 'row', 'col')
The draws below stay inside these ranges and needn't reach their ends.
Inputs may be any that keep to these rules, and one draw needn't show every extreme that they name: `receiving_panel`: the tile is numbered row tile times the number of column tiles plus column tile, inside the owning device's layer group; among the slots of one device at most 4 name the same tile, and exactly 4 do on some device in every draw. `subsquare_placement`: row-major over the tile's patch rows and patch columns. `holder_chip_module`: never falls along a device's slots; every block of a device has 1 to 8 slots.
All inputs are finite; a program needn't handle non-finite values.
Results may differ from the reference program's by a relative error of at most 0.0012.
Values may be sent and summed in bfloat16 or wider, within the bound.
No kernel may reach another device: no remote copies, remote signals or barrier semaphores. Data moves between devices by JAX's collectives and lax.ppermute only.
A program may use at most 64 MiB of HBM per device.

```python
import math
import jax
import jax.numpy as jnp
import numpy as np
from jax import lax

SUBSQUARE_EXTENT = 64
CR = 128
CC = 128
CL = 4
SWEEPS = 3
S = 64
NB_DEV = 16
CAP = 4
NLAY = 32
NROWS = 512
NCOLS = 2048
N_ROW = 4
N_COL = 16
N_LAYER = 8
DEVICES = 512


def draw_earlier_warming_amount(key, part):
    first_key, second_key = jax.random.split(jax.random.fold_in(key, 11))
    coarse_shape = (NLAY, NROWS // SUBSQUARE_EXTENT, NCOLS // SUBSQUARE_EXTENT)
    coarse = jax.random.uniform(first_key, coarse_shape, jnp.float32, -1.0, 1.0)
    fine = 0.3 * jnp.clip(jax.random.normal(second_key, (NLAY, NROWS, NCOLS), jnp.float32), -3.0, 3.0)
    spread_out = jnp.repeat(jnp.repeat(coarse, SUBSQUARE_EXTENT, axis=1), SUBSQUARE_EXTENT, axis=2)
    return spread_out + fine


def touch_ends(values, key, least, top_value):
    shape = values.shape
    place = [jax.random.randint(jax.random.fold_in(key, axis), (), 0, shape[axis]) for axis in range(len(shape))]
    values = values.at[tuple(place)].set(least)
    longest = shape.index(max(shape))
    place[longest] = (place[longest] + 1) % shape[longest]
    return values.at[tuple(place)].set(top_value)


def level_of(rng, shape, cuts, low, high):
    gain = 1.0
    for position, blocks in cuts:
        draws = jax.random.uniform(jax.random.fold_in(jax.random.fold_in(rng, 6), position), (blocks,), jnp.float32, low / len(cuts), high / len(cuts))
        gain = gain * jnp.repeat(jnp.exp(draws), shape[position] // blocks).reshape((-1,) + (1,) * (len(shape) - 1 - position))
    return gain


def split_up(count, total, reach, lean):
    loads = [(1 << 20) // math.isqrt(rank ** lean) + 1 for rank in range(2, count + 1)]
    rest, holding = total - reach - (count - 1), [1] * (count - 1)
    while rest > 0:
        free = [i for i in range(count - 1) if holding[i] < reach]
        mass, budget = sum([loads[i] for i in free]), rest
        for i in free:
            more = min(reach - holding[i], max(1, budget * loads[i] // mass), rest)
            holding[i] = holding[i] + more
            rest = rest - more
    return np.array([reach] + holding)


def ragged_sizes(stream_key, number_of, total, bound, slope):
    if number_of == 2:
        one = jax.random.randint(stream_key, (), max(1, total - bound), min(bound, total - 1) + 1)
        return jnp.stack([one, total - one])
    sizes = jnp.asarray(split_up(number_of, total, bound, slope), jnp.int32)
    pairs = (number_of - 1) // 2
    source_of, taker = sizes[1:1 + 2 * pairs:2], sizes[2:2 + 2 * pairs:2]
    margin = jnp.minimum(source_of - 1, bound - taker)
    shifted = jax.random.randint(jax.random.fold_in(stream_key, 1), (pairs,), 0, 1 << 20) % (margin + 1)
    sizes = sizes.at[1:1 + 2 * pairs:2].set(source_of - shifted).at[2:2 + 2 * pairs:2].set(taker + shifted)
    return sizes[jax.random.permutation(jax.random.fold_in(stream_key, 2), number_of)]


def routed_block(stream_key, own, number, rows, count, top, reach, skew):
    sequence = jax.random.permutation(stream_key, count)
    crowded, common = load_shares(count, rows * top, reach, skew, True), load_shares(count, rows * top, reach, skew, False)
    places = jnp.arange(count)

    def named(lengths, turn):
        used = int((lengths > 0).sum())
        fixed = max(1, used // 4)
        passed = fixed + (places - fixed + turn * (used - fixed)) % max(1, count - fixed)
        return jnp.zeros((count,), jnp.int32).at[sequence[jnp.where(places < fixed, places, passed)]].set(jnp.asarray(lengths, jnp.int32))

    lengths = jnp.where(number % 4 == 0, named(crowded, number // 4), named(common, number - number // 4 - 1))
    mixed = jax.random.permutation(jax.random.fold_in(own, 3), count)
    donor, taker = mixed[0:count // 2 * 2:2], mixed[1:count // 2 * 2:2]
    room = jnp.minimum(lengths[donor] - 1, reach - lengths[taker]) // 2
    room = jnp.where((donor == sequence[0]) | (taker == sequence[0]) | (lengths[taker] == 0), 0, jnp.maximum(room, 0))
    passed = jax.random.randint(jax.random.fold_in(own, 4), (count // 2,), 0, 1 << 20) % (room + 1)
    lengths = lengths.at[donor].add(-passed).at[taker].add(passed)
    members = jnp.searchsorted(jnp.cumsum(lengths), jnp.arange(rows * top), side="right").astype(jnp.int32)
    listing = members.reshape(top, rows).T
    listing = listing[jax.random.permutation(jax.random.fold_in(own, 1), rows)]
    turn = jax.random.randint(jax.random.fold_in(own, 2), (rows, 1), 0, top)
    return jnp.take_along_axis(listing, (jnp.arange(top)[None, :] + turn) % top, axis=1)


def load_shares(amount, total, most, skew, full):
    loads = [(1 << 20) // math.isqrt(rank ** skew) + 1 for rank in range(1, amount + 1)]
    largest = most if full else min(most, max(-(-total // amount), total * loads[0] // sum(loads)))
    least = 1 if total - largest >= amount - 1 else 0
    holding, rest = [largest] + [least] * (amount - 1), total - largest - least * (amount - 1)
    while rest > 0:
        free = [i for i in range(1, amount) if holding[i] < largest] or [i for i in range(1, amount) if holding[i] < most]
        whole, remaining = sum([loads[i] for i in free]), rest
        for i in free:
            more = min(most - holding[i], max(1, remaining * loads[i] // whole), rest)
            holding[i] = holding[i] + more
            rest = rest - more
    return np.array(holding)


def setup_inputs(seed: int = 0) -> dict:
    keys = jax.random.split(jax.random.key(seed), 11)
    earlier_warming_amount = draw_earlier_warming_amount(jax.random.fold_in(keys[10], 71), 0)
    conductive_capability = jnp.clip(jnp.exp(math.log(2.0) - 1.3862944 * jax.random.uniform(keys[1], (NLAY, NROWS, NCOLS), jnp.float32) ** level_of(keys[1], (NLAY, NROWS, NCOLS), ((0, 8), (1, 4), (2, 16)), -0.2, 0.2)), 0.5, 2.0)
    thermal_mass_timewise = jnp.clip(0.5 + 1.5 * jax.random.uniform(keys[2], (NLAY, NROWS, NCOLS), jnp.float32) ** level_of(keys[2], (NLAY, NROWS, NCOLS), ((0, 8), (1, 4), (2, 16)), -0.2, 0.2), 0.5, 2.0)
    toggling_wattage_map = jnp.clip(jnp.exp(math.log(1.0) - 2.9996462 * jax.random.uniform(keys[3], (DEVICES, S, SUBSQUARE_EXTENT * SUBSQUARE_EXTENT), jnp.float32) ** level_of(keys[3], (DEVICES, S, SUBSQUARE_EXTENT * SUBSQUARE_EXTENT), ((0, 512),), -0.2, 0.2)), 0.049804688, 1.0).astype(jnp.bfloat16)
    baseline_loss_wattage = jnp.clip(jnp.exp(math.log(1.0) - 2.9996462 * jax.random.uniform(keys[4], (DEVICES, S, SUBSQUARE_EXTENT * SUBSQUARE_EXTENT), jnp.float32) ** level_of(keys[4], (DEVICES, S, SUBSQUARE_EXTENT * SUBSQUARE_EXTENT), ((0, 512),), -0.2, 0.2)), 0.049804688, 1.0).astype(jnp.bfloat16)
    receiving_panel_keys = jax.random.split(jax.random.fold_in(keys[5], 1), DEVICES * S // S)
    receiving_panel_turns = jax.random.permutation(jax.random.fold_in(keys[5], 3), DEVICES * S // S)
    receiving_panel = jax.vmap(lambda own, number: routed_block(jax.random.fold_in(keys[5], 2), own, number, S, N_ROW * N_COL, 1, CAP, 2))(receiving_panel_keys, receiving_panel_turns).reshape((DEVICES, S, 1))
    subsquare_placement = touch_ends(jax.random.randint(keys[6], (DEVICES, S), 0, (CR // SUBSQUARE_EXTENT) * (CC // SUBSQUARE_EXTENT)), jax.random.fold_in(keys[6], 1), 0, ((CR // SUBSQUARE_EXTENT) * (CC // SUBSQUARE_EXTENT)) - 1).astype(jnp.int32)
    holder_chip_module = jax.vmap(lambda own: jnp.searchsorted(jnp.cumsum(ragged_sizes(own, NB_DEV, S, 2 * S // NB_DEV, 2)), jnp.arange(S), side="right"))(jax.random.split(keys[7], DEVICES)).reshape((DEVICES, S)).astype(jnp.int32)
    module_tier_order = touch_ends(jax.random.randint(keys[8], (DEVICES, NB_DEV), 0, CL), jax.random.fold_in(keys[8], 1), 0, CL - 1).astype(jnp.int32)
    warming_sensitivity = jnp.clip(jnp.exp(math.log(2.0) - 1.3862944 * jax.random.uniform(keys[9], (DEVICES, NB_DEV), jnp.float32) ** level_of(keys[9], (DEVICES, NB_DEV), ((0, 512),), -0.2, 0.2)), 0.5, 2.0)
    return dict(earlier_warming_amount=earlier_warming_amount, conductive_capability=conductive_capability, thermal_mass_timewise=thermal_mass_timewise, toggling_wattage_map=toggling_wattage_map, baseline_loss_wattage=baseline_loss_wattage, receiving_panel=receiving_panel, subsquare_placement=subsquare_placement, holder_chip_module=holder_chip_module, module_tier_order=module_tier_order, warming_sensitivity=warming_sensitivity)


eig_low = 0.1
eig_high = 2.0


def neighbours(padded):
    return [padded[2:, 1:-1, 1:-1], padded[:-2, 1:-1, 1:-1], padded[1:-1, 2:, 1:-1],
            padded[1:-1, :-2, 1:-1], padded[1:-1, 1:-1, 2:], padded[1:-1, 1:-1, :-2]]


def face_terms(padded_cond):
    center = padded_cond[1:-1, 1:-1, 1:-1]
    return [0.5 * (center + beside) for beside in neighbours(padded_cond)]


def diagonal_of(thermal_mass_timewise, nearby_conductance_factors):
    running = thermal_mass_timewise
    for face_term in nearby_conductance_factors:
        running = running + face_term
    return running


def linear_mapping_result(padded, nearby_conductance_factors, linear_pivot_coefficients):
    result = linear_pivot_coefficients * padded[1:-1, 1:-1, 1:-1]
    for face_term, beside in zip(nearby_conductance_factors, neighbours(padded)):
        result = result - face_term * beside
    return result


def reference(earlier_warming_amount, conductive_capability, thermal_mass_timewise, toggling_wattage_map, baseline_loss_wattage, receiving_panel, subsquare_placement, holder_chip_module, module_tier_order, warming_sensitivity):
    third_axis_extent, first_axis_extent, second_axis_extent = earlier_warming_amount.shape
    subsquares_eastward = first_axis_extent // SUBSQUARE_EXTENT
    subsquares_northward = second_axis_extent // SUBSQUARE_EXTENT
    slots_all = DEVICES * S
    owner = jnp.arange(slots_all, dtype=jnp.int32) // S
    owner_group = owner % N_LAYER
    target = receiving_panel.reshape(slots_all).astype(jnp.int32)
    local_block = holder_chip_module.reshape(slots_all).astype(jnp.int32)
    global_block = owner * NB_DEV + local_block
    die_layer = module_tier_order.reshape(DEVICES * NB_DEV)[global_block] + owner_group * CL
    offsets = subsquare_placement.reshape(slots_all)
    patch_row = (target // N_COL) * (CR // SUBSQUARE_EXTENT) + offsets // (CC // SUBSQUARE_EXTENT)
    patch_col = (target % N_COL) * (CC // SUBSQUARE_EXTENT) + offsets % (CC // SUBSQUARE_EXTENT)
    patch_index = ((die_layer * subsquares_eastward + patch_row) * subsquares_northward + patch_col).astype(jnp.int32)
    subsquare_averaged = earlier_warming_amount.reshape(third_axis_extent, subsquares_eastward, SUBSQUARE_EXTENT, subsquares_northward, SUBSQUARE_EXTENT).mean(axis=(2, 4)).reshape(-1)
    slot_means = subsquare_averaged[patch_index]
    blocks_all = DEVICES * NB_DEV
    block_sums = jax.ops.segment_sum(slot_means, global_block, num_segments=blocks_all)
    block_sizes = jax.ops.segment_sum(jnp.ones((slots_all,), jnp.float32), global_block, num_segments=blocks_all)
    factor = jnp.exp(warming_sensitivity.reshape(blocks_all) * (block_sums / block_sizes))
    slot_power = toggling_wattage_map.reshape(slots_all, SUBSQUARE_EXTENT * SUBSQUARE_EXTENT).astype(jnp.float32) + factor[global_block][:, None] * baseline_loss_wattage.reshape(slots_all, SUBSQUARE_EXTENT * SUBSQUARE_EXTENT).astype(jnp.float32)
    slot_power = lax.optimization_barrier(slot_power.astype(jnp.bfloat16)).astype(jnp.float32)
    footprint_wattage = jax.ops.segment_sum(slot_power, patch_index, num_segments=third_axis_extent * subsquares_eastward * subsquares_northward)
    supplied_wattage_density = footprint_wattage.reshape(third_axis_extent, subsquares_eastward, subsquares_northward, SUBSQUARE_EXTENT, SUBSQUARE_EXTENT).transpose(0, 1, 3, 2, 4).reshape(third_axis_extent, first_axis_extent, second_axis_extent)
    nearby_conductance_factors = face_terms(jnp.pad(conductive_capability, 1))
    linear_pivot_coefficients = diagonal_of(thermal_mass_timewise, nearby_conductance_factors)
    middle = (eig_low + eig_high) / 2.0
    spread = (eig_high - eig_low) / 2.0
    ratio_sigma = middle / spread
    weight_now = 1.0 / ratio_sigma
    iterate_guess = earlier_warming_amount
    remaining_imbalance = thermal_mass_timewise * earlier_warming_amount + supplied_wattage_density - linear_mapping_result(jnp.pad(iterate_guess, 1), nearby_conductance_factors, linear_pivot_coefficients)
    direction = remaining_imbalance / (linear_pivot_coefficients * middle)
    for sweep in range(SWEEPS):
        iterate_guess = iterate_guess + direction
        if sweep < SWEEPS - 1:
            remaining_imbalance = remaining_imbalance - linear_mapping_result(jnp.pad(direction, 1), nearby_conductance_factors, linear_pivot_coefficients)
            weight_new = 1.0 / (2.0 * ratio_sigma - weight_now)
            direction = weight_new * weight_now * direction + (2.0 * weight_new / spread) * (remaining_imbalance / linear_pivot_coefficients)
            weight_now = weight_new
    return iterate_guess, supplied_wattage_density
```

```python
import jax
import jax.numpy as jnp
from jax import lax
from jax.experimental import pallas as pl
from jax.experimental.pallas import tpu as pltpu
from jax.sharding import Mesh
from jax.sharding import PartitionSpec as P

SWEEPS = 3
eig_low = 0.1
eig_high = 2.0

LAYER = ("zhi", "core")
COL = ("zlo", "y")
CUBE = ("row", "zlo", "y")
PLANE = ("row", "y")

F32, BF16, I32 = jnp.float32, jnp.bfloat16, jnp.int32


def params(mib):
    return pltpu.CompilerParams(vmem_limit_bytes=mib * 2**20)


def iota(shape, dim):
    return lax.broadcasted_iota(I32, shape, dim)


def as_column(row):
    n = row.shape[1]
    return jnp.sum(jnp.where(iota((n, n), 0) == iota((n, n), 1), row, 0), axis=1, keepdims=True)


def slot_rows(panel, place, holder, tier):
    layer = jnp.sum(jnp.where(iota((16, 64), 0) == holder, as_column(tier), 0), axis=0, keepdims=True)
    pos = layer * 4 + place
    ident = ((panel >> 2) & 3) * 16 + pos
    column = (panel >> 4) * 4 + (panel & 3)
    same = (as_column(column) == column) & (iota((64, 64), 0) < iota((64, 64), 1))
    rank = jnp.sum(same.astype(I32), axis=0, keepdims=True)
    return pos, ident, column * 16 + rank


def message_kernel(temp, panel, place, holder, tier, out):
    _, ident, dest = slot_rows(panel[...], place[...], holder[...], tier[...])
    sums = jnp.sum(temp[...].reshape(8, 64, 128), axis=1)
    lane = iota((8, 128), 1)
    first = jnp.sum(jnp.where(lane < 64, sums, 0.0), axis=1, keepdims=True)
    second = jnp.sum(jnp.where(lane < 64, 0.0, sums), axis=1, keepdims=True)
    at = iota((8, 128), 0) * 2
    means = jnp.where(lane == at, first, jnp.where(lane == at + 1, second, 0.0))
    means = jnp.sum(means, axis=0, keepdims=True) * (1.0 / 4096.0)
    code = (dest * 64 + ident).astype(F32)
    row = jnp.where(iota((1, 128), 1) < 64, means, jnp.concatenate([code, code], axis=1))
    out[...] = jnp.broadcast_to(row, (64, 128))


def placing_kernel(panel, place, holder, tier, placing, columns):
    pos, _, dest = slot_rows(panel[...], place[...], holder[...], tier[...])
    placing[...] = jnp.where(iota((256, 64), 0) == dest, 1.0, 0.0).astype(BF16)
    lane = iota((64, 128), 1)
    columns[...] = jnp.where(
        lane == 0,
        as_column(panel[...]),
        jnp.where(lane == 1, as_column(pos), as_column(holder[...])),
    )


def power_kernel(messages, columns, warming, toggling, baseline, placing, out):
    tile, pos, holder = (columns[:, k : k + 1] for k in range(3))
    pick = jnp.where(iota((64, 64), 1) == tile, 1.0, 0.0)
    means = jnp.dot(pick, messages[...], precision=lax.Precision.HIGHEST, preferred_element_type=F32)
    slot_mean = jnp.sum(jnp.where(iota((64, 128), 1) == pos, means, 0.0), axis=1, keepdims=True)
    member = iota((64, 16), 1) == holder
    total = jnp.sum(jnp.where(member, slot_mean, 0.0), axis=0, keepdims=True)
    count = jnp.sum(jnp.where(member, 1.0, 0.0), axis=0, keepdims=True)
    leak = jnp.exp(warming[...] * (total / count))
    factor = jnp.sum(jnp.where(member, leak, 0.0), axis=1, keepdims=True)
    width = 512
    for k in range(4096 // width):
        at = pl.ds(k * width, width)
        power = toggling[:, at].astype(F32) + factor * baseline[:, at].astype(F32)
        out[:, at] = jnp.dot(placing[...], power.astype(BF16), preferred_element_type=F32).astype(BF16)


def selector_kernel(messages, out):
    mine = lax.axis_index("row") * 4 + lax.axis_index("y")
    plane = lax.axis_index("zlo")
    code = jnp.concatenate(
        [messages[pl.ds(r * 16 + plane * 4, 4), :] for r in range(4)], axis=0
    )
    code = jnp.where(iota((16, 128), 1) < 64, -1.0, code).astype(I32)
    dest, ident = code >> 6, code & 63
    lane = iota((16, 256), 1)
    ids = jnp.zeros((16, 256), I32)
    for r in range(16):
        hit = jnp.sum(jnp.where(dest == mine * 16 + r, ident + 1, 0), axis=1, keepdims=True)
        ids = jnp.where((lane & 15) == r, hit, ids)
    ids = jnp.sum(jnp.where((lane >> 4) == iota((16, 256), 0), ids, 0), axis=0, keepdims=True)
    out[...] = jnp.where(iota((64, 256), 0) + 1 == ids, 1.0, 0.0).astype(BF16)


def combine_kernel(selector, received, out):
    width = 512
    for k in range(4096 // width):
        at = pl.ds(k * width, width)
        out[:, at] = jnp.dot(selector[...], received[:, at], preferred_element_type=F32).astype(BF16)


def unpack_kernel(parts, out, turned):
    for k in range(32):
        at = pl.ds(k * 128, 128)
        whole = parts[0, :, at].astype(F32)
        for z in range(1, 4):
            whole = whole + parts[z, :, at].astype(F32)
        turned[pl.ds(k * 16, 16), :] = whole
    low = iota((32, 128), 1) < 64
    for layer in range(4):
        for r in range(2):
            left = turned[pl.ds(layer * 4 + r * 2, 32, stride=16), :]
            right = turned[pl.ds(layer * 4 + r * 2 + 1, 32, stride=16), :]
            base = layer * 128 + r * 64
            out[pl.ds(base, 32, stride=2), :] = jnp.where(low, left, pltpu.roll(right, 64, 1))
            out[pl.ds(base + 1, 32, stride=2), :] = jnp.where(low, pltpu.roll(left, 64, 1), right)


def call(kernel, shape, args, mib=16, scratch=()):
    return pl.pallas_call(
        kernel,
        out_shape=shape,
        in_specs=[pl.BlockSpec(memory_space=pltpu.VMEM)] * len(args),
        out_specs=jax.tree.map(lambda _: pl.BlockSpec(memory_space=pltpu.VMEM), shape),
        scratch_shapes=list(scratch),
        compiler_params=params(mib),
    )(*args)


def sds(shape, dtype):
    return jax.ShapeDtypeStruct(shape, dtype)


def with_halo(array, sides, width):
    edges = {}
    for axis, dim in sides:
        count, length = (lax.axis_size(axis), array.shape[dim])
        up = [(i, (i + 1) % count) for i in range(count - 1)]
        last = lax.slice_in_dim(array, length - width, length, axis=dim)
        leading = lax.slice_in_dim(array, 0, width, axis=dim)
        edges[dim] = (
            lax.ppermute(last, axis, up),
            lax.ppermute(leading, axis, [(b, a) for a, b in up]),
        )
    done = []
    for _, dim in sides:
        low, high = edges[dim]
        around = [(width, width) if d in done else (0, 0) for d in range(array.ndim)]
        array = jnp.concatenate([jnp.pad(low, around), array, jnp.pad(high, around)], axis=dim)
        done.append(dim)
    return array


def neighbours(padded):
    return [
        padded[2:, 1:-1, 1:-1],
        padded[:-2, 1:-1, 1:-1],
        padded[1:-1, 2:, 1:-1],
        padded[1:-1, :-2, 1:-1],
        padded[1:-1, 1:-1, 2:],
        padded[1:-1, 1:-1, :-2],
    ]


def face_terms(padded_cond):
    center = padded_cond[1:-1, 1:-1, 1:-1]
    return [0.5 * (center + beside) for beside in neighbours(padded_cond)]


def linear_mapping_result(padded, faces, diagonal):
    result = diagonal * padded[1:-1, 1:-1, 1:-1]
    for face_term, beside in zip(faces, neighbours(padded)):
        result = result - face_term * beside
    return result


def shards(temp, cond, mass, toggling, baseline, panel, place, holder, tier, warming):
    panel = panel.reshape(1, 64)
    slots = (panel, place, holder, tier)
    message = call(message_kernel, sds((64, 128), F32), (temp, *slots))
    messages = lax.all_to_all(message.reshape(64, 1, 128), CUBE, split_axis=0, concat_axis=0, tiled=True)
    messages = messages.reshape(64, 128)
    placing, columns = call(placing_kernel, (sds((256, 64), BF16), sds((64, 128), I32)), slots)
    send = call(
        power_kernel,
        sds((256, 4096), BF16),
        (messages, columns, warming, toggling[0], baseline[0], placing),
    )
    received = lax.all_to_all(send.reshape(16, 16, 4096), PLANE, split_axis=0, concat_axis=0, tiled=True)
    selector = call(selector_kernel, sds((64, 256), BF16), (messages,))
    partial = call(combine_kernel, sds((64, 4096), BF16), (selector, received.reshape(256, 4096)))
    parts = lax.all_to_all(partial.reshape(4, 16, 4096), "zlo", split_axis=0, concat_axis=0, tiled=True)
    density = call(
        unpack_kernel, sds((512, 128), F32), (parts,), scratch=[pltpu.VMEM((512, 128), F32)]
    ).reshape(4, 128, 128)

    middle = (eig_low + eig_high) / 2.0
    spread = (eig_high - eig_low) / 2.0
    ratio_sigma = middle / spread
    weight_now = 1.0 / ratio_sigma
    both_sides = with_halo(jnp.stack([temp, cond]), (("row", 2), (COL, 3), (LAYER, 1)), 1)
    faces = face_terms(both_sides[1])
    diagonal = mass
    for face in faces:
        diagonal = diagonal + face
    guess = temp
    imbalance = mass * temp + density - linear_mapping_result(both_sides[0], faces, diagonal)
    direction = imbalance / (diagonal * middle)
    for sweep in range(SWEEPS):
        guess = guess + direction
        if sweep < SWEEPS - 1:
            padded = with_halo(direction, (("row", 1), (COL, 2), (LAYER, 0)), 1)
            imbalance = imbalance - linear_mapping_result(padded, faces, diagonal)
            weight_new = 1.0 / (2.0 * ratio_sigma - weight_now)
            direction = weight_new * weight_now * direction + 2.0 * weight_new / spread * (
                imbalance / diagonal
            )
            weight_now = weight_new
    return guess, density


def solution(mesh):
    fine = Mesh(mesh.devices.reshape(4, 4, 4, 4, 2), ("row", "zlo", "y", "zhi", "core"))
    grid = P(LAYER, "row", COL)
    slot = ("row", "zlo", "y", "zhi", "core")
    return jax.shard_map(
        shards,
        mesh=fine,
        in_specs=(
            grid,
            grid,
            grid,
            P(slot, None, None),
            P(slot, None, None),
            P(slot, None, None),
            P(slot, None),
            P(slot, None),
            P(slot, None),
            P(slot, None),
        ),
        out_specs=(grid, grid),
        check_vma=False,
    )
```

```python
import jax
import jax.numpy as jnp
from jax import lax
from jax.experimental import pallas as pl
from jax.experimental.pallas import tpu as pltpu
from jax.sharding import Mesh
from jax.sharding import PartitionSpec as P

eig_low = 0.1
eig_high = 2.0

LAYER = ("zhi", "core")
COL = ("zlo", "y")
CUBE = ("row", "zlo", "y")
PLANE = ("row", "y")

F32, BF16, I32 = jnp.float32, jnp.bfloat16, jnp.int32


def iota(shape, dim):
    return lax.broadcasted_iota(I32, shape, dim)


def as_column(row):
    n = row.shape[1]
    return jnp.sum(jnp.where(iota((n, n), 0) == iota((n, n), 1), row, 0), axis=1, keepdims=True)


def slot_rows(panel, place, holder, tier):
    layer = jnp.sum(jnp.where(iota((16, 64), 0) == holder, as_column(tier), 0), axis=0, keepdims=True)
    pos = layer * 4 + place
    ident = ((panel >> 2) & 3) * 16 + pos
    column = (panel >> 4) * 4 + (panel & 3)
    same = (as_column(column) == column) & (iota((64, 64), 0) < iota((64, 64), 1))
    rank = jnp.sum(same.astype(I32), axis=0, keepdims=True)
    return pos, ident, column * 16 + rank


def message_kernel(temp, panel, place, holder, tier, out, meta, temp_v, panel_v, place_v, holder_v, tier_v, sems):
    pairs = [(panel, panel_v), (place, place_v), (holder, holder_v), (tier, tier_v), (temp, temp_v)]
    copies = [pltpu.make_async_copy(a, b, sems.at[i]) for i, (a, b) in enumerate(pairs)]
    for copy in copies:
        copy.start()
    for copy in copies[:4]:
        copy.wait()
    panel_row, holder_row = panel_v[...], holder_v[...]
    pos, ident, dest = slot_rows(panel_row, place_v[...], holder_row, tier_v[...])
    for k, row in enumerate((panel_row, pos, dest, holder_row)):
        meta[k : k + 1, :] = jnp.concatenate([row, row], axis=1)
    meta[4:8, :] = jnp.zeros((4, 128), I32)
    code = (dest * 64 + ident).astype(F32)
    copies[4].wait()
    sums = jnp.sum(temp_v[...].reshape(8, 64, 128), axis=1)
    lane = iota((8, 128), 1)
    first = jnp.sum(jnp.where(lane < 64, sums, 0.0), axis=1, keepdims=True)
    second = jnp.sum(jnp.where(lane < 64, 0.0, sums), axis=1, keepdims=True)
    at = iota((8, 128), 0) * 2
    means = jnp.where(lane == at, first, jnp.where(lane == at + 1, second, 0.0))
    means = jnp.sum(means, axis=0, keepdims=True) * (1.0 / 4096.0)
    row = jnp.where(iota((1, 128), 1) < 64, means, jnp.concatenate([code, code], axis=1))
    out[...] = jnp.broadcast_to(row, (64, 128))


def placing_kernel(meta, toggling, baseline, warming, placing, columns, toggling_v, baseline_v, warming_v, sems):
    pairs = [(toggling, toggling_v), (baseline, baseline_v), (warming, warming_v)]
    copies = [pltpu.make_async_copy(a, b, sems.at[i]) for i, (a, b) in enumerate(pairs)]
    for copy in copies:
        copy.start()
    panel, pos, dest, holder = (meta[k : k + 1, 0:64] for k in range(4))
    x, y, rank = panel >> 4, panel & 3, dest & 15
    lower, right = (pos >> 1) & 1, pos & 1
    next_x = x + lower * 2 - 1
    next_y = (y + right * 2 + 3) & 3
    inside = (next_x >= 0) & (next_x <= 3)
    targets = (
        dest,
        jnp.where(inside, (next_x * 4 + y) * 16 + rank, -1),
        (x * 4 + next_y) * 16 + rank,
        jnp.where(inside, (next_x * 4 + next_y) * 16 + rank, -1),
    )
    for k, target in enumerate(targets):
        placing[pl.ds(k * 256, 256), :] = jnp.where(iota((256, 64), 0) == target, 1.0, 0.0).astype(BF16)
    lane = iota((64, 128), 1)
    columns[...] = jnp.where(
        lane == 0, as_column(panel), jnp.where(lane == 1, as_column(pos), as_column(holder))
    )
    for copy in copies:
        copy.wait()


def power_kernel(messages, columns, warming, toggling, baseline, placing, out, sent, sems):
    tile, pos, holder = (columns[:, k : k + 1] for k in range(3))
    lower, right = (pos >> 1) & 1, pos & 1
    pick = jnp.where(iota((64, 64), 1) == tile, 1.0, 0.0)
    means = jnp.dot(pick, messages[...], precision=lax.Precision.HIGHEST, preferred_element_type=F32)
    lane = iota((64, 128), 1)
    slot_mean = jnp.sum(jnp.where(lane == pos, means, 0.0), axis=1, keepdims=True)
    member = iota((64, 16), 1) == holder
    total = jnp.sum(jnp.where(member, slot_mean, 0.0), axis=0, keepdims=True)
    count = jnp.sum(jnp.where(member, 1.0, 0.0), axis=0, keepdims=True)
    leak = jnp.exp(warming[...] * (total / count))
    factor = jnp.sum(jnp.where(member, leak, 0.0), axis=1, keepdims=True)

    def place(kind, values):
        at = placing[kind * 256 : (kind + 1) * 256, :]
        return jnp.dot(at, values.astype(BF16), preferred_element_type=F32).astype(BF16)

    copies = []

    def send(start, width):
        at = pl.ds(start, width)
        copy = pltpu.make_async_copy(sent.at[:, at], out.at[:, at], sems.at[len(copies)])
        copy.start()
        copies.append(copy)

    edge = ((lane & 63) >> 1) == right * 31
    sides = jnp.zeros((64, 128), F32)
    width = 512
    for k in range(8):
        at = pl.ds(k * width, width)
        power = (toggling[:, at].astype(F32) + factor * baseline[:, at].astype(F32)).astype(BF16)
        sent[:, at] = place(0, power)
        send(k * width, width)
        power = power.astype(F32)
        for t in range(4):
            piece = power[:, t * 128 : (t + 1) * 128]
            shift = 2 * (4 * k + t)
            kept = jnp.where(edge, piece, 0.0)
            sides = sides + (pltpu.roll(kept, shift, 1) if shift else kept)
            if k == 0 and t == 0:
                top = piece
    rows = jnp.where(lower == 0, top, piece)
    sides = jnp.where(right == 0, sides, pltpu.roll(sides, 66, 1))
    corner = jnp.sum(jnp.where(lane == lower * 64 + right * 63, rows, 0.0), axis=1, keepdims=True)
    quarter = (1 - lower) * 2 + 1 - right
    both = jnp.concatenate([jnp.where(lower == 1, rows, 0.0), jnp.where(lower == 0, rows, 0.0)], axis=1)
    sent[:, 4096:4352] = place(1, both)
    both = jnp.concatenate([jnp.where(right == 1, sides, 0.0), jnp.where(right == 0, sides, 0.0)], axis=1)
    sent[:, 4352:4608] = place(2, both)
    sent[:, 4608:4736] = place(3, jnp.where(lane == quarter, corner, 0.0))
    send(4096, 640)
    for copy in copies:
        copy.wait()


def selector_kernel(messages, out):
    x, y = lax.axis_index("row"), lax.axis_index("y")
    plane = lax.axis_index("zlo")
    code = jnp.concatenate([messages[pl.ds(r * 16 + plane * 4, 4), :] for r in range(4)], axis=0)
    code = jnp.where(iota((16, 128), 1) < 64, -1.0, code).astype(I32)
    dest, ident = code >> 6, code & 63
    lane = iota((16, 256), 1)

    def idents(dx, dy):
        base = ((x + dx) * 4 + ((y + dy + 4) & 3)) * 16
        ids = jnp.zeros((16, 256), I32)
        for r in range(16):
            hit = jnp.sum(jnp.where(dest == base + r, ident + 1, 0), axis=1, keepdims=True)
            ids = jnp.where((lane & 15) == r, hit, ids)
        ids = jnp.sum(jnp.where((lane >> 4) == iota((16, 256), 0), ids, 0), axis=0, keepdims=True) - 1
        turn = jnp.where(y == 0, 1, 0) if dy < 0 else jnp.where(y == 3, -1, 0) if dy > 0 else 0
        return ids, (ids >> 4) + turn, (ids >> 2) & 3, (ids >> 1) & 1, ids & 1

    def put(k, ids, target):
        out[pl.ds(k * 64, 64), :] = jnp.where(
            (iota((64, 256), 0) == target) & (ids >= 0), 1.0, 0.0
        ).astype(BF16)

    ids, *_ = idents(0, 0)
    put(0, ids, ids)
    for k, dx in enumerate((-1, 1)):
        ids, z, layer, _, pc = idents(dx, 0)
        put(1 + k, ids, z * 16 + k * 8 + layer * 2 + pc)
    for k, dy in enumerate((-1, 1)):
        ids, z, layer, pr, _ = idents(0, dy)
        put(3 + k, ids, z * 16 + k * 8 + layer * 2 + pr)
    for k in range(4):
        ids, z, layer, _, _ = idents((k >> 1) * 2 - 1, (k & 1) * 2 - 1)
        put(5 + k, ids, z * 16 + layer)


def combine_kernel(selector, received, out):
    def add(k, start, width):
        return jnp.dot(
            selector[k * 64 : (k + 1) * 64, :],
            received[:, start : start + width],
            preferred_element_type=F32,
        )

    for k in range(8):
        out[:, k * 512 : (k + 1) * 512] = add(0, k * 512, 512)
    out[:, 4096:4224] = add(1, 4096, 128) + add(2, 4224, 128)
    out[:, 4224:4352] = add(3, 4352, 128) + add(4, 4480, 128)
    lane = iota((64, 128), 1)
    corners = jnp.zeros((64, 128), F32)
    for k in range(4):
        corners = jnp.where(lane == k, add(5 + k, 4608, 128), corners)
    out[:, 4352:4480] = corners


def unpack_kernel(whole, density, main, side, up, down, turned):
    for k in range(32):
        turned[k * 16 : (k + 1) * 16, :] = whole[:, k * 128 : (k + 1) * 128]
    low = iota((32, 128), 1) < 64
    lane = iota((64, 128), 1)
    low_row = iota((1, 128), 1) < 64
    lane16, row16 = iota((16, 128), 1), iota((16, 128), 0)
    rows, columns, corners = whole[:, 4096:4224], whole[:, 4224:4352], whole[:, 4352:4480]
    cell = iota((64, 128), 0)
    turn = []
    for c in range(2):
        pick = jnp.where(lane == (cell & 1) * 64 + (cell - (cell & 1)) + c, 1.0, 0.0)
        turn.append(
            lax.dot_general(
                pick, columns, (((1,), (1,)), ((), ())),
                precision=lax.Precision.HIGHEST, preferred_element_type=F32,
            )
        )
    for layer in range(4):
        base = layer * 144
        for r in range(2):
            left = turned[pl.ds(layer * 4 + r * 2, 32, stride=16), :]
            right = turned[pl.ds(layer * 4 + r * 2 + 1, 32, stride=16), :]
            at = base + r * 64
            main[pl.ds(at, 32, stride=2), :] = jnp.where(low, left, pltpu.roll(right, 64, 1))
            main[pl.ds(at + 1, 32, stride=2), :] = jnp.where(low, pltpu.roll(left, 64, 1), right)
            k = layer * 2 + r
            strip = jnp.where(lane == 0, turn[0][:, 8 + k : 9 + k], 0.0)
            strip = jnp.where(lane == 1, turn[1][:, 8 + k : 9 + k], strip)
            strip = jnp.where(lane == 126, turn[0][:, k : k + 1], strip)
            side[at : at + 64, :] = jnp.where(lane == 127, turn[1][:, k : k + 1], strip)
        block = jnp.zeros((16, 128), F32)
        for kind, first_row in ((0, 14), (1, 0)):
            k = kind * 8 + layer * 2
            a, b = rows[k : k + 1, :], rows[k + 1 : k + 2, :]
            first = jnp.where(low_row, a, pltpu.roll(b, 64, 1))
            second = jnp.where(low_row, pltpu.roll(a, 64, 1), b)
            block = jnp.where(row16 == first_row, first, block)
            block = jnp.where(row16 == first_row + 1, second, block)
        main[base + 128 : base + 144, :] = block
        block = jnp.zeros((16, 128), F32)
        for k, (r, at_lane) in enumerate(((15, 127), (15, 0), (0, 127), (0, 0))):
            value = corners[layer : layer + 1, k : k + 1]
            block = jnp.where((row16 == r) & (lane16 == at_lane), value, block)
        side[base + 128 : base + 144, :] = block
        density[layer * 128 : (layer + 1) * 128, :] = main[base : base + 128, :]
    for out, first in ((up, 288), (down, 0)):
        out[0:288, :] = main[first : first + 288, :].astype(BF16)
        second = side[first + 144 : first + 288, :]
        out[288:432, :] = (side[first : first + 144, :] + pltpu.roll(second, 4, 1)).astype(BF16)


def gather_kernel(temp, cond, mass, lo, hi, above, below, out, to_left, to_right, own, sems):
    copies = [pltpu.make_async_copy(a, own.at[i], sems.at[i]) for i, a in enumerate((temp, cond, mass))]
    for copy in copies:
        copy.start()
    over, under = above[...].astype(F32), below[...].astype(F32)
    lane = iota((144, 128), 1)
    left, right = jnp.zeros((144, 128), F32), jnp.zeros((144, 128), F32)
    for copy in copies:
        copy.wait()
    for a in range(3):
        for layer in range(10):
            i = a * 10 + layer
            if layer < 3:
                source = lo[3 * a + layer].astype(F32)
            elif layer < 7:
                source = own[a, layer - 3]
            else:
                source = hi[3 * a + layer - 7].astype(F32)
            piece = jnp.concatenate([source, under[8 * i : 8 * i + 8], over[8 * i : 8 * i + 8]], axis=0)
            out[i] = piece
            base = a * 40 + layer * 4
            here = (lane >= base) & (lane < base + 3)
            left = jnp.where(here, pltpu.roll(piece, base, 1) if base else piece, left)
            right = jnp.where(here, pltpu.roll(piece, base + 3, 1), right)
    to_left[...] = left.astype(BF16)
    to_right[...] = right.astype(BF16)


def turned_by(x, shift, axis):
    return pltpu.roll(x, shift % x.shape[axis], axis)


def around(face_row, face_col, v):
    return (
        face_row * turned_by(v, -1, 0)
        + turned_by(face_row * v, 1, 0)
        + face_col * turned_by(v, -1, 1)
        + turned_by(face_col * v, 1, 1)
    )


def operator_kernel(grids, from_left, from_right, face_layer, face_row, face_col, inverse, residual, wide):
    left, right = from_left[...].astype(F32), from_right[...].astype(F32)
    lane = iota((144, 128), 1)
    for a in range(3):
        for layer in range(10):
            i, base = a * 10 + layer, a * 40 + layer * 4
            high = turned_by(right, -base, 1) if base else right
            side = jnp.where(lane < 3, high, jnp.where(lane >= 125, turned_by(left, 125 - base, 1), 0.0))
            wide[i, :, 0:128] = grids[i]
            wide[i, :, 128:256] = side
    for layer in range(9):
        face_layer[layer] = 0.5 * (wide[10 + layer] + wide[11 + layer])
    for layer in range(1, 9):
        temp, cond, mass = (wide[a * 10 + layer] for a in range(3))
        rows = 0.5 * (cond + turned_by(cond, -1, 0))
        cols = 0.5 * (cond + turned_by(cond, -1, 1))
        face_row[layer - 1] = rows
        face_col[layer - 1] = cols
        after, before = face_layer[layer], face_layer[layer - 1]
        diagonal = mass + after + before + rows + turned_by(rows, 1, 0) + cols + turned_by(cols, 1, 1)
        share = after * wide[layer + 1] + before * wide[layer - 1] + around(rows, cols, temp)
        residual[layer - 1] = mass * temp + (share - diagonal * temp)
        inverse[layer - 1] = jnp.where(mass > 0.0, 1.0 / diagonal, 0.0)


MIDDLE = (eig_low + eig_high) / 2.0
SPREAD = (eig_high - eig_low) / 2.0
W0 = SPREAD / MIDDLE
W1 = 1.0 / (2.0 * MIDDLE / SPREAD - W0)
W2 = 1.0 / (2.0 * MIDDLE / SPREAD - W1)


def sweep_kernel(main, side, lo, hi, grids, face_layer, face_row, face_col, inverse, residual, out, d0, d1, rest):
    lane = iota((144, 128), 1)
    kept = (lane < 2) | (lane >= 126)

    def supplied(i):
        if 3 <= i <= 6:
            at = (i - 3) * 144
            return main[at : at + 144, :], side[at : at + 144, :]
        source, second = (lo, i == 2) if i < 3 else (hi, i == 8)
        at = 144 if second else 0
        beside = source[288:432, :].astype(F32)
        if second:
            beside = turned_by(beside, -4, 1)
        return source[at : at + 144, :].astype(F32), jnp.where(kept, beside, 0.0)

    for i in range(1, 9):
        start = residual[i - 1] + jnp.concatenate(supplied(i), axis=1)
        rest[i - 1] = start
        d0[i - 1] = start * inverse[i - 1] * (1.0 / MIDDLE)

    def share(i, d):
        return (
            face_layer[i] * d[i]
            + face_layer[i - 1] * d[i - 2]
            + around(face_row[i - 1], face_col[i - 1], d[i - 1])
        )

    for i in range(2, 8):
        start = rest[i - 1]
        later = start * (1.0 - 1.0 / MIDDLE) + share(i, d0)
        d1[i - 1] = W1 * W0 * d0[i - 1] + (2.0 * W1 / SPREAD) * (later * inverse[i - 1])
        rest[i - 1] = later - (W1 * W0 / MIDDLE) * start - (2.0 * W1 / SPREAD) * later
    for i in range(3, 7):
        last = rest[i - 1] + share(i, d1)
        step = d0[i - 1] + d1[i - 1] * (1.0 + W2 * W1) + (2.0 * W2 / SPREAD) * (last * inverse[i - 1])
        at = (i - 3) * 128
        out[at : at + 128, :] = grids[i, 0:128, :] + step[0:128, 0:128]


def sds(shape, dtype):
    return jax.ShapeDtypeStruct(shape, dtype)


def call(kernel, shape, args, mib=16, scratch=(), far=(), far_out=False):
    vmem, anywhere = pl.BlockSpec(memory_space=pltpu.VMEM), pl.BlockSpec(memory_space=pl.ANY)
    return pl.pallas_call(
        kernel,
        out_shape=shape,
        in_specs=[anywhere if i in far else vmem for i in range(len(args))],
        out_specs=jax.tree.map(lambda _: anywhere if far_out else vmem, shape),
        scratch_shapes=list(scratch),
        compiler_params=pltpu.CompilerParams(vmem_limit_bytes=mib * 2**20),
    )(*args)


def pairs(axis):
    up = [(i, i + 1) for i in range(lax.axis_size(axis) - 1)]
    return up, [(b, a) for a, b in up]


def exchange(to_next, to_last, axis):
    up, down = pairs(axis)
    return lax.ppermute(to_next, axis, up), lax.ppermute(to_last, axis, down)


def extended_operator(temp, cond, mass):
    grids = (temp, cond, mass)
    lo, hi = exchange(
        jnp.concatenate([g[1:4] for g in grids]).astype(BF16),
        jnp.concatenate([g[0:3] for g in grids]).astype(BF16),
        LAYER,
    )

    def rows(at):
        parts = []
        for a, g in enumerate(grids):
            parts += [lo[3 * a : 3 * a + 3, at], g[:, at].astype(BF16), hi[3 * a : 3 * a + 3, at]]
        return jnp.concatenate(parts).reshape(240, 128)

    above, below = exchange(rows(slice(120, 128)), rows(slice(0, 8)), "row")
    wide, to_left, to_right = call(
        gather_kernel,
        (sds((30, 144, 128), F32), sds((144, 128), BF16), sds((144, 128), BF16)),
        (*grids, lo, hi, above, below),
        mib=24,
        scratch=[pltpu.VMEM((3, 4, 128, 128), F32), pltpu.SemaphoreType.DMA((3,))],
        far=(0, 1, 2),
    )
    from_left, from_right = exchange(to_right, to_left, COL)
    eight = sds((8, 144, 256), F32)
    terms = call(
        operator_kernel,
        (sds((9, 144, 256), F32), eight, eight, eight, eight),
        (wide, from_left, from_right),
        mib=32,
        scratch=[pltpu.VMEM((30, 144, 256), F32)],
    )
    return wide, terms


def shards(temp, cond, mass, toggling, baseline, panel, place, holder, tier, warming):
    row64 = pltpu.VMEM((1, 64), I32)
    message, meta = call(
        message_kernel,
        (sds((64, 128), F32), sds((8, 128), I32)),
        (temp, panel.reshape(1, 64), place, holder, tier),
        scratch=[
            pltpu.VMEM((4, 128, 128), F32), row64, row64, row64,
            pltpu.VMEM((1, 16), I32), pltpu.SemaphoreType.DMA((5,)),
        ],
        far=range(5),
    )
    messages = lax.all_to_all(message.reshape(64, 1, 128), CUBE, split_axis=0, concat_axis=0, tiled=True)
    messages = messages.reshape(64, 128)
    placing, columns, toggling, baseline, warming = call(
        placing_kernel,
        (
            sds((1024, 64), BF16), sds((64, 128), I32),
            sds((64, 4096), BF16), sds((64, 4096), BF16), sds((1, 16), F32),
        ),
        (meta, toggling[0], baseline[0], warming),
        scratch=[pltpu.SemaphoreType.DMA((3,))],
        far=(1, 2, 3),
    )
    send = call(
        power_kernel,
        sds((256, 4736), BF16),
        (messages, columns, warming, toggling, baseline, placing),
        mib=24,
        scratch=[pltpu.VMEM((256, 4736), BF16), pltpu.SemaphoreType.DMA((9,))],
        far_out=True,
    )
    received = lax.all_to_all(send.reshape(16, 16, 4736), PLANE, split_axis=0, concat_axis=0, tiled=True)
    selector = call(selector_kernel, sds((576, 256), BF16), (messages,))
    partial = call(combine_kernel, sds((64, 4480), F32), (selector, received.reshape(256, 4736)))
    parts = lax.all_to_all(
        partial.astype(jnp.float16).reshape(4, 16, 4480), "zlo", split_axis=0, concat_axis=0, tiled=True
    )
    wide, terms = extended_operator(temp, cond, mass)
    block, strip = sds((576, 128), F32), sds((432, 128), BF16)
    density, main, side, up, down = call(
        unpack_kernel,
        (sds((512, 128), F32), block, block, strip, strip),
        (jnp.sum(parts.astype(F32), axis=0),),
        scratch=[pltpu.VMEM((512, 128), F32)],
    )
    lo, hi = exchange(up, down, LAYER)
    eight = pltpu.VMEM((8, 144, 256), F32)
    guess = call(
        sweep_kernel,
        sds((512, 128), F32),
        (main, side, lo, hi, wide, *terms),
        mib=40,
        scratch=[eight, eight, eight],
    )
    return guess.reshape(4, 128, 128), density.reshape(4, 128, 128)


def solution(mesh):
    fine = Mesh(mesh.devices.reshape(4, 4, 4, 4, 2), ("row", "zlo", "y", "zhi", "core"))
    grid = P(LAYER, "row", COL)
    slot = ("row", "zlo", "y", "zhi", "core")
    return jax.shard_map(
        shards,
        mesh=fine,
        in_specs=(
            grid,
            grid,
            grid,
            P(slot, None, None),
            P(slot, None, None),
            P(slot, None, None),
            P(slot, None),
            P(slot, None),
            P(slot, None),
            P(slot, None),
        ),
        out_specs=(grid, grid),
        check_vma=False,
    )
```

```python
import jax
import jax.numpy as jnp
from jax import lax
from jax.experimental import pallas as pl
from jax.experimental.pallas import tpu as pltpu
from jax.sharding import Mesh
from jax.sharding import PartitionSpec as P

eig_low = 0.1
eig_high = 2.0

LAYER = ("zhi", "core")
COL = ("zlo", "y")
CUBE = ("row", "zlo", "y")
PLANE = ("row", "y")

F32, BF16, I32 = jnp.float32, jnp.bfloat16, jnp.int32


def iota(shape, dim):
    return lax.broadcasted_iota(I32, shape, dim)


def as_column(row):
    n = row.shape[1]
    return jnp.sum(jnp.where(iota((n, n), 0) == iota((n, n), 1), row, 0), axis=1, keepdims=True)


def slot_rows(panel, place, holder, tier):
    layer = jnp.sum(jnp.where(iota((16, 64), 0) == holder, as_column(tier), 0), axis=0, keepdims=True)
    pos = layer * 4 + place
    ident = ((panel >> 2) & 3) * 16 + pos
    column = (panel >> 4) * 4 + (panel & 3)
    same = (as_column(column) == column) & (iota((64, 64), 0) < iota((64, 64), 1))
    rank = jnp.sum(same.astype(I32), axis=0, keepdims=True)
    return pos, ident, column * 16 + rank


def message_kernel(temp, panel, place, holder, tier, out, meta, temp_v, panel_v, place_v, holder_v, tier_v, sems):
    pairs = [(panel, panel_v), (place, place_v), (holder, holder_v), (tier, tier_v), (temp, temp_v)]
    copies = [pltpu.make_async_copy(a, b, sems.at[i]) for i, (a, b) in enumerate(pairs)]
    for copy in copies:
        copy.start()
    for copy in copies[:4]:
        copy.wait()
    panel_row, holder_row = panel_v[...], holder_v[...]
    pos, ident, dest = slot_rows(panel_row, place_v[...], holder_row, tier_v[...])
    for k, row in enumerate((panel_row, pos, dest, holder_row)):
        meta[k : k + 1, :] = jnp.concatenate([row, row], axis=1)
    meta[4:8, :] = jnp.zeros((4, 128), I32)
    code = (dest * 64 + ident).astype(F32)
    copies[4].wait()
    sums = jnp.sum(temp_v[...].reshape(8, 64, 128), axis=1)
    lane = iota((8, 128), 1)
    first = jnp.sum(jnp.where(lane < 64, sums, 0.0), axis=1, keepdims=True)
    second = jnp.sum(jnp.where(lane < 64, 0.0, sums), axis=1, keepdims=True)
    at = iota((8, 128), 0) * 2
    means = jnp.where(lane == at, first, jnp.where(lane == at + 1, second, 0.0))
    means = jnp.sum(means, axis=0, keepdims=True) * (1.0 / 4096.0)
    row = jnp.where(iota((1, 128), 1) < 64, means, jnp.concatenate([code, code], axis=1))
    out[...] = jnp.broadcast_to(row, (64, 128))


def placing_kernel(meta, toggling, baseline, warming, placing, columns, toggling_v, baseline_v, warming_v, sems):
    pairs = [(toggling, toggling_v), (baseline, baseline_v), (warming, warming_v)]
    copies = [pltpu.make_async_copy(a, b, sems.at[i]) for i, (a, b) in enumerate(pairs)]
    for copy in copies:
        copy.start()
    panel, pos, dest, holder = (meta[k : k + 1, 0:64] for k in range(4))
    x, y, rank = panel >> 4, panel & 3, dest & 15
    lower, right = (pos >> 1) & 1, pos & 1
    next_x = x + lower * 2 - 1
    next_y = (y + right * 2 + 3) & 3
    inside = (next_x >= 0) & (next_x <= 3)
    targets = (
        dest,
        jnp.where(inside, (next_x * 4 + y) * 16 + rank, -1),
        (x * 4 + next_y) * 16 + rank,
        jnp.where(inside, (next_x * 4 + next_y) * 16 + rank, -1),
    )
    for k, target in enumerate(targets):
        placing[pl.ds(k * 256, 256), :] = jnp.where(iota((256, 64), 0) == target, 1.0, 0.0).astype(BF16)
    lane = iota((64, 128), 1)
    columns[...] = jnp.where(
        lane == 0, as_column(panel), jnp.where(lane == 1, as_column(pos), as_column(holder))
    )
    for copy in copies:
        copy.wait()


def power_kernel(messages, columns, warming, toggling, baseline, placing, out, sent, sems):
    tile, pos, holder = (columns[:, k : k + 1] for k in range(3))
    lower, right = (pos >> 1) & 1, pos & 1
    pick = jnp.where(iota((64, 64), 1) == tile, 1.0, 0.0)
    means = jnp.dot(pick, messages[...], precision=lax.Precision.HIGHEST, preferred_element_type=F32)
    lane = iota((64, 128), 1)
    slot_mean = jnp.sum(jnp.where(lane == pos, means, 0.0), axis=1, keepdims=True)
    member = iota((64, 16), 1) == holder
    total = jnp.sum(jnp.where(member, slot_mean, 0.0), axis=0, keepdims=True)
    count = jnp.sum(jnp.where(member, 1.0, 0.0), axis=0, keepdims=True)
    leak = jnp.exp(warming[...] * (total / count))
    factor = jnp.sum(jnp.where(member, leak, 0.0), axis=1, keepdims=True)

    def place(kind, values):
        at = placing[kind * 256 : (kind + 1) * 256, :]
        return jnp.dot(at, values.astype(BF16), preferred_element_type=F32).astype(BF16)

    copies = []

    def send(start, width):
        at = pl.ds(start, width)
        copy = pltpu.make_async_copy(sent.at[:, at], out.at[:, at], sems.at[len(copies)])
        copy.start()
        copies.append(copy)

    edge = ((lane & 63) >> 1) == right * 31
    sides = jnp.zeros((64, 128), F32)
    width = 512
    for k in range(8):
        at = pl.ds(k * width, width)
        power = (toggling[:, at].astype(F32) + factor * baseline[:, at].astype(F32)).astype(BF16)
        sent[:, at] = place(0, power)
        send(k * width, width)
        power = power.astype(F32)
        for t in range(4):
            piece = power[:, t * 128 : (t + 1) * 128]
            shift = 2 * (4 * k + t)
            kept = jnp.where(edge, piece, 0.0)
            sides = sides + (pltpu.roll(kept, shift, 1) if shift else kept)
            if k == 0 and t == 0:
                top = piece
    rows = jnp.where(lower == 0, top, piece)
    sides = jnp.where(right == 0, sides, pltpu.roll(sides, 66, 1))
    corner = jnp.sum(jnp.where(lane == lower * 64 + right * 63, rows, 0.0), axis=1, keepdims=True)
    quarter = (1 - lower) * 2 + 1 - right
    both = jnp.concatenate([jnp.where(lower == 1, rows, 0.0), jnp.where(lower == 0, rows, 0.0)], axis=1)
    sent[:, 4096:4352] = place(1, both)
    both = jnp.concatenate([jnp.where(right == 1, sides, 0.0), jnp.where(right == 0, sides, 0.0)], axis=1)
    sent[:, 4352:4608] = place(2, both)
    sent[:, 4608:4736] = place(3, jnp.where(lane == quarter, corner, 0.0))
    send(4096, 640)
    for copy in copies:
        copy.wait()


def selector_kernel(messages, out):
    x, y = lax.axis_index("row"), lax.axis_index("y")
    plane = lax.axis_index("zlo")
    code = jnp.concatenate([messages[pl.ds(r * 16 + plane * 4, 4), :] for r in range(4)], axis=0)
    code = jnp.where(iota((16, 128), 1) < 64, -1.0, code).astype(I32)
    dest, ident = code >> 6, code & 63
    lane = iota((16, 256), 1)

    def idents(dx, dy):
        base = ((x + dx) * 4 + ((y + dy + 4) & 3)) * 16
        ids = jnp.zeros((16, 256), I32)
        for r in range(16):
            hit = jnp.sum(jnp.where(dest == base + r, ident + 1, 0), axis=1, keepdims=True)
            ids = jnp.where((lane & 15) == r, hit, ids)
        ids = jnp.sum(jnp.where((lane >> 4) == iota((16, 256), 0), ids, 0), axis=0, keepdims=True) - 1
        turn = jnp.where(y == 0, 1, 0) if dy < 0 else jnp.where(y == 3, -1, 0) if dy > 0 else 0
        return ids, (ids >> 4) + turn, (ids >> 2) & 3, (ids >> 1) & 1, ids & 1

    def put(k, ids, target):
        out[pl.ds(k * 64, 64), :] = jnp.where(
            (iota((64, 256), 0) == target) & (ids >= 0), 1.0, 0.0
        ).astype(BF16)

    ids, *_ = idents(0, 0)
    put(0, ids, ids)
    for k, dx in enumerate((-1, 1)):
        ids, z, layer, _, pc = idents(dx, 0)
        put(1 + k, ids, z * 16 + k * 8 + layer * 2 + pc)
    for k, dy in enumerate((-1, 1)):
        ids, z, layer, pr, _ = idents(0, dy)
        put(3 + k, ids, z * 16 + k * 8 + layer * 2 + pr)
    for k in range(4):
        ids, z, layer, _, _ = idents((k >> 1) * 2 - 1, (k & 1) * 2 - 1)
        put(5 + k, ids, z * 16 + layer)


def combine_kernel(selector, received, _left, _right, out):
    def add(k, start, width):
        return jnp.dot(
            selector[k * 64 : (k + 1) * 64, :],
            received[:, start : start + width],
            preferred_element_type=F32,
        )

    for k in range(8):
        out[:, k * 512 : (k + 1) * 512] = add(0, k * 512, 512)
    out[:, 4096:4224] = add(1, 4096, 128) + add(2, 4224, 128)
    out[:, 4224:4352] = add(3, 4352, 128) + add(4, 4480, 128)
    lane = iota((64, 128), 1)
    corners = jnp.zeros((64, 128), F32)
    for k in range(4):
        corners = jnp.where(lane == k, add(5 + k, 4608, 128), corners)
    out[:, 4352:4480] = corners


def unpack_kernel(whole, density, main, side, up, down, turned):
    for k in range(32):
        turned[k * 16 : (k + 1) * 16, :] = whole[:, k * 128 : (k + 1) * 128]
    low = iota((32, 128), 1) < 64
    lane = iota((64, 128), 1)
    low_row = iota((1, 128), 1) < 64
    lane16, row16 = iota((16, 128), 1), iota((16, 128), 0)
    rows, columns, corners = whole[:, 4096:4224], whole[:, 4224:4352], whole[:, 4352:4480]
    cell = iota((64, 128), 0)
    turn = []
    for c in range(2):
        pick = jnp.where(lane == (cell & 1) * 64 + (cell - (cell & 1)) + c, 1.0, 0.0)
        turn.append(
            lax.dot_general(
                pick, columns, (((1,), (1,)), ((), ())),
                precision=lax.Precision.HIGHEST, preferred_element_type=F32,
            )
        )
    for layer in range(4):
        base = layer * 144
        for r in range(2):
            left = turned[pl.ds(layer * 4 + r * 2, 32, stride=16), :]
            right = turned[pl.ds(layer * 4 + r * 2 + 1, 32, stride=16), :]
            at = base + r * 64
            main[pl.ds(at, 32, stride=2), :] = jnp.where(low, left, pltpu.roll(right, 64, 1))
            main[pl.ds(at + 1, 32, stride=2), :] = jnp.where(low, pltpu.roll(left, 64, 1), right)
            k = layer * 2 + r
            strip = jnp.where(lane == 0, turn[0][:, 8 + k : 9 + k], 0.0)
            strip = jnp.where(lane == 1, turn[1][:, 8 + k : 9 + k], strip)
            strip = jnp.where(lane == 126, turn[0][:, k : k + 1], strip)
            side[at : at + 64, :] = jnp.where(lane == 127, turn[1][:, k : k + 1], strip)
        block = jnp.zeros((16, 128), F32)
        for kind, first_row in ((0, 14), (1, 0)):
            k = kind * 8 + layer * 2
            a, b = rows[k : k + 1, :], rows[k + 1 : k + 2, :]
            first = jnp.where(low_row, a, pltpu.roll(b, 64, 1))
            second = jnp.where(low_row, pltpu.roll(a, 64, 1), b)
            block = jnp.where(row16 == first_row, first, block)
            block = jnp.where(row16 == first_row + 1, second, block)
        main[base + 128 : base + 144, :] = block
        block = jnp.zeros((16, 128), F32)
        for k, (r, at_lane) in enumerate(((15, 127), (15, 0), (0, 127), (0, 0))):
            value = corners[layer : layer + 1, k : k + 1]
            block = jnp.where((row16 == r) & (lane16 == at_lane), value, block)
        side[base + 128 : base + 144, :] = block
        density[layer * 128 : (layer + 1) * 128, :] = main[base : base + 128, :]
    for out, first in ((up, 288), (down, 0)):
        out[0:288, :] = main[first : first + 288, :].astype(BF16)
        second = side[first + 144 : first + 288, :]
        out[288:432, :] = (side[first : first + 144, :] + pltpu.roll(second, 4, 1)).astype(BF16)


def layers_kernel(temp, cond, mass, own, up, down, sems):
    copies = [pltpu.make_async_copy(a, own.at[i], sems.at[i]) for i, a in enumerate((temp, cond, mass))]
    for copy in copies:
        copy.start()
    for a, copy in enumerate(copies):
        copy.wait()
        for k in range(3):
            up[3 * a + k] = own[a, 1 + k].astype(BF16)
            down[3 * a + k] = own[a, k].astype(BF16)


def rows_kernel(own, lo, hi, last, first):
    lasts, firsts = [], []
    for a in range(3):
        for layer in range(10):
            if 3 <= layer < 7:
                lasts.append(own[a, layer - 3, 120:128, :])
                firsts.append(own[a, layer - 3, 0:8, :])
            else:
                source, k = (lo, 3 * a + layer) if layer < 3 else (hi, 3 * a + layer - 7)
                lasts.append(source[k, 112:128, :].astype(F32)[8:16])
                firsts.append(source[k, 0:16, :].astype(F32)[0:8])
    last[...] = jnp.concatenate(lasts, axis=0).astype(BF16)
    first[...] = jnp.concatenate(firsts, axis=0).astype(BF16)


def gather_kernel(own, lo, hi, above, below, out, to_left, to_right):
    over, under = above[...].astype(F32), below[...].astype(F32)
    lane = iota((144, 128), 1)
    left, right = jnp.zeros((144, 128), F32), jnp.zeros((144, 128), F32)
    for a in range(3):
        for layer in range(10):
            i = a * 10 + layer
            if layer < 3:
                source = lo[3 * a + layer].astype(F32)
            elif layer < 7:
                source = own[a, layer - 3]
            else:
                source = hi[3 * a + layer - 7].astype(F32)
            piece = jnp.concatenate([source, under[8 * i : 8 * i + 8], over[8 * i : 8 * i + 8]], axis=0)
            out[i] = piece
            base = a * 40 + layer * 4
            here = (lane >= base) & (lane < base + 3)
            left = jnp.where(here, pltpu.roll(piece, base, 1) if base else piece, left)
            right = jnp.where(here, pltpu.roll(piece, base + 3, 1), right)
    to_left[...] = left.astype(BF16)
    to_right[...] = right.astype(BF16)


def turned_by(x, shift, axis):
    return pltpu.roll(x, shift % x.shape[axis], axis)


def around(face_row, face_col, v):
    return (
        face_row * turned_by(v, -1, 0)
        + turned_by(face_row * v, 1, 0)
        + face_col * turned_by(v, -1, 1)
        + turned_by(face_col * v, 1, 1)
    )


def operator_kernel(grids, from_left, from_right, face_layer, face_row, face_col, inverse, residual, wide):
    left, right = from_left[...].astype(F32), from_right[...].astype(F32)
    lane = iota((144, 128), 1)
    for a in range(3):
        for layer in range(10):
            i, base = a * 10 + layer, a * 40 + layer * 4
            high = turned_by(right, -base, 1) if base else right
            side = jnp.where(lane < 3, high, jnp.where(lane >= 125, turned_by(left, 125 - base, 1), 0.0))
            wide[i, :, 0:128] = grids[i]
            wide[i, :, 128:256] = side
    for layer in range(9):
        face_layer[layer] = 0.5 * (wide[10 + layer] + wide[11 + layer])
    for layer in range(1, 9):
        temp, cond, mass = (wide[a * 10 + layer] for a in range(3))
        rows = 0.5 * (cond + turned_by(cond, -1, 0))
        cols = 0.5 * (cond + turned_by(cond, -1, 1))
        face_row[layer - 1] = rows
        face_col[layer - 1] = cols
        after, before = face_layer[layer], face_layer[layer - 1]
        diagonal = mass + after + before + rows + turned_by(rows, 1, 0) + cols + turned_by(cols, 1, 1)
        share = after * wide[layer + 1] + before * wide[layer - 1] + around(rows, cols, temp)
        residual[layer - 1] = mass * temp + (share - diagonal * temp)
        inverse[layer - 1] = jnp.where(mass > 0.0, 1.0 / diagonal, 0.0)


MIDDLE = (eig_low + eig_high) / 2.0
SPREAD = (eig_high - eig_low) / 2.0
W0 = SPREAD / MIDDLE
W1 = 1.0 / (2.0 * MIDDLE / SPREAD - W0)
W2 = 1.0 / (2.0 * MIDDLE / SPREAD - W1)


def sweep_kernel(main, side, lo, hi, grids, face_layer, face_row, face_col, inverse, residual, out, d0, d1, rest):
    lane = iota((144, 128), 1)
    kept = (lane < 2) | (lane >= 126)

    def supplied(i):
        if 3 <= i <= 6:
            at = (i - 3) * 144
            return main[at : at + 144, :], side[at : at + 144, :]
        source, second = (lo, i == 2) if i < 3 else (hi, i == 8)
        at = 144 if second else 0
        beside = source[288:432, :].astype(F32)
        if second:
            beside = turned_by(beside, -4, 1)
        return source[at : at + 144, :].astype(F32), jnp.where(kept, beside, 0.0)

    for i in range(1, 9):
        start = residual[i - 1] + jnp.concatenate(supplied(i), axis=1)
        rest[i - 1] = start
        d0[i - 1] = start * inverse[i - 1] * (1.0 / MIDDLE)

    def share(i, d):
        return (
            face_layer[i] * d[i]
            + face_layer[i - 1] * d[i - 2]
            + around(face_row[i - 1], face_col[i - 1], d[i - 1])
        )

    for i in range(2, 8):
        start = rest[i - 1]
        later = start * (1.0 - 1.0 / MIDDLE) + share(i, d0)
        d1[i - 1] = W1 * W0 * d0[i - 1] + (2.0 * W1 / SPREAD) * (later * inverse[i - 1])
        rest[i - 1] = later - (W1 * W0 / MIDDLE) * start - (2.0 * W1 / SPREAD) * later
    for i in range(3, 7):
        last = rest[i - 1] + share(i, d1)
        step = d0[i - 1] + d1[i - 1] * (1.0 + W2 * W1) + (2.0 * W2 / SPREAD) * (last * inverse[i - 1])
        at = (i - 3) * 128
        out[at : at + 128, :] = grids[i, 0:128, :] + step[0:128, 0:128]


def sds(shape, dtype):
    return jax.ShapeDtypeStruct(shape, dtype)


def call(kernel, shape, args, mib=16, scratch=(), far=(), far_out=False):
    vmem, anywhere = pl.BlockSpec(memory_space=pltpu.VMEM), pl.BlockSpec(memory_space=pltpu.HBM)
    return pl.pallas_call(
        kernel,
        out_shape=shape,
        in_specs=[anywhere if i in far else vmem for i in range(len(args))],
        out_specs=jax.tree.map(lambda _: anywhere if far_out else vmem, shape),
        scratch_shapes=list(scratch),
        compiler_params=pltpu.CompilerParams(vmem_limit_bytes=mib * 2**20),
    )(*args)


def pairs(axis):
    up = [(i, i + 1) for i in range(lax.axis_size(axis) - 1)]
    return up, [(b, a) for a, b in up]


def exchange(to_next, to_last, axis):
    up, down = pairs(axis)
    return lax.ppermute(to_next, axis, up), lax.ppermute(to_last, axis, down)


def extended_grids(temp, cond, mass):
    nine, rows, edge = sds((9, 128, 128), BF16), sds((240, 128), BF16), sds((144, 128), BF16)
    own, up, down = call(
        layers_kernel,
        (sds((3, 4, 128, 128), F32), nine, nine),
        (temp, cond, mass),
        scratch=[pltpu.SemaphoreType.DMA((3,))],
        far=range(3),
    )
    lo, hi = exchange(up, down, LAYER)
    above, below = exchange(*call(rows_kernel, (rows, rows), (own, lo, hi)), "row")
    wide, to_left, to_right = call(
        gather_kernel, (sds((30, 144, 128), F32), edge, edge), (own, lo, hi, above, below), mib=24
    )
    return wide, exchange(to_right, to_left, COL)


def operator(wide, from_left, from_right):
    eight = sds((8, 144, 256), F32)
    return call(
        operator_kernel,
        (sds((9, 144, 256), F32), eight, eight, eight, eight),
        (wide, from_left, from_right),
        mib=32,
        scratch=[pltpu.VMEM((30, 144, 256), F32)],
    )


def shards(temp, cond, mass, toggling, baseline, panel, place, holder, tier, warming):
    row64 = pltpu.VMEM((1, 64), I32)
    message, meta = call(
        message_kernel,
        (sds((64, 128), F32), sds((8, 128), I32)),
        (temp, panel.reshape(1, 64), place, holder, tier),
        mib=60,
        scratch=[
            pltpu.VMEM((4, 128, 128), F32), row64, row64, row64,
            pltpu.VMEM((1, 16), I32), pltpu.SemaphoreType.DMA((5,)),
        ],
        far=range(5),
    )
    messages = lax.all_to_all(message.reshape(64, 1, 128), CUBE, split_axis=0, concat_axis=0, tiled=True)
    messages = messages.reshape(64, 128)
    placing, columns, toggling, baseline, warming = call(
        placing_kernel,
        (
            sds((1024, 64), BF16), sds((64, 128), I32),
            sds((64, 4096), BF16), sds((64, 4096), BF16), sds((1, 16), F32),
        ),
        (meta, toggling[0], baseline[0], warming),
        scratch=[pltpu.SemaphoreType.DMA((3,))],
        far=(1, 2, 3),
    )
    send = call(
        power_kernel,
        sds((256, 4736), BF16),
        (messages, columns, warming, toggling, baseline, placing),
        mib=24,
        scratch=[pltpu.VMEM((256, 4736), BF16), pltpu.SemaphoreType.DMA((9,))],
        far_out=True,
    )
    received = lax.all_to_all(send.reshape(16, 16, 4736), PLANE, split_axis=0, concat_axis=0, tiled=True)
    selector = call(selector_kernel, sds((576, 256), BF16), (messages,))
    wide, beside = extended_grids(temp, cond, mass)
    partial = call(
        combine_kernel, sds((64, 4480), F32), (selector, received.reshape(256, 4736), *beside)
    )
    parts = lax.all_to_all(
        partial.astype(jnp.float16).reshape(4, 16, 4480), "zlo", split_axis=0, concat_axis=0, tiled=True
    )
    terms = operator(wide, *beside)
    block, strip = sds((576, 128), F32), sds((432, 128), BF16)
    density, main, side, up, down = call(
        unpack_kernel,
        (sds((512, 128), F32), block, block, strip, strip),
        (jnp.sum(parts.astype(F32), axis=0),),
        scratch=[pltpu.VMEM((512, 128), F32)],
    )
    lo, hi = exchange(up, down, LAYER)
    eight = pltpu.VMEM((8, 144, 256), F32)
    guess = call(
        sweep_kernel,
        sds((512, 128), F32),
        (main, side, lo, hi, wide, *terms),
        mib=40,
        scratch=[eight, eight, eight],
    )
    return guess.reshape(4, 128, 128), density.reshape(4, 128, 128)


def solution(mesh):
    fine = Mesh(mesh.devices.reshape(4, 4, 4, 4, 2), ("row", "zlo", "y", "zhi", "core"))
    grid = P(LAYER, "row", COL)
    slot = ("row", "zlo", "y", "zhi", "core")
    return jax.shard_map(
        shards,
        mesh=fine,
        in_specs=(
            grid,
            grid,
            grid,
            P(slot, None, None),
            P(slot, None, None),
            P(slot, None, None),
            P(slot, None),
            P(slot, None),
            P(slot, None),
            P(slot, None),
        ),
        out_specs=(grid, grid),
        check_vma=False,
    )
```

```python
import jax
import jax.numpy as jnp
from jax import lax
from jax.experimental import pallas as pl
from jax.experimental.pallas import tpu as pltpu
from jax.sharding import Mesh
from jax.sharding import PartitionSpec as P

eig_low = 0.1
eig_high = 2.0

LAYER = ("zhi", "core")
COL = ("zlo", "y")
CUBE = ("row", "zlo", "y")
PLANE = ("row", "y")

F32, BF16, I32 = jnp.float32, jnp.bfloat16, jnp.int32


def iota(shape, dim):
    return lax.broadcasted_iota(I32, shape, dim)


def as_column(row):
    n = row.shape[1]
    return jnp.sum(jnp.where(iota((n, n), 0) == iota((n, n), 1), row, 0), axis=1, keepdims=True)


def slot_rows(panel, place, holder, tier):
    layer = jnp.sum(jnp.where(iota((16, 64), 0) == holder, as_column(tier), 0), axis=0, keepdims=True)
    pos = layer * 4 + place
    ident = ((panel >> 2) & 3) * 16 + pos
    column = (panel >> 4) * 4 + (panel & 3)
    same = (as_column(column) == column) & (iota((64, 64), 0) < iota((64, 64), 1))
    rank = jnp.sum(same.astype(I32), axis=0, keepdims=True)
    return pos, ident, column * 16 + rank


def place_slots(panel, pos, dest, holder, placing, columns):
    x, y, rank = panel >> 4, panel & 3, dest & 15
    lower, right = (pos >> 1) & 1, pos & 1
    next_x = x + lower * 2 - 1
    next_y = (y + right * 2 + 3) & 3
    inside = (next_x >= 0) & (next_x <= 3)
    targets = (
        dest,
        jnp.where(inside, (next_x * 4 + y) * 16 + rank, -1),
        (x * 4 + next_y) * 16 + rank,
        jnp.where(inside, (next_x * 4 + next_y) * 16 + rank, -1),
    )
    for k, target in enumerate(targets):
        placing[pl.ds(k * 256, 256), :] = jnp.where(iota((256, 64), 0) == target, 1.0, 0.0).astype(BF16)
    lane = iota((64, 128), 1)
    columns[...] = jnp.where(
        lane == 0, as_column(panel), jnp.where(lane == 1, as_column(pos), as_column(holder))
    )


def message_kernel(temp, panel, place, holder, tier, out, placing, columns, temp_v, panel_v, place_v, holder_v, tier_v, sems):
    pairs = [(panel, panel_v), (place, place_v), (holder, holder_v), (tier, tier_v), (temp, temp_v)]
    copies = [pltpu.make_async_copy(a, b, sems.at[i]) for i, (a, b) in enumerate(pairs)]
    for copy in copies:
        copy.start()
    for copy in copies[:4]:
        copy.wait()
    panel_row, holder_row = panel_v[...], holder_v[...]
    pos, ident, dest = slot_rows(panel_row, place_v[...], holder_row, tier_v[...])
    place_slots(panel_row, pos, dest, holder_row, placing, columns)
    code = (dest * 64 + ident).astype(F32)
    copies[4].wait()
    sums = jnp.sum(temp_v[...].reshape(8, 64, 128), axis=1)
    lane = iota((8, 128), 1)
    first = jnp.sum(jnp.where(lane < 64, sums, 0.0), axis=1, keepdims=True)
    second = jnp.sum(jnp.where(lane < 64, 0.0, sums), axis=1, keepdims=True)
    at = iota((8, 128), 0) * 2
    means = jnp.where(lane == at, first, jnp.where(lane == at + 1, second, 0.0))
    means = jnp.sum(means, axis=0, keepdims=True) * (1.0 / 4096.0)
    row = jnp.where(iota((1, 128), 1) < 64, means, jnp.concatenate([code, code], axis=1))
    out[...] = jnp.broadcast_to(row, (64, 128))


def power_kernel(
    far_messages, far_columns, far_warming, far_toggling, far_baseline, far_placing, out,
    messages, columns, warming, toggling, baseline, placing, sent, sems,
):
    pairs = [
        (far_messages, messages),
        (far_columns, columns),
        (far_warming, warming),
        (far_toggling, toggling),
        (far_baseline, baseline),
        (far_placing, placing),
    ]
    loads = [pltpu.make_async_copy(a, b, sems.at[9 + i]) for i, (a, b) in enumerate(pairs)]
    for load in loads:
        load.start()
    loads[0].wait()
    loads[1].wait()
    tile, pos, holder = (columns[:, k : k + 1] for k in range(3))
    lower, right = (pos >> 1) & 1, pos & 1
    pick = jnp.where(iota((64, 64), 1) == tile, 1.0, 0.0)
    means = jnp.dot(pick, messages[...], precision=lax.Precision.HIGHEST, preferred_element_type=F32)
    lane = iota((64, 128), 1)
    slot_mean = jnp.sum(jnp.where(lane == pos, means, 0.0), axis=1, keepdims=True)
    member = iota((64, 16), 1) == holder
    total = jnp.sum(jnp.where(member, slot_mean, 0.0), axis=0, keepdims=True)
    count = jnp.sum(jnp.where(member, 1.0, 0.0), axis=0, keepdims=True)
    loads[2].wait()
    leak = jnp.exp(warming[...] * (total / count))
    factor = jnp.sum(jnp.where(member, leak, 0.0), axis=1, keepdims=True)

    def place(kind, values):
        at = placing[kind * 256 : (kind + 1) * 256, :]
        return jnp.dot(at, values.astype(BF16), preferred_element_type=F32).astype(BF16)

    copies = []

    def send(start, width):
        at = pl.ds(start, width)
        copy = pltpu.make_async_copy(sent.at[:, at], out.at[:, at], sems.at[len(copies)])
        copy.start()
        copies.append(copy)

    for load in loads[3:]:
        load.wait()
    edge = ((lane & 63) >> 1) == right * 31
    sides = jnp.zeros((64, 128), F32)
    width = 512
    for k in range(8):
        at = pl.ds(k * width, width)
        power = (toggling[:, at].astype(F32) + factor * baseline[:, at].astype(F32)).astype(BF16)
        sent[:, at] = place(0, power)
        send(k * width, width)
        power = power.astype(F32)
        for t in range(4):
            piece = power[:, t * 128 : (t + 1) * 128]
            shift = 2 * (4 * k + t)
            kept = jnp.where(edge, piece, 0.0)
            sides = sides + (pltpu.roll(kept, shift, 1) if shift else kept)
            if k == 0 and t == 0:
                top = piece
    rows = jnp.where(lower == 0, top, piece)
    sides = jnp.where(right == 0, sides, pltpu.roll(sides, 66, 1))
    corner = jnp.sum(jnp.where(lane == lower * 64 + right * 63, rows, 0.0), axis=1, keepdims=True)
    quarter = (1 - lower) * 2 + 1 - right
    both = jnp.concatenate([jnp.where(lower == 1, rows, 0.0), jnp.where(lower == 0, rows, 0.0)], axis=1)
    sent[:, 4096:4352] = place(1, both)
    both = jnp.concatenate([jnp.where(right == 1, sides, 0.0), jnp.where(right == 0, sides, 0.0)], axis=1)
    sent[:, 4352:4608] = place(2, both)
    sent[:, 4608:4736] = place(3, jnp.where(lane == quarter, corner, 0.0))
    send(4096, 640)
    for copy in copies:
        copy.wait()


def selector_kernel(messages, out):
    x, y = lax.axis_index("row"), lax.axis_index("y")
    plane = lax.axis_index("zlo")
    code = jnp.concatenate([messages[pl.ds(r * 16 + plane * 4, 4), :] for r in range(4)], axis=0)
    code = jnp.where(iota((16, 128), 1) < 64, -1.0, code).astype(I32)
    dest, ident = code >> 6, code & 63
    lane = iota((16, 256), 1)

    def idents(dx, dy):
        base = ((x + dx) * 4 + ((y + dy + 4) & 3)) * 16
        ids = jnp.zeros((16, 256), I32)
        for r in range(16):
            hit = jnp.sum(jnp.where(dest == base + r, ident + 1, 0), axis=1, keepdims=True)
            ids = jnp.where((lane & 15) == r, hit, ids)
        ids = jnp.sum(jnp.where((lane >> 4) == iota((16, 256), 0), ids, 0), axis=0, keepdims=True) - 1
        turn = jnp.where(y == 0, 1, 0) if dy < 0 else jnp.where(y == 3, -1, 0) if dy > 0 else 0
        return ids, (ids >> 4) + turn, (ids >> 2) & 3, (ids >> 1) & 1, ids & 1

    def put(k, ids, target):
        out[pl.ds(k * 64, 64), :] = jnp.where(
            (iota((64, 256), 0) == target) & (ids >= 0), 1.0, 0.0
        ).astype(BF16)

    ids, *_ = idents(0, 0)
    put(0, ids, ids)
    for k, dx in enumerate((-1, 1)):
        ids, z, layer, _, pc = idents(dx, 0)
        put(1 + k, ids, z * 16 + k * 8 + layer * 2 + pc)
    for k, dy in enumerate((-1, 1)):
        ids, z, layer, pr, _ = idents(0, dy)
        put(3 + k, ids, z * 16 + k * 8 + layer * 2 + pr)
    for k in range(4):
        ids, z, layer, _, _ = idents((k >> 1) * 2 - 1, (k & 1) * 2 - 1)
        put(5 + k, ids, z * 16 + layer)


def combine_kernel(selector, received, _to_left, _to_right, out):
    def add(k, start, width):
        return jnp.dot(
            selector[k * 64 : (k + 1) * 64, :],
            received[:, start : start + width],
            preferred_element_type=F32,
        )

    for k in range(8):
        out[:, k * 512 : (k + 1) * 512] = add(0, k * 512, 512)
    out[:, 4096:4224] = add(1, 4096, 128) + add(2, 4224, 128)
    out[:, 4224:4352] = add(3, 4352, 128) + add(4, 4480, 128)
    lane = iota((64, 128), 1)
    corners = jnp.zeros((64, 128), F32)
    for k in range(4):
        corners = jnp.where(lane == k, add(5 + k, 4608, 128), corners)
    out[:, 4352:4480] = corners


def unpack_kernel(whole, _left, _right, density, main, side, up, down, turned):
    for k in range(32):
        turned[k * 16 : (k + 1) * 16, :] = whole[:, k * 128 : (k + 1) * 128]
    low = iota((32, 128), 1) < 64
    lane = iota((64, 128), 1)
    low_row = iota((1, 128), 1) < 64
    lane16, row16 = iota((16, 128), 1), iota((16, 128), 0)
    rows, columns, corners = whole[:, 4096:4224], whole[:, 4224:4352], whole[:, 4352:4480]
    cell = iota((64, 128), 0)
    turn = []
    for c in range(2):
        pick = jnp.where(lane == (cell & 1) * 64 + (cell - (cell & 1)) + c, 1.0, 0.0)
        turn.append(
            lax.dot_general(
                pick, columns, (((1,), (1,)), ((), ())),
                precision=lax.Precision.HIGHEST, preferred_element_type=F32,
            )
        )
    for layer in range(4):
        base = layer * 144
        for r in range(2):
            left = turned[pl.ds(layer * 4 + r * 2, 32, stride=16), :]
            right = turned[pl.ds(layer * 4 + r * 2 + 1, 32, stride=16), :]
            at = base + r * 64
            main[pl.ds(at, 32, stride=2), :] = jnp.where(low, left, pltpu.roll(right, 64, 1))
            main[pl.ds(at + 1, 32, stride=2), :] = jnp.where(low, pltpu.roll(left, 64, 1), right)
            k = layer * 2 + r
            strip = jnp.where(lane == 0, turn[0][:, 8 + k : 9 + k], 0.0)
            strip = jnp.where(lane == 1, turn[1][:, 8 + k : 9 + k], strip)
            strip = jnp.where(lane == 126, turn[0][:, k : k + 1], strip)
            side[at : at + 64, :] = jnp.where(lane == 127, turn[1][:, k : k + 1], strip)
        block = jnp.zeros((16, 128), F32)
        for kind, first_row in ((0, 14), (1, 0)):
            k = kind * 8 + layer * 2
            a, b = rows[k : k + 1, :], rows[k + 1 : k + 2, :]
            first = jnp.where(low_row, a, pltpu.roll(b, 64, 1))
            second = jnp.where(low_row, pltpu.roll(a, 64, 1), b)
            block = jnp.where(row16 == first_row, first, block)
            block = jnp.where(row16 == first_row + 1, second, block)
        main[base + 128 : base + 144, :] = block
        block = jnp.zeros((16, 128), F32)
        for k, (r, at_lane) in enumerate(((15, 127), (15, 0), (0, 127), (0, 0))):
            value = corners[layer : layer + 1, k : k + 1]
            block = jnp.where((row16 == r) & (lane16 == at_lane), value, block)
        side[base + 128 : base + 144, :] = block
        density[layer * 128 : (layer + 1) * 128, :] = main[base : base + 128, :]
    for out, first in ((up, 288), (down, 0)):
        out[0:288, :] = main[first : first + 288, :].astype(BF16)
        second = side[first + 144 : first + 288, :]
        out[288:432, :] = (side[first : first + 144, :] + pltpu.roll(second, 4, 1)).astype(BF16)


def depth(a):
    return 3 if a < 2 else 2


def beyond(lo, hi, a, layer):
    if layer < 3:
        k = layer - 3 + depth(a)
        return (lo, 3 * a + k) if k >= 0 else None
    k = layer - 7
    return (hi, 3 * a + k) if k < depth(a) else None


def layers_kernel(temp, cond, mass, own, up, down, sems):
    copies = [pltpu.make_async_copy(a, own.at[i], sems.at[i]) for i, a in enumerate((temp, cond, mass))]
    for copy in copies:
        copy.start()
    for a, copy in enumerate(copies):
        copy.wait()
        for k in range(depth(a)):
            up[3 * a + k] = own[a, 4 - depth(a) + k].astype(BF16)
            down[3 * a + k] = own[a, k].astype(BF16)


def rows_kernel(own, lo, hi, last, first):
    lasts, firsts = [], []
    for a in range(3):
        for layer in range(10):
            if 3 <= layer < 7:
                lasts.append(own[a, layer - 3, 120:128, :])
                firsts.append(own[a, layer - 3, 0:8, :])
            elif found := beyond(lo, hi, a, layer):
                source, k = found
                lasts.append(source[k, 112:128, :].astype(F32)[8:16])
                firsts.append(source[k, 0:16, :].astype(F32)[0:8])
            else:
                lasts.append(jnp.zeros((8, 128), F32))
                firsts.append(jnp.zeros((8, 128), F32))
    last[...] = jnp.concatenate(lasts, axis=0).astype(BF16)
    first[...] = jnp.concatenate(firsts, axis=0).astype(BF16)


def gather_kernel(own, lo, hi, above, below, out, to_left, to_right):
    over, under = above[...].astype(F32), below[...].astype(F32)
    lane = iota((144, 128), 1)
    left, right = jnp.zeros((144, 128), F32), jnp.zeros((144, 128), F32)
    for a in range(3):
        for layer in range(10):
            i = a * 10 + layer
            if 3 <= layer < 7:
                source = own[a, layer - 3]
            elif found := beyond(lo, hi, a, layer):
                source = found[0][found[1]].astype(F32)
            else:
                source = jnp.zeros((128, 128), F32)
            piece = jnp.concatenate([source, under[8 * i : 8 * i + 8], over[8 * i : 8 * i + 8]], axis=0)
            out[i] = piece
            base = a * 40 + layer * 4
            here = (lane >= base) & (lane < base + 3)
            left = jnp.where(here, pltpu.roll(piece, base, 1) if base else piece, left)
            right = jnp.where(here, pltpu.roll(piece, base + 3, 1), right)
    to_left[...] = left.astype(BF16)
    to_right[...] = right.astype(BF16)


def turned_by(x, shift, axis):
    return pltpu.roll(x, shift % x.shape[axis], axis)


def around(face_row, face_col, v):
    return (
        face_row * turned_by(v, -1, 0)
        + turned_by(face_row * v, 1, 0)
        + face_col * turned_by(v, -1, 1)
        + turned_by(face_col * v, 1, 1)
    )


def operator_kernel(grids, from_left, from_right, face_layer, face_row, face_col, inverse, residual, wide):
    left, right = from_left[...].astype(F32), from_right[...].astype(F32)
    lane = iota((144, 128), 1)
    for a in range(3):
        for layer in range(10):
            i, base = a * 10 + layer, a * 40 + layer * 4
            high = turned_by(right, -base, 1) if base else right
            side = jnp.where(lane < 3, high, jnp.where(lane >= 125, turned_by(left, 125 - base, 1), 0.0))
            wide[i, :, 0:128] = grids[i]
            wide[i, :, 128:256] = side
    for layer in range(9):
        face_layer[layer] = 0.5 * (wide[10 + layer] + wide[11 + layer])
    for layer in range(1, 9):
        temp, cond, mass = (wide[a * 10 + layer] for a in range(3))
        rows = 0.5 * (cond + turned_by(cond, -1, 0))
        cols = 0.5 * (cond + turned_by(cond, -1, 1))
        face_row[layer - 1] = rows
        face_col[layer - 1] = cols
        after, before = face_layer[layer], face_layer[layer - 1]
        diagonal = mass + after + before + rows + turned_by(rows, 1, 0) + cols + turned_by(cols, 1, 1)
        share = after * wide[layer + 1] + before * wide[layer - 1] + around(rows, cols, temp)
        residual[layer - 1] = mass * temp + (share - diagonal * temp)
        inverse[layer - 1] = jnp.where(mass > 0.0, 1.0 / diagonal, 0.0)


MIDDLE = (eig_low + eig_high) / 2.0
SPREAD = (eig_high - eig_low) / 2.0
W0 = SPREAD / MIDDLE
W1 = 1.0 / (2.0 * MIDDLE / SPREAD - W0)
W2 = 1.0 / (2.0 * MIDDLE / SPREAD - W1)


def sweep_kernel(main, side, lo, hi, grids, face_layer, face_row, face_col, inverse, residual, out, d0, d1, rest):
    lane = iota((144, 128), 1)
    kept = (lane < 2) | (lane >= 126)

    def supplied(i):
        if 3 <= i <= 6:
            at = (i - 3) * 144
            return main[at : at + 144, :], side[at : at + 144, :]
        source, second = (lo, i == 2) if i < 3 else (hi, i == 8)
        at = 144 if second else 0
        beside = source[288:432, :].astype(F32)
        if second:
            beside = turned_by(beside, -4, 1)
        return source[at : at + 144, :].astype(F32), jnp.where(kept, beside, 0.0)

    for i in range(1, 9):
        start = residual[i - 1] + jnp.concatenate(supplied(i), axis=1)
        rest[i - 1] = start
        d0[i - 1] = start * inverse[i - 1] * (1.0 / MIDDLE)

    def share(i, d):
        return (
            face_layer[i] * d[i]
            + face_layer[i - 1] * d[i - 2]
            + around(face_row[i - 1], face_col[i - 1], d[i - 1])
        )

    for i in range(2, 8):
        start = rest[i - 1]
        later = start * (1.0 - 1.0 / MIDDLE) + share(i, d0)
        d1[i - 1] = W1 * W0 * d0[i - 1] + (2.0 * W1 / SPREAD) * (later * inverse[i - 1])
        rest[i - 1] = later - (W1 * W0 / MIDDLE) * start - (2.0 * W1 / SPREAD) * later
    for i in range(3, 7):
        last = rest[i - 1] + share(i, d1)
        step = d0[i - 1] + d1[i - 1] * (1.0 + W2 * W1) + (2.0 * W2 / SPREAD) * (last * inverse[i - 1])
        at = (i - 3) * 128
        out[at : at + 128, :] = grids[i, 0:128, :] + step[0:128, 0:128]


def sds(shape, dtype):
    return jax.ShapeDtypeStruct(shape, dtype)


def call(kernel, shape, args, mib=16, scratch=(), far=(), far_out=False):
    vmem, anywhere = pl.BlockSpec(memory_space=pltpu.VMEM), pl.BlockSpec(memory_space=pltpu.HBM)
    return pl.pallas_call(
        kernel,
        out_shape=shape,
        in_specs=[anywhere if i in far else vmem for i in range(len(args))],
        out_specs=jax.tree.map(lambda _: anywhere if far_out else vmem, shape),
        scratch_shapes=list(scratch),
        compiler_params=pltpu.CompilerParams(vmem_limit_bytes=mib * 2**20),
    )(*args)


def pairs(axis):
    up = [(i, i + 1) for i in range(lax.axis_size(axis) - 1)]
    return up, [(b, a) for a, b in up]


def exchange(to_next, to_last, axis):
    up, down = pairs(axis)
    return lax.ppermute(to_next, axis, up), lax.ppermute(to_last, axis, down)


def extended_grids(temp, cond, mass):
    eight, rows, edge = sds((8, 128, 128), BF16), sds((240, 128), BF16), sds((144, 128), BF16)
    own, up, down = call(
        layers_kernel,
        (sds((3, 4, 128, 128), F32), eight, eight),
        (temp, cond, mass),
        scratch=[pltpu.SemaphoreType.DMA((3,))],
        far=range(3),
    )
    lo, hi = exchange(up, down, LAYER)
    above, below = exchange(*call(rows_kernel, (rows, rows), (own, lo, hi)), "row")
    wide, to_left, to_right = call(
        gather_kernel, (sds((30, 144, 128), F32), edge, edge), (own, lo, hi, above, below), mib=24
    )
    return wide, (to_left, to_right), exchange(to_right, to_left, COL)


def operator(wide, from_left, from_right):
    eight = sds((8, 144, 256), F32)
    return call(
        operator_kernel,
        (sds((9, 144, 256), F32), eight, eight, eight, eight),
        (wide, from_left, from_right),
        mib=32,
        scratch=[pltpu.VMEM((30, 144, 256), F32)],
    )


def shards(temp, cond, mass, toggling, baseline, panel, place, holder, tier, warming):
    row64 = pltpu.VMEM((1, 64), I32)
    message, placing, columns = call(
        message_kernel,
        (sds((64, 128), F32), sds((1024, 64), BF16), sds((64, 128), I32)),
        (temp, panel.reshape(1, 64), place, holder, tier),
        mib=60,
        scratch=[
            pltpu.VMEM((4, 128, 128), F32), row64, row64, row64,
            pltpu.VMEM((1, 16), I32), pltpu.SemaphoreType.DMA((5,)),
        ],
        far=range(5),
    )
    messages = lax.all_to_all(message.reshape(64, 1, 128), CUBE, split_axis=0, concat_axis=0, tiled=True)
    messages = messages.reshape(64, 128)
    send = call(
        power_kernel,
        sds((256, 4736), BF16),
        (messages, columns, warming, toggling[0], baseline[0], placing),
        mib=60,
        scratch=[
            pltpu.VMEM((64, 128), F32), pltpu.VMEM((64, 128), I32), pltpu.VMEM((1, 16), F32),
            pltpu.VMEM((64, 4096), BF16), pltpu.VMEM((64, 4096), BF16), pltpu.VMEM((1024, 64), BF16),
            pltpu.VMEM((256, 4736), BF16), pltpu.SemaphoreType.DMA((15,)),
        ],
        far=range(6),
        far_out=True,
    )
    received = lax.all_to_all(send.reshape(16, 16, 4736), PLANE, split_axis=0, concat_axis=0, tiled=True)
    selector = call(selector_kernel, sds((576, 256), BF16), (messages,))
    wide, edges, beside = extended_grids(temp, cond, mass)
    partial = call(
        combine_kernel, sds((64, 4480), F32), (selector, received.reshape(256, 4736), *edges)
    )
    parts = lax.all_to_all(
        partial.astype(jnp.float16).reshape(4, 16, 4480), "zlo", split_axis=0, concat_axis=0, tiled=True
    )
    terms = operator(wide, *beside)
    block, strip = sds((576, 128), F32), sds((432, 128), BF16)
    density, main, side, up, down = call(
        unpack_kernel,
        (sds((512, 128), F32), block, block, strip, strip),
        (jnp.sum(parts.astype(F32), axis=0), *beside),
        scratch=[pltpu.VMEM((512, 128), F32)],
    )
    lo, hi = exchange(up, down, LAYER)
    eight = pltpu.VMEM((8, 144, 256), F32)
    guess = call(
        sweep_kernel,
        sds((512, 128), F32),
        (main, side, lo, hi, wide, *terms),
        mib=40,
        scratch=[eight, eight, eight],
    )
    return guess.reshape(4, 128, 128), density.reshape(4, 128, 128)


def solution(mesh):
    fine = Mesh(mesh.devices.reshape(4, 4, 4, 4, 2), ("row", "zlo", "y", "zhi", "core"))
    grid = P(LAYER, "row", COL)
    slot = ("row", "zlo", "y", "zhi", "core")
    return jax.shard_map(
        shards,
        mesh=fine,
        in_specs=(
            grid,
            grid,
            grid,
            P(slot, None, None),
            P(slot, None, None),
            P(slot, None, None),
            P(slot, None),
            P(slot, None),
            P(slot, None),
            P(slot, None),
        ),
        out_specs=(grid, grid),
        check_vma=False,
    )
```

```python
import jax
import jax.numpy as jnp
from jax import lax
from jax.experimental import pallas as pl
from jax.experimental.pallas import tpu as pltpu
from jax.sharding import Mesh
from jax.sharding import PartitionSpec as P

eig_low = 0.1
eig_high = 2.0

LAYER = ("zhi", "core")
COL = ("zlo", "y")
CUBE = ("row", "zlo", "y")
PLANE = ("row", "y")

F32, BF16, I32 = jnp.float32, jnp.bfloat16, jnp.int32


def iota(shape, dim):
    return lax.broadcasted_iota(I32, shape, dim)


def as_column(row):
    n = row.shape[1]
    return jnp.sum(jnp.where(iota((n, n), 0) == iota((n, n), 1), row, 0), axis=1, keepdims=True)


def slot_rows(panel, place, holder, tier):
    layer = jnp.sum(jnp.where(iota((16, 64), 0) == holder, as_column(tier), 0), axis=0, keepdims=True)
    pos = layer * 4 + place
    ident = ((panel >> 2) & 3) * 16 + pos
    column = (panel >> 4) * 4 + (panel & 3)
    same = (as_column(column) == column) & (iota((64, 64), 0) < iota((64, 64), 1))
    rank = jnp.sum(same.astype(I32), axis=0, keepdims=True)
    return pos, ident, column * 16 + rank


def place_slots(panel, pos, dest, holder, placing, columns):
    x, y, rank = panel >> 4, panel & 3, dest & 15
    lower, right = (pos >> 1) & 1, pos & 1
    next_x = x + lower * 2 - 1
    next_y = (y + right * 2 + 3) & 3
    inside = (next_x >= 0) & (next_x <= 3)
    targets = (
        dest,
        jnp.where(inside, (next_x * 4 + y) * 16 + rank, -1),
        (x * 4 + next_y) * 16 + rank,
        jnp.where(inside, (next_x * 4 + next_y) * 16 + rank, -1),
    )
    for k, target in enumerate(targets):
        placing[pl.ds(k * 256, 256), :] = jnp.where(iota((256, 64), 0) == target, 1.0, 0.0).astype(BF16)
    lane = iota((64, 128), 1)
    columns[...] = jnp.where(
        lane == 0, as_column(panel), jnp.where(lane == 1, as_column(pos), as_column(holder))
    )


def depth(a):
    return 3 if a < 2 else 2


def message_kernel(
    temp, cond, mass, panel, place, holder, tier, out, placing, columns, own, up, down,
    panel_v, place_v, holder_v, tier_v, sems,
):
    pairs = [(panel, panel_v), (place, place_v), (holder, holder_v), (tier, tier_v)]
    pairs += [(grid, own.at[a]) for a, grid in enumerate((temp, cond, mass))]
    copies = [pltpu.make_async_copy(a, b, sems.at[i]) for i, (a, b) in enumerate(pairs)]
    for copy in copies:
        copy.start()
    for copy in copies[:4]:
        copy.wait()
    panel_row, holder_row = panel_v[...], holder_v[...]
    pos, ident, dest = slot_rows(panel_row, place_v[...], holder_row, tier_v[...])
    place_slots(panel_row, pos, dest, holder_row, placing, columns)
    code = (dest * 64 + ident).astype(F32)
    for a in range(3):
        copies[4 + a].wait()
        for k in range(depth(a)):
            up[3 * a + k] = own[a, 4 - depth(a) + k].astype(BF16)
            down[3 * a + k] = own[a, k].astype(BF16)
    sums = jnp.sum(own[0].reshape(8, 64, 128), axis=1)
    lane = iota((8, 128), 1)
    first = jnp.sum(jnp.where(lane < 64, sums, 0.0), axis=1, keepdims=True)
    second = jnp.sum(jnp.where(lane < 64, 0.0, sums), axis=1, keepdims=True)
    at = iota((8, 128), 0) * 2
    means = jnp.where(lane == at, first, jnp.where(lane == at + 1, second, 0.0))
    means = jnp.sum(means, axis=0, keepdims=True) * (1.0 / 4096.0)
    row = jnp.where(iota((1, 128), 1) < 64, means, jnp.concatenate([code, code], axis=1))
    out[...] = jnp.broadcast_to(row, (64, 128))


def power_kernel(
    far_messages, far_columns, far_warming, far_toggling, far_baseline, far_placing, _lo, _hi, out,
    messages, columns, warming, toggling, baseline, placing, sent, sems,
):
    pairs = [
        (far_messages, messages),
        (far_columns, columns),
        (far_warming, warming),
        (far_toggling, toggling),
        (far_baseline, baseline),
        (far_placing, placing),
    ]
    loads = [pltpu.make_async_copy(a, b, sems.at[9 + i]) for i, (a, b) in enumerate(pairs)]
    for load in loads:
        load.start()
    loads[0].wait()
    loads[1].wait()
    tile, pos, holder = (columns[:, k : k + 1] for k in range(3))
    lower, right = (pos >> 1) & 1, pos & 1
    pick = jnp.where(iota((64, 64), 1) == tile, 1.0, 0.0)
    means = jnp.dot(pick, messages[...], precision=lax.Precision.HIGHEST, preferred_element_type=F32)
    lane = iota((64, 128), 1)
    slot_mean = jnp.sum(jnp.where(lane == pos, means, 0.0), axis=1, keepdims=True)
    member = iota((64, 16), 1) == holder
    total = jnp.sum(jnp.where(member, slot_mean, 0.0), axis=0, keepdims=True)
    count = jnp.sum(jnp.where(member, 1.0, 0.0), axis=0, keepdims=True)
    loads[2].wait()
    leak = jnp.exp(warming[...] * (total / count))
    factor = jnp.sum(jnp.where(member, leak, 0.0), axis=1, keepdims=True)

    def place(kind, values):
        at = placing[kind * 256 : (kind + 1) * 256, :]
        return jnp.dot(at, values.astype(BF16), preferred_element_type=F32).astype(BF16)

    copies = []

    def send(start, width):
        at = pl.ds(start, width)
        copy = pltpu.make_async_copy(sent.at[:, at], out.at[:, at], sems.at[len(copies)])
        copy.start()
        copies.append(copy)

    for load in loads[3:]:
        load.wait()
    edge = ((lane & 63) >> 1) == right * 31
    sides = jnp.zeros((64, 128), F32)
    width = 512
    for k in range(8):
        at = pl.ds(k * width, width)
        power = (toggling[:, at].astype(F32) + factor * baseline[:, at].astype(F32)).astype(BF16)
        sent[:, at] = place(0, power)
        send(k * width, width)
        power = power.astype(F32)
        for t in range(4):
            piece = power[:, t * 128 : (t + 1) * 128]
            shift = 2 * (4 * k + t)
            kept = jnp.where(edge, piece, 0.0)
            sides = sides + (pltpu.roll(kept, shift, 1) if shift else kept)
            if k == 0 and t == 0:
                top = piece
    rows = jnp.where(lower == 0, top, piece)
    sides = jnp.where(right == 0, sides, pltpu.roll(sides, 66, 1))
    corner = jnp.sum(jnp.where(lane == lower * 64 + right * 63, rows, 0.0), axis=1, keepdims=True)
    quarter = (1 - lower) * 2 + 1 - right
    both = jnp.concatenate([jnp.where(lower == 1, rows, 0.0), jnp.where(lower == 0, rows, 0.0)], axis=1)
    sent[:, 4096:4352] = place(1, both)
    both = jnp.concatenate([jnp.where(right == 1, sides, 0.0), jnp.where(right == 0, sides, 0.0)], axis=1)
    sent[:, 4352:4608] = place(2, both)
    sent[:, 4608:4736] = place(3, jnp.where(lane == quarter, corner, 0.0))
    send(4096, 640)
    for copy in copies:
        copy.wait()


def selector_kernel(messages, out):
    x, y = lax.axis_index("row"), lax.axis_index("y")
    plane = lax.axis_index("zlo")
    code = jnp.concatenate([messages[pl.ds(r * 16 + plane * 4, 4), :] for r in range(4)], axis=0)
    code = jnp.where(iota((16, 128), 1) < 64, -1.0, code).astype(I32)
    dest, ident = code >> 6, code & 63
    lane = iota((16, 256), 1)

    def idents(dx, dy):
        base = ((x + dx) * 4 + ((y + dy + 4) & 3)) * 16
        ids = jnp.zeros((16, 256), I32)
        for r in range(16):
            hit = jnp.sum(jnp.where(dest == base + r, ident + 1, 0), axis=1, keepdims=True)
            ids = jnp.where((lane & 15) == r, hit, ids)
        ids = jnp.sum(jnp.where((lane >> 4) == iota((16, 256), 0), ids, 0), axis=0, keepdims=True) - 1
        turn = jnp.where(y == 0, 1, 0) if dy < 0 else jnp.where(y == 3, -1, 0) if dy > 0 else 0
        return ids, (ids >> 4) + turn, (ids >> 2) & 3, (ids >> 1) & 1, ids & 1

    def put(k, ids, target):
        out[pl.ds(k * 64, 64), :] = jnp.where(
            (iota((64, 256), 0) == target) & (ids >= 0), 1.0, 0.0
        ).astype(BF16)

    ids, *_ = idents(0, 0)
    put(0, ids, ids)
    for k, dx in enumerate((-1, 1)):
        ids, z, layer, _, pc = idents(dx, 0)
        put(1 + k, ids, z * 16 + k * 8 + layer * 2 + pc)
    for k, dy in enumerate((-1, 1)):
        ids, z, layer, pr, _ = idents(0, dy)
        put(3 + k, ids, z * 16 + k * 8 + layer * 2 + pr)
    for k in range(4):
        ids, z, layer, _, _ = idents((k >> 1) * 2 - 1, (k & 1) * 2 - 1)
        put(5 + k, ids, z * 16 + layer)


def combine_kernel(selector, received, _to_left, _to_right, out):
    def add(k, start, width):
        return jnp.dot(
            selector[k * 64 : (k + 1) * 64, :],
            received[:, start : start + width],
            preferred_element_type=F32,
        )

    for k in range(8):
        out[:, k * 512 : (k + 1) * 512] = add(0, k * 512, 512)
    out[:, 4096:4224] = add(1, 4096, 128) + add(2, 4224, 128)
    out[:, 4224:4352] = add(3, 4352, 128) + add(4, 4480, 128)
    lane = iota((64, 128), 1)
    corners = jnp.zeros((64, 128), F32)
    for k in range(4):
        corners = jnp.where(lane == k, add(5 + k, 4608, 128), corners)
    out[:, 4352:4480] = corners


def unpack_kernel(whole, _left, _right, density, main, side, up, down, turned):
    for k in range(32):
        turned[k * 16 : (k + 1) * 16, :] = whole[:, k * 128 : (k + 1) * 128]
    low = iota((32, 128), 1) < 64
    lane = iota((64, 128), 1)
    low_row = iota((1, 128), 1) < 64
    lane16, row16 = iota((16, 128), 1), iota((16, 128), 0)
    rows, columns, corners = whole[:, 4096:4224], whole[:, 4224:4352], whole[:, 4352:4480]
    cell = iota((64, 128), 0)
    turn = []
    for c in range(2):
        pick = jnp.where(lane == (cell & 1) * 64 + (cell - (cell & 1)) + c, 1.0, 0.0)
        turn.append(
            lax.dot_general(
                pick, columns, (((1,), (1,)), ((), ())),
                precision=lax.Precision.HIGHEST, preferred_element_type=F32,
            )
        )
    for layer in range(4):
        base = layer * 144
        for r in range(2):
            left = turned[pl.ds(layer * 4 + r * 2, 32, stride=16), :]
            right = turned[pl.ds(layer * 4 + r * 2 + 1, 32, stride=16), :]
            at = base + r * 64
            main[pl.ds(at, 32, stride=2), :] = jnp.where(low, left, pltpu.roll(right, 64, 1))
            main[pl.ds(at + 1, 32, stride=2), :] = jnp.where(low, pltpu.roll(left, 64, 1), right)
            k = layer * 2 + r
            strip = jnp.where(lane == 0, turn[0][:, 8 + k : 9 + k], 0.0)
            strip = jnp.where(lane == 1, turn[1][:, 8 + k : 9 + k], strip)
            strip = jnp.where(lane == 126, turn[0][:, k : k + 1], strip)
            side[at : at + 64, :] = jnp.where(lane == 127, turn[1][:, k : k + 1], strip)
        block = jnp.zeros((16, 128), F32)
        for kind, first_row in ((0, 14), (1, 0)):
            k = kind * 8 + layer * 2
            a, b = rows[k : k + 1, :], rows[k + 1 : k + 2, :]
            first = jnp.where(low_row, a, pltpu.roll(b, 64, 1))
            second = jnp.where(low_row, pltpu.roll(a, 64, 1), b)
            block = jnp.where(row16 == first_row, first, block)
            block = jnp.where(row16 == first_row + 1, second, block)
        main[base + 128 : base + 144, :] = block
        block = jnp.zeros((16, 128), F32)
        for k, (r, at_lane) in enumerate(((15, 127), (15, 0), (0, 127), (0, 0))):
            value = corners[layer : layer + 1, k : k + 1]
            block = jnp.where((row16 == r) & (lane16 == at_lane), value, block)
        side[base + 128 : base + 144, :] = block
        density[layer * 128 : (layer + 1) * 128, :] = main[base : base + 128, :]
    for out, first in ((up, 288), (down, 0)):
        out[0:288, :] = main[first : first + 288, :].astype(BF16)
        second = side[first + 144 : first + 288, :]
        out[288:432, :] = (side[first : first + 144, :] + pltpu.roll(second, 4, 1)).astype(BF16)


def beyond(lo, hi, a, layer):
    if layer < 3:
        k = layer - 3 + depth(a)
        return (lo, 3 * a + k) if k >= 0 else None
    k = layer - 7
    return (hi, 3 * a + k) if k < depth(a) else None


def rows_kernel(own, lo, hi, last, first):
    lasts, firsts = [], []
    for a in range(3):
        for layer in range(10):
            if 3 <= layer < 7:
                lasts.append(own[a, layer - 3, 120:128, :])
                firsts.append(own[a, layer - 3, 0:8, :])
            elif found := beyond(lo, hi, a, layer):
                source, k = found
                lasts.append(source[k, 112:128, :].astype(F32)[8:16])
                firsts.append(source[k, 0:16, :].astype(F32)[0:8])
            else:
                lasts.append(jnp.zeros((8, 128), F32))
                firsts.append(jnp.zeros((8, 128), F32))
    last[...] = jnp.concatenate(lasts, axis=0).astype(BF16)
    first[...] = jnp.concatenate(firsts, axis=0).astype(BF16)


def gather_kernel(own, lo, hi, above, below, out, to_left, to_right):
    over, under = above[...].astype(F32), below[...].astype(F32)
    lane = iota((144, 128), 1)
    left, right = jnp.zeros((144, 128), F32), jnp.zeros((144, 128), F32)
    for a in range(3):
        for layer in range(10):
            i = a * 10 + layer
            if 3 <= layer < 7:
                source = own[a, layer - 3]
            elif found := beyond(lo, hi, a, layer):
                source = found[0][found[1]].astype(F32)
            else:
                source = jnp.zeros((128, 128), F32)
            piece = jnp.concatenate([source, under[8 * i : 8 * i + 8], over[8 * i : 8 * i + 8]], axis=0)
            out[i] = piece
            base = a * 40 + layer * 4
            here = (lane >= base) & (lane < base + 3)
            left = jnp.where(here, pltpu.roll(piece, base, 1) if base else piece, left)
            right = jnp.where(here, pltpu.roll(piece, base + 3, 1), right)
    to_left[...] = left.astype(BF16)
    to_right[...] = right.astype(BF16)


def turned_by(x, shift, axis):
    return pltpu.roll(x, shift % x.shape[axis], axis)


def around(face_row, face_col, v):
    return (
        face_row * turned_by(v, -1, 0)
        + turned_by(face_row * v, 1, 0)
        + face_col * turned_by(v, -1, 1)
        + turned_by(face_col * v, 1, 1)
    )


def operator_kernel(grids, from_left, from_right, face_layer, face_row, face_col, inverse, residual, wide):
    left, right = from_left[...].astype(F32), from_right[...].astype(F32)
    lane = iota((144, 128), 1)
    for a in range(3):
        for layer in range(10):
            i, base = a * 10 + layer, a * 40 + layer * 4
            high = turned_by(right, -base, 1) if base else right
            side = jnp.where(lane < 3, high, jnp.where(lane >= 125, turned_by(left, 125 - base, 1), 0.0))
            wide[i, :, 0:128] = grids[i]
            wide[i, :, 128:256] = side
    for layer in range(9):
        face_layer[layer] = 0.5 * (wide[10 + layer] + wide[11 + layer])
    for layer in range(1, 9):
        temp, cond, mass = (wide[a * 10 + layer] for a in range(3))
        rows = 0.5 * (cond + turned_by(cond, -1, 0))
        cols = 0.5 * (cond + turned_by(cond, -1, 1))
        face_row[layer - 1] = rows
        face_col[layer - 1] = cols
        after, before = face_layer[layer], face_layer[layer - 1]
        diagonal = mass + after + before + rows + turned_by(rows, 1, 0) + cols + turned_by(cols, 1, 1)
        share = after * wide[layer + 1] + before * wide[layer - 1] + around(rows, cols, temp)
        residual[layer - 1] = mass * temp + (share - diagonal * temp)
        inverse[layer - 1] = jnp.where(mass > 0.0, 1.0 / diagonal, 0.0)


MIDDLE = (eig_low + eig_high) / 2.0
SPREAD = (eig_high - eig_low) / 2.0
W0 = SPREAD / MIDDLE
W1 = 1.0 / (2.0 * MIDDLE / SPREAD - W0)
W2 = 1.0 / (2.0 * MIDDLE / SPREAD - W1)


def sweep_kernel(main, side, lo, hi, grids, face_layer, face_row, face_col, inverse, residual, out, d0, d1, rest):
    lane = iota((144, 128), 1)
    kept = (lane < 2) | (lane >= 126)

    def supplied(i):
        if 3 <= i <= 6:
            at = (i - 3) * 144
            return main[at : at + 144, :], side[at : at + 144, :]
        source, second = (lo, i == 2) if i < 3 else (hi, i == 8)
        at = 144 if second else 0
        beside = source[288:432, :].astype(F32)
        if second:
            beside = turned_by(beside, -4, 1)
        return source[at : at + 144, :].astype(F32), jnp.where(kept, beside, 0.0)

    for i in range(1, 9):
        start = residual[i - 1] + jnp.concatenate(supplied(i), axis=1)
        rest[i - 1] = start
        d0[i - 1] = start * inverse[i - 1] * (1.0 / MIDDLE)

    def share(i, d):
        return (
            face_layer[i] * d[i]
            + face_layer[i - 1] * d[i - 2]
            + around(face_row[i - 1], face_col[i - 1], d[i - 1])
        )

    for i in range(2, 8):
        start = rest[i - 1]
        later = start * (1.0 - 1.0 / MIDDLE) + share(i, d0)
        d1[i - 1] = W1 * W0 * d0[i - 1] + (2.0 * W1 / SPREAD) * (later * inverse[i - 1])
        rest[i - 1] = later - (W1 * W0 / MIDDLE) * start - (2.0 * W1 / SPREAD) * later
    for i in range(3, 7):
        last = rest[i - 1] + share(i, d1)
        step = d0[i - 1] + d1[i - 1] * (1.0 + W2 * W1) + (2.0 * W2 / SPREAD) * (last * inverse[i - 1])
        at = (i - 3) * 128
        out[at : at + 128, :] = grids[i, 0:128, :] + step[0:128, 0:128]


def sds(shape, dtype):
    return jax.ShapeDtypeStruct(shape, dtype)


def call(kernel, shape, args, mib=16, scratch=(), far=(), far_out=False):
    vmem, anywhere = pl.BlockSpec(memory_space=pltpu.VMEM), pl.BlockSpec(memory_space=pltpu.HBM)
    return pl.pallas_call(
        kernel,
        out_shape=shape,
        in_specs=[anywhere if i in far else vmem for i in range(len(args))],
        out_specs=jax.tree.map(lambda _: anywhere if far_out else vmem, shape),
        scratch_shapes=list(scratch),
        compiler_params=pltpu.CompilerParams(vmem_limit_bytes=mib * 2**20),
    )(*args)


def pairs(axis):
    up = [(i, i + 1) for i in range(lax.axis_size(axis) - 1)]
    return up, [(b, a) for a, b in up]


def exchange(to_next, to_last, axis):
    up, down = pairs(axis)
    return lax.ppermute(to_next, axis, up), lax.ppermute(to_last, axis, down)


def extended_grids(own, lo, hi):
    rows, edge = sds((240, 128), BF16), sds((144, 128), BF16)
    above, below = exchange(*call(rows_kernel, (rows, rows), (own, lo, hi)), "row")
    wide, to_left, to_right = call(
        gather_kernel, (sds((30, 144, 128), F32), edge, edge), (own, lo, hi, above, below), mib=24
    )
    return wide, (to_left, to_right), exchange(to_right, to_left, COL)


def operator(wide, from_left, from_right):
    eight = sds((8, 144, 256), F32)
    return call(
        operator_kernel,
        (sds((9, 144, 256), F32), eight, eight, eight, eight),
        (wide, from_left, from_right),
        mib=32,
        scratch=[pltpu.VMEM((30, 144, 256), F32)],
    )


def shards(temp, cond, mass, toggling, baseline, panel, place, holder, tier, warming):
    row64 = pltpu.VMEM((1, 64), I32)
    eight = sds((8, 128, 128), BF16)
    message, placing, columns, own, up, down = call(
        message_kernel,
        (
            sds((64, 128), F32), sds((1024, 64), BF16), sds((64, 128), I32),
            sds((3, 4, 128, 128), F32), eight, eight,
        ),
        (temp, cond, mass, panel.reshape(1, 64), place, holder, tier),
        mib=60,
        scratch=[row64, row64, row64, pltpu.VMEM((1, 16), I32), pltpu.SemaphoreType.DMA((7,))],
        far=range(7),
    )
    lo, hi = exchange(up, down, LAYER)
    messages = lax.all_to_all(message.reshape(64, 1, 128), CUBE, split_axis=0, concat_axis=0, tiled=True)
    messages = messages.reshape(64, 128)
    send = call(
        power_kernel,
        sds((256, 4736), BF16),
        (messages, columns, warming, toggling[0], baseline[0], placing, lo, hi),
        mib=60,
        scratch=[
            pltpu.VMEM((64, 128), F32), pltpu.VMEM((64, 128), I32), pltpu.VMEM((1, 16), F32),
            pltpu.VMEM((64, 4096), BF16), pltpu.VMEM((64, 4096), BF16), pltpu.VMEM((1024, 64), BF16),
            pltpu.VMEM((256, 4736), BF16), pltpu.SemaphoreType.DMA((15,)),
        ],
        far=range(8),
        far_out=True,
    )
    received = lax.all_to_all(send.reshape(16, 16, 4736), PLANE, split_axis=0, concat_axis=0, tiled=True)
    selector = call(selector_kernel, sds((576, 256), BF16), (messages,))
    wide, edges, beside = extended_grids(own, lo, hi)
    partial = call(
        combine_kernel, sds((64, 4480), F32), (selector, received.reshape(256, 4736), *edges)
    )
    parts = lax.all_to_all(
        partial.astype(jnp.float16).reshape(4, 16, 4480), "zlo", split_axis=0, concat_axis=0, tiled=True
    )
    terms = operator(wide, *beside)
    block, strip = sds((576, 128), F32), sds((432, 128), BF16)
    density, main, side, up, down = call(
        unpack_kernel,
        (sds((512, 128), F32), block, block, strip, strip),
        (jnp.sum(parts.astype(F32), axis=0), *beside),
        scratch=[pltpu.VMEM((512, 128), F32)],
    )
    lo, hi = exchange(up, down, LAYER)
    eight = pltpu.VMEM((8, 144, 256), F32)
    guess = call(
        sweep_kernel,
        sds((512, 128), F32),
        (main, side, lo, hi, wide, *terms),
        mib=40,
        scratch=[eight, eight, eight],
    )
    return guess.reshape(4, 128, 128), density.reshape(4, 128, 128)


def solution(mesh):
    fine = Mesh(mesh.devices.reshape(4, 4, 4, 4, 2), ("row", "zlo", "y", "zhi", "core"))
    grid = P(LAYER, "row", COL)
    slot = ("row", "zlo", "y", "zhi", "core")
    return jax.shard_map(
        shards,
        mesh=fine,
        in_specs=(
            grid,
            grid,
            grid,
            P(slot, None, None),
            P(slot, None, None),
            P(slot, None, None),
            P(slot, None),
            P(slot, None),
            P(slot, None),
            P(slot, None),
        ),
        out_specs=(grid, grid),
        check_vma=False,
    )
```

```python
import jax
import jax.numpy as jnp
from jax import lax
from jax.experimental import pallas as pl
from jax.experimental.pallas import tpu as pltpu
from jax.sharding import Mesh
from jax.sharding import PartitionSpec as P

eig_low = 0.1
eig_high = 2.0

LAYER = ("zhi", "core")
COL = ("zlo", "y")
CUBE = ("row", "zlo", "y")
PLANE = ("row", "y")

F32, BF16, I32 = jnp.float32, jnp.bfloat16, jnp.int32


def iota(shape, dim):
    return lax.broadcasted_iota(I32, shape, dim)


def as_column(row):
    n = row.shape[1]
    return jnp.sum(jnp.where(iota((n, n), 0) == iota((n, n), 1), row, 0), axis=1, keepdims=True)


def slot_rows(panel, place, holder, tier):
    layer = jnp.sum(jnp.where(iota((16, 64), 0) == holder, as_column(tier), 0), axis=0, keepdims=True)
    pos = layer * 4 + place
    ident = ((panel >> 2) & 3) * 16 + pos
    column = (panel >> 4) * 4 + (panel & 3)
    same = (as_column(column) == column) & (iota((64, 64), 0) < iota((64, 64), 1))
    rank = jnp.sum(same.astype(I32), axis=0, keepdims=True)
    return pos, ident, column * 16 + rank


def place_slots(panel, pos, dest, holder, placing, columns):
    x, y, rank = panel >> 4, panel & 3, dest & 15
    lower, right = (pos >> 1) & 1, pos & 1
    next_x = x + lower * 2 - 1
    next_y = (y + right * 2 + 3) & 3
    inside = (next_x >= 0) & (next_x <= 3)
    targets = (
        dest,
        jnp.where(inside, (next_x * 4 + y) * 16 + rank, -1),
        (x * 4 + next_y) * 16 + rank,
        jnp.where(inside, (next_x * 4 + next_y) * 16 + rank, -1),
    )
    for k, target in enumerate(targets):
        placing[pl.ds(k * 256, 256), :] = jnp.where(iota((256, 64), 0) == target, 1.0, 0.0).astype(BF16)
    lane = iota((64, 128), 1)
    columns[...] = jnp.where(
        lane == 0, as_column(panel), jnp.where(lane == 1, as_column(pos), as_column(holder))
    )


def message_kernel(temp, panel, place, holder, tier, out, placing, columns, temp_v, panel_v, place_v, holder_v, tier_v, sems):
    pairs = [(panel, panel_v), (place, place_v), (holder, holder_v), (tier, tier_v), (temp, temp_v)]
    copies = [pltpu.make_async_copy(a, b, sems.at[i]) for i, (a, b) in enumerate(pairs)]
    for copy in copies:
        copy.start()
    for copy in copies[:4]:
        copy.wait()
    panel_row, holder_row = panel_v[...], holder_v[...]
    pos, ident, dest = slot_rows(panel_row, place_v[...], holder_row, tier_v[...])
    place_slots(panel_row, pos, dest, holder_row, placing, columns)
    code = (dest * 64 + ident).astype(F32)
    copies[4].wait()
    sums = jnp.sum(temp_v[...].reshape(8, 64, 128), axis=1)
    lane = iota((8, 128), 1)
    first = jnp.sum(jnp.where(lane < 64, sums, 0.0), axis=1, keepdims=True)
    second = jnp.sum(jnp.where(lane < 64, 0.0, sums), axis=1, keepdims=True)
    at = iota((8, 128), 0) * 2
    means = jnp.where(lane == at, first, jnp.where(lane == at + 1, second, 0.0))
    means = jnp.sum(means, axis=0, keepdims=True) * (1.0 / 4096.0)
    row = jnp.where(iota((1, 128), 1) < 64, means, jnp.concatenate([code, code], axis=1))
    out[...] = jnp.broadcast_to(row, (64, 128))


def power_kernel(
    far_messages, far_columns, far_warming, far_toggling, far_baseline, far_placing, out,
    messages, columns, warming, toggling, baseline, placing, sent, sems,
):
    pairs = [
        (far_messages, messages),
        (far_columns, columns),
        (far_warming, warming),
        (far_toggling, toggling),
        (far_baseline, baseline),
        (far_placing, placing),
    ]
    loads = [pltpu.make_async_copy(a, b, sems.at[9 + i]) for i, (a, b) in enumerate(pairs)]
    for load in loads:
        load.start()
    loads[0].wait()
    loads[1].wait()
    tile, pos, holder = (columns[:, k : k + 1] for k in range(3))
    lower, right = (pos >> 1) & 1, pos & 1
    pick = jnp.where(iota((64, 64), 1) == tile, 1.0, 0.0)
    means = jnp.dot(pick, messages[...], precision=lax.Precision.HIGHEST, preferred_element_type=F32)
    lane = iota((64, 128), 1)
    slot_mean = jnp.sum(jnp.where(lane == pos, means, 0.0), axis=1, keepdims=True)
    member = iota((64, 16), 1) == holder
    total = jnp.sum(jnp.where(member, slot_mean, 0.0), axis=0, keepdims=True)
    count = jnp.sum(jnp.where(member, 1.0, 0.0), axis=0, keepdims=True)
    loads[2].wait()
    leak = jnp.exp(warming[...] * (total / count))
    factor = jnp.sum(jnp.where(member, leak, 0.0), axis=1, keepdims=True)

    def place(kind, values):
        at = placing[kind * 256 : (kind + 1) * 256, :]
        return jnp.dot(at, values.astype(BF16), preferred_element_type=F32).astype(BF16)

    copies = []

    def send(start, width):
        at = pl.ds(start, width)
        copy = pltpu.make_async_copy(sent.at[:, at], out.at[:, at], sems.at[len(copies)])
        copy.start()
        copies.append(copy)

    for load in loads[3:]:
        load.wait()
    edge = ((lane & 63) >> 1) == right * 31
    sides = jnp.zeros((64, 128), F32)
    width = 512
    for k in range(8):
        at = pl.ds(k * width, width)
        power = (toggling[:, at].astype(F32) + factor * baseline[:, at].astype(F32)).astype(BF16)
        sent[:, at] = place(0, power)
        send(k * width, width)
        power = power.astype(F32)
        for t in range(4):
            piece = power[:, t * 128 : (t + 1) * 128]
            shift = 2 * (4 * k + t)
            kept = jnp.where(edge, piece, 0.0)
            sides = sides + (pltpu.roll(kept, shift, 1) if shift else kept)
            if k == 0 and t == 0:
                top = piece
    rows = jnp.where(lower == 0, top, piece)
    sides = jnp.where(right == 0, sides, pltpu.roll(sides, 66, 1))
    corner = jnp.sum(jnp.where(lane == lower * 64 + right * 63, rows, 0.0), axis=1, keepdims=True)
    quarter = (1 - lower) * 2 + 1 - right
    both = jnp.concatenate([jnp.where(lower == 1, rows, 0.0), jnp.where(lower == 0, rows, 0.0)], axis=1)
    sent[:, 4096:4352] = place(1, both)
    both = jnp.concatenate([jnp.where(right == 1, sides, 0.0), jnp.where(right == 0, sides, 0.0)], axis=1)
    sent[:, 4352:4608] = place(2, both)
    sent[:, 4608:4736] = place(3, jnp.where(lane == quarter, corner, 0.0))
    send(4096, 640)
    for copy in copies:
        copy.wait()


def selector_kernel(messages, _last, _first, out):
    x, y = lax.axis_index("row"), lax.axis_index("y")
    plane = lax.axis_index("zlo")
    code = jnp.concatenate([messages[pl.ds(r * 16 + plane * 4, 4), :] for r in range(4)], axis=0)
    code = jnp.where(iota((16, 128), 1) < 64, -1.0, code).astype(I32)
    dest, ident = code >> 6, code & 63
    lane = iota((16, 256), 1)

    def idents(dx, dy):
        base = ((x + dx) * 4 + ((y + dy + 4) & 3)) * 16
        ids = jnp.zeros((16, 256), I32)
        for r in range(16):
            hit = jnp.sum(jnp.where(dest == base + r, ident + 1, 0), axis=1, keepdims=True)
            ids = jnp.where((lane & 15) == r, hit, ids)
        ids = jnp.sum(jnp.where((lane >> 4) == iota((16, 256), 0), ids, 0), axis=0, keepdims=True) - 1
        turn = jnp.where(y == 0, 1, 0) if dy < 0 else jnp.where(y == 3, -1, 0) if dy > 0 else 0
        return ids, (ids >> 4) + turn, (ids >> 2) & 3, (ids >> 1) & 1, ids & 1

    def put(k, ids, target):
        out[pl.ds(k * 64, 64), :] = jnp.where(
            (iota((64, 256), 0) == target) & (ids >= 0), 1.0, 0.0
        ).astype(BF16)

    ids, *_ = idents(0, 0)
    put(0, ids, ids)
    for k, dx in enumerate((-1, 1)):
        ids, z, layer, _, pc = idents(dx, 0)
        put(1 + k, ids, z * 16 + k * 8 + layer * 2 + pc)
    for k, dy in enumerate((-1, 1)):
        ids, z, layer, pr, _ = idents(0, dy)
        put(3 + k, ids, z * 16 + k * 8 + layer * 2 + pr)
    for k in range(4):
        ids, z, layer, _, _ = idents((k >> 1) * 2 - 1, (k & 1) * 2 - 1)
        put(5 + k, ids, z * 16 + layer)


def combine_kernel(selector, received, out):
    def add(k, start, width):
        return jnp.dot(
            selector[k * 64 : (k + 1) * 64, :],
            received[:, start : start + width],
            preferred_element_type=F32,
        )

    for k in range(8):
        out[:, k * 512 : (k + 1) * 512] = add(0, k * 512, 512)
    out[:, 4096:4224] = add(1, 4096, 128) + add(2, 4224, 128)
    out[:, 4224:4352] = add(3, 4352, 128) + add(4, 4480, 128)
    lane = iota((64, 128), 1)
    corners = jnp.zeros((64, 128), F32)
    for k in range(4):
        corners = jnp.where(lane == k, add(5 + k, 4608, 128), corners)
    out[:, 4352:4480] = corners


def unpack_kernel(whole, _to_left, _to_right, density, main, side, up, down, turned):
    for k in range(32):
        turned[k * 16 : (k + 1) * 16, :] = whole[:, k * 128 : (k + 1) * 128]
    low = iota((32, 128), 1) < 64
    lane = iota((64, 128), 1)
    low_row = iota((1, 128), 1) < 64
    lane16, row16 = iota((16, 128), 1), iota((16, 128), 0)
    rows, columns, corners = whole[:, 4096:4224], whole[:, 4224:4352], whole[:, 4352:4480]
    cell = iota((64, 128), 0)
    turn = []
    for c in range(2):
        pick = jnp.where(lane == (cell & 1) * 64 + (cell - (cell & 1)) + c, 1.0, 0.0)
        turn.append(
            lax.dot_general(
                pick, columns, (((1,), (1,)), ((), ())),
                precision=lax.Precision.HIGHEST, preferred_element_type=F32,
            )
        )
    for layer in range(4):
        base = layer * 144
        for r in range(2):
            left = turned[pl.ds(layer * 4 + r * 2, 32, stride=16), :]
            right = turned[pl.ds(layer * 4 + r * 2 + 1, 32, stride=16), :]
            at = base + r * 64
            main[pl.ds(at, 32, stride=2), :] = jnp.where(low, left, pltpu.roll(right, 64, 1))
            main[pl.ds(at + 1, 32, stride=2), :] = jnp.where(low, pltpu.roll(left, 64, 1), right)
            k = layer * 2 + r
            strip = jnp.where(lane == 0, turn[0][:, 8 + k : 9 + k], 0.0)
            strip = jnp.where(lane == 1, turn[1][:, 8 + k : 9 + k], strip)
            strip = jnp.where(lane == 126, turn[0][:, k : k + 1], strip)
            side[at : at + 64, :] = jnp.where(lane == 127, turn[1][:, k : k + 1], strip)
        block = jnp.zeros((16, 128), F32)
        for kind, first_row in ((0, 14), (1, 0)):
            k = kind * 8 + layer * 2
            a, b = rows[k : k + 1, :], rows[k + 1 : k + 2, :]
            first = jnp.where(low_row, a, pltpu.roll(b, 64, 1))
            second = jnp.where(low_row, pltpu.roll(a, 64, 1), b)
            block = jnp.where(row16 == first_row, first, block)
            block = jnp.where(row16 == first_row + 1, second, block)
        main[base + 128 : base + 144, :] = block
        block = jnp.zeros((16, 128), F32)
        for k, (r, at_lane) in enumerate(((15, 127), (15, 0), (0, 127), (0, 0))):
            value = corners[layer : layer + 1, k : k + 1]
            block = jnp.where((row16 == r) & (lane16 == at_lane), value, block)
        side[base + 128 : base + 144, :] = block
        density[layer * 128 : (layer + 1) * 128, :] = main[base : base + 128, :]
    for out, first in ((up, 288), (down, 0)):
        out[0:288, :] = main[first : first + 288, :].astype(BF16)
        second = side[first + 144 : first + 288, :]
        out[288:432, :] = (side[first : first + 144, :] + pltpu.roll(second, 4, 1)).astype(BF16)


def depth(a):
    return 3 if a < 2 else 2


def beyond(lo, hi, a, layer):
    if layer < 3:
        k = layer - 3 + depth(a)
        return (lo, 3 * a + k) if k >= 0 else None
    k = layer - 7
    return (hi, 3 * a + k) if k < depth(a) else None


def layers_kernel(temp, cond, mass, own, up, down, sems):
    copies = [pltpu.make_async_copy(a, own.at[i], sems.at[i]) for i, a in enumerate((temp, cond, mass))]
    for copy in copies:
        copy.start()
    for a, copy in enumerate(copies):
        copy.wait()
        for k in range(depth(a)):
            up[3 * a + k] = own[a, 4 - depth(a) + k].astype(BF16)
            down[3 * a + k] = own[a, k].astype(BF16)


def rows_kernel(own, lo, hi, last, first):
    lasts, firsts = [], []
    for a in range(3):
        for layer in range(10):
            if 3 <= layer < 7:
                lasts.append(own[a, layer - 3, 120:128, :])
                firsts.append(own[a, layer - 3, 0:8, :])
            elif found := beyond(lo, hi, a, layer):
                source, k = found
                lasts.append(source[k, 112:128, :].astype(F32)[8:16])
                firsts.append(source[k, 0:16, :].astype(F32)[0:8])
            else:
                lasts.append(jnp.zeros((8, 128), F32))
                firsts.append(jnp.zeros((8, 128), F32))
    last[...] = jnp.concatenate(lasts, axis=0).astype(BF16)
    first[...] = jnp.concatenate(firsts, axis=0).astype(BF16)


def gather_kernel(own, lo, hi, above, below, out, to_left, to_right):
    over, under = above[...].astype(F32), below[...].astype(F32)
    lane = iota((144, 128), 1)
    left, right = jnp.zeros((144, 128), F32), jnp.zeros((144, 128), F32)
    for a in range(3):
        for layer in range(10):
            i = a * 10 + layer
            if 3 <= layer < 7:
                source = own[a, layer - 3]
            elif found := beyond(lo, hi, a, layer):
                source = found[0][found[1]].astype(F32)
            else:
                source = jnp.zeros((128, 128), F32)
            piece = jnp.concatenate([source, under[8 * i : 8 * i + 8], over[8 * i : 8 * i + 8]], axis=0)
            out[i] = piece
            base = a * 40 + layer * 4
            here = (lane >= base) & (lane < base + 3)
            left = jnp.where(here, pltpu.roll(piece, base, 1) if base else piece, left)
            right = jnp.where(here, pltpu.roll(piece, base + 3, 1), right)
    to_left[...] = left.astype(BF16)
    to_right[...] = right.astype(BF16)


def turned_by(x, shift, axis):
    return pltpu.roll(x, shift % x.shape[axis], axis)


def around(face_row, face_col, v):
    return (
        face_row * turned_by(v, -1, 0)
        + turned_by(face_row * v, 1, 0)
        + face_col * turned_by(v, -1, 1)
        + turned_by(face_col * v, 1, 1)
    )


def operator_kernel(grids, from_left, from_right, face_layer, face_row, face_col, inverse, residual, wide):
    left, right = from_left[...].astype(F32), from_right[...].astype(F32)
    lane = iota((144, 128), 1)
    for a in range(3):
        for layer in range(10):
            i, base = a * 10 + layer, a * 40 + layer * 4
            high = turned_by(right, -base, 1) if base else right
            side = jnp.where(lane < 3, high, jnp.where(lane >= 125, turned_by(left, 125 - base, 1), 0.0))
            wide[i, :, 0:128] = grids[i]
            wide[i, :, 128:256] = side
    for layer in range(9):
        face_layer[layer] = 0.5 * (wide[10 + layer] + wide[11 + layer])
    for layer in range(1, 9):
        temp, cond, mass = (wide[a * 10 + layer] for a in range(3))
        rows = 0.5 * (cond + turned_by(cond, -1, 0))
        cols = 0.5 * (cond + turned_by(cond, -1, 1))
        face_row[layer - 1] = rows
        face_col[layer - 1] = cols
        after, before = face_layer[layer], face_layer[layer - 1]
        diagonal = mass + after + before + rows + turned_by(rows, 1, 0) + cols + turned_by(cols, 1, 1)
        share = after * wide[layer + 1] + before * wide[layer - 1] + around(rows, cols, temp)
        residual[layer - 1] = mass * temp + (share - diagonal * temp)
        inverse[layer - 1] = jnp.where(mass > 0.0, 1.0 / diagonal, 0.0)


MIDDLE = (eig_low + eig_high) / 2.0
SPREAD = (eig_high - eig_low) / 2.0
W0 = SPREAD / MIDDLE
W1 = 1.0 / (2.0 * MIDDLE / SPREAD - W0)
W2 = 1.0 / (2.0 * MIDDLE / SPREAD - W1)


def sweep_kernel(main, side, lo, hi, grids, face_layer, face_row, face_col, inverse, residual, out, d0, d1, rest):
    lane = iota((144, 128), 1)
    kept = (lane < 2) | (lane >= 126)

    def supplied(i):
        if 3 <= i <= 6:
            at = (i - 3) * 144
            return main[at : at + 144, :], side[at : at + 144, :]
        source, second = (lo, i == 2) if i < 3 else (hi, i == 8)
        at = 144 if second else 0
        beside = source[288:432, :].astype(F32)
        if second:
            beside = turned_by(beside, -4, 1)
        return source[at : at + 144, :].astype(F32), jnp.where(kept, beside, 0.0)

    for i in range(1, 9):
        start = residual[i - 1] + jnp.concatenate(supplied(i), axis=1)
        rest[i - 1] = start
        d0[i - 1] = start * inverse[i - 1] * (1.0 / MIDDLE)

    def share(i, d):
        return (
            face_layer[i] * d[i]
            + face_layer[i - 1] * d[i - 2]
            + around(face_row[i - 1], face_col[i - 1], d[i - 1])
        )

    for i in range(2, 8):
        start = rest[i - 1]
        later = start * (1.0 - 1.0 / MIDDLE) + share(i, d0)
        d1[i - 1] = W1 * W0 * d0[i - 1] + (2.0 * W1 / SPREAD) * (later * inverse[i - 1])
        rest[i - 1] = later - (W1 * W0 / MIDDLE) * start - (2.0 * W1 / SPREAD) * later
    for i in range(3, 7):
        last = rest[i - 1] + share(i, d1)
        step = d0[i - 1] + d1[i - 1] * (1.0 + W2 * W1) + (2.0 * W2 / SPREAD) * (last * inverse[i - 1])
        at = (i - 3) * 128
        out[at : at + 128, :] = grids[i, 0:128, :] + step[0:128, 0:128]


def sds(shape, dtype):
    return jax.ShapeDtypeStruct(shape, dtype)


def call(kernel, shape, args, mib=16, scratch=(), far=(), far_out=False):
    vmem, anywhere = pl.BlockSpec(memory_space=pltpu.VMEM), pl.BlockSpec(memory_space=pltpu.HBM)
    return pl.pallas_call(
        kernel,
        out_shape=shape,
        in_specs=[anywhere if i in far else vmem for i in range(len(args))],
        out_specs=jax.tree.map(lambda _: anywhere if far_out else vmem, shape),
        scratch_shapes=list(scratch),
        compiler_params=pltpu.CompilerParams(vmem_limit_bytes=mib * 2**20),
    )(*args)


def pairs(axis):
    up = [(i, i + 1) for i in range(lax.axis_size(axis) - 1)]
    return up, [(b, a) for a, b in up]


def exchange(to_next, to_last, axis):
    up, down = pairs(axis)
    return lax.ppermute(to_next, axis, up), lax.ppermute(to_last, axis, down)


def extended_grids(temp, cond, mass):
    eight, rows, edge = sds((8, 128, 128), BF16), sds((240, 128), BF16), sds((144, 128), BF16)
    own, up, down = call(
        layers_kernel,
        (sds((3, 4, 128, 128), F32), eight, eight),
        (temp, cond, mass),
        scratch=[pltpu.SemaphoreType.DMA((3,))],
        far=range(3),
    )
    lo, hi = exchange(up, down, LAYER)
    ends = call(rows_kernel, (rows, rows), (own, lo, hi))
    above, below = exchange(*ends, "row")
    wide, to_left, to_right = call(
        gather_kernel, (sds((30, 144, 128), F32), edge, edge), (own, lo, hi, above, below), mib=24
    )
    return wide, ends, (to_left, to_right), exchange(to_right, to_left, COL)


def operator(wide, from_left, from_right):
    eight = sds((8, 144, 256), F32)
    return call(
        operator_kernel,
        (sds((9, 144, 256), F32), eight, eight, eight, eight),
        (wide, from_left, from_right),
        mib=32,
        scratch=[pltpu.VMEM((30, 144, 256), F32)],
    )


def shards(temp, cond, mass, toggling, baseline, panel, place, holder, tier, warming):
    row64 = pltpu.VMEM((1, 64), I32)
    message, placing, columns = call(
        message_kernel,
        (sds((64, 128), F32), sds((1024, 64), BF16), sds((64, 128), I32)),
        (temp, panel.reshape(1, 64), place, holder, tier),
        mib=60,
        scratch=[
            pltpu.VMEM((4, 128, 128), F32), row64, row64, row64,
            pltpu.VMEM((1, 16), I32), pltpu.SemaphoreType.DMA((5,)),
        ],
        far=range(5),
    )
    messages = lax.all_to_all(message.reshape(64, 1, 128), CUBE, split_axis=0, concat_axis=0, tiled=True)
    messages = messages.reshape(64, 128)
    send = call(
        power_kernel,
        sds((256, 4736), BF16),
        (messages, columns, warming, toggling[0], baseline[0], placing),
        mib=60,
        scratch=[
            pltpu.VMEM((64, 128), F32), pltpu.VMEM((64, 128), I32), pltpu.VMEM((1, 16), F32),
            pltpu.VMEM((64, 4096), BF16), pltpu.VMEM((64, 4096), BF16), pltpu.VMEM((1024, 64), BF16),
            pltpu.VMEM((256, 4736), BF16), pltpu.SemaphoreType.DMA((15,)),
        ],
        far=range(6),
        far_out=True,
    )
    received = lax.all_to_all(send.reshape(16, 16, 4736), PLANE, split_axis=0, concat_axis=0, tiled=True)
    wide, ends, edges, beside = extended_grids(temp, cond, mass)
    selector = call(selector_kernel, sds((576, 256), BF16), (messages, *ends))
    partial = call(
        combine_kernel, sds((64, 4480), F32), (selector, received.reshape(256, 4736))
    )
    parts = lax.all_to_all(
        partial.astype(jnp.float16).reshape(4, 16, 4480), "zlo", split_axis=0, concat_axis=0, tiled=True
    )
    terms = operator(wide, *beside)
    block, strip = sds((576, 128), F32), sds((432, 128), BF16)
    density, main, side, up, down = call(
        unpack_kernel,
        (sds((512, 128), F32), block, block, strip, strip),
        (jnp.sum(parts.astype(F32), axis=0), *edges),
        scratch=[pltpu.VMEM((512, 128), F32)],
    )
    lo, hi = exchange(up, down, LAYER)
    eight = pltpu.VMEM((8, 144, 256), F32)
    guess = call(
        sweep_kernel,
        sds((512, 128), F32),
        (main, side, lo, hi, wide, *terms),
        mib=40,
        scratch=[eight, eight, eight],
    )
    return guess.reshape(4, 128, 128), density.reshape(4, 128, 128)


def solution(mesh):
    fine = Mesh(mesh.devices.reshape(4, 4, 4, 4, 2), ("row", "zlo", "y", "zhi", "core"))
    grid = P(LAYER, "row", COL)
    slot = ("row", "zlo", "y", "zhi", "core")
    return jax.shard_map(
        shards,
        mesh=fine,
        in_specs=(
            grid,
            grid,
            grid,
            P(slot, None, None),
            P(slot, None, None),
            P(slot, None, None),
            P(slot, None),
            P(slot, None),
            P(slot, None),
            P(slot, None),
        ),
        out_specs=(grid, grid),
        check_vma=False,
    )
```

```python
import jax
import jax.numpy as jnp
from jax import lax
from jax.experimental import pallas as pl
from jax.experimental.pallas import tpu as pltpu
from jax.sharding import Mesh
from jax.sharding import PartitionSpec as P

eig_low = 0.1
eig_high = 2.0

LAYER = ("zhi", "core")
COL = ("zlo", "y")
CUBE = ("row", "zlo", "y")
PLANE = ("row", "y")

F32, BF16, I32 = jnp.float32, jnp.bfloat16, jnp.int32


def iota(shape, dim):
    return lax.broadcasted_iota(I32, shape, dim)


def as_column(row):
    n = row.shape[1]
    return jnp.sum(jnp.where(iota((n, n), 0) == iota((n, n), 1), row, 0), axis=1, keepdims=True)


def slot_rows(panel, place, holder, tier):
    layer = jnp.sum(jnp.where(iota((16, 64), 0) == holder, as_column(tier), 0), axis=0, keepdims=True)
    pos = layer * 4 + place
    ident = ((panel >> 2) & 3) * 16 + pos
    column = (panel >> 4) * 4 + (panel & 3)
    same = (as_column(column) == column) & (iota((64, 64), 0) < iota((64, 64), 1))
    rank = jnp.sum(same.astype(I32), axis=0, keepdims=True)
    return pos, ident, column * 16 + rank


def place_slots(panel, pos, dest, holder, placing, columns):
    x, y, rank = panel >> 4, panel & 3, dest & 15
    lower, right = (pos >> 1) & 1, pos & 1
    next_x = x + lower * 2 - 1
    next_y = (y + right * 2 + 3) & 3
    inside = (next_x >= 0) & (next_x <= 3)
    targets = (
        dest,
        jnp.where(inside, (next_x * 4 + y) * 16 + rank, -1),
        (x * 4 + next_y) * 16 + rank,
        jnp.where(inside, (next_x * 4 + next_y) * 16 + rank, -1),
    )
    for k, target in enumerate(targets):
        placing[pl.ds(k * 256, 256), :] = jnp.where(iota((256, 64), 0) == target, 1.0, 0.0).astype(BF16)
    lane = iota((64, 128), 1)
    columns[...] = jnp.where(
        lane == 0, as_column(panel), jnp.where(lane == 1, as_column(pos), as_column(holder))
    )


def message_kernel(temp, panel, place, holder, tier, out, placing, columns, temp_v, panel_v, place_v, holder_v, tier_v, sems):
    pairs = [(panel, panel_v), (place, place_v), (holder, holder_v), (tier, tier_v), (temp, temp_v)]
    copies = [pltpu.make_async_copy(a, b, sems.at[i]) for i, (a, b) in enumerate(pairs)]
    for copy in copies:
        copy.start()
    for copy in copies[:4]:
        copy.wait()
    panel_row, holder_row = panel_v[...], holder_v[...]
    pos, ident, dest = slot_rows(panel_row, place_v[...], holder_row, tier_v[...])
    place_slots(panel_row, pos, dest, holder_row, placing, columns)
    code = (dest * 64 + ident).astype(F32)
    copies[4].wait()
    sums = jnp.sum(temp_v[...].reshape(8, 64, 128), axis=1)
    lane = iota((8, 128), 1)
    first = jnp.sum(jnp.where(lane < 64, sums, 0.0), axis=1, keepdims=True)
    second = jnp.sum(jnp.where(lane < 64, 0.0, sums), axis=1, keepdims=True)
    at = iota((8, 128), 0) * 2
    means = jnp.where(lane == at, first, jnp.where(lane == at + 1, second, 0.0))
    means = jnp.sum(means, axis=0, keepdims=True) * (1.0 / 4096.0)
    row = jnp.where(iota((1, 128), 1) < 64, means, jnp.concatenate([code, code], axis=1))
    out[...] = jnp.broadcast_to(row, (64, 128))


def power_kernel(
    far_messages, far_columns, far_warming, far_toggling, far_baseline, far_placing, out,
    messages, columns, warming, toggling, baseline, placing, sent, sems,
):
    pairs = [
        (far_messages, messages),
        (far_columns, columns),
        (far_warming, warming),
        (far_toggling, toggling),
        (far_baseline, baseline),
        (far_placing, placing),
    ]
    loads = [pltpu.make_async_copy(a, b, sems.at[9 + i]) for i, (a, b) in enumerate(pairs)]
    for load in loads:
        load.start()
    loads[0].wait()
    loads[1].wait()
    tile, pos, holder = (columns[:, k : k + 1] for k in range(3))
    lower, right = (pos >> 1) & 1, pos & 1
    pick = jnp.where(iota((64, 64), 1) == tile, 1.0, 0.0)
    means = jnp.dot(pick, messages[...], precision=lax.Precision.HIGHEST, preferred_element_type=F32)
    lane = iota((64, 128), 1)
    slot_mean = jnp.sum(jnp.where(lane == pos, means, 0.0), axis=1, keepdims=True)
    member = iota((64, 16), 1) == holder
    total = jnp.sum(jnp.where(member, slot_mean, 0.0), axis=0, keepdims=True)
    count = jnp.sum(jnp.where(member, 1.0, 0.0), axis=0, keepdims=True)
    loads[2].wait()
    leak = jnp.exp(warming[...] * (total / count))
    factor = jnp.sum(jnp.where(member, leak, 0.0), axis=1, keepdims=True)

    def place(kind, values):
        at = placing[kind * 256 : (kind + 1) * 256, :]
        return jnp.dot(at, values.astype(BF16), preferred_element_type=F32).astype(BF16)

    copies = []

    def send(start, width):
        at = pl.ds(start, width)
        copy = pltpu.make_async_copy(sent.at[:, at], out.at[:, at], sems.at[len(copies)])
        copy.start()
        copies.append(copy)

    for load in loads[3:]:
        load.wait()
    edge = ((lane & 63) >> 1) == right * 31
    sides = jnp.zeros((64, 128), F32)
    width = 512
    for k in range(8):
        at = pl.ds(k * width, width)
        power = (toggling[:, at].astype(F32) + factor * baseline[:, at].astype(F32)).astype(BF16)
        sent[:, at] = place(0, power)
        send(k * width, width)
        power = power.astype(F32)
        for t in range(4):
            piece = power[:, t * 128 : (t + 1) * 128]
            shift = 2 * (4 * k + t)
            kept = jnp.where(edge, piece, 0.0)
            sides = sides + (pltpu.roll(kept, shift, 1) if shift else kept)
            if k == 0 and t == 0:
                top = piece
    rows = jnp.where(lower == 0, top, piece)
    sides = jnp.where(right == 0, sides, pltpu.roll(sides, 66, 1))
    corner = jnp.sum(jnp.where(lane == lower * 64 + right * 63, rows, 0.0), axis=1, keepdims=True)
    quarter = (1 - lower) * 2 + 1 - right
    both = jnp.concatenate([jnp.where(lower == 1, rows, 0.0), jnp.where(lower == 0, rows, 0.0)], axis=1)
    sent[:, 4096:4352] = place(1, both)
    both = jnp.concatenate([jnp.where(right == 1, sides, 0.0), jnp.where(right == 0, sides, 0.0)], axis=1)
    sent[:, 4352:4608] = place(2, both)
    sent[:, 4608:4736] = place(3, jnp.where(lane == quarter, corner, 0.0))
    send(4096, 640)
    for copy in copies:
        copy.wait()


def selector_kernel(messages, _last, _first, out):
    x, y = lax.axis_index("row"), lax.axis_index("y")
    plane = lax.axis_index("zlo")
    code = jnp.concatenate([messages[pl.ds(r * 16 + plane * 4, 4), :] for r in range(4)], axis=0)
    code = jnp.where(iota((16, 128), 1) < 64, -1.0, code).astype(I32)
    dest, ident = code >> 6, code & 63
    lane = iota((16, 256), 1)

    def idents(dx, dy):
        base = ((x + dx) * 4 + ((y + dy + 4) & 3)) * 16
        ids = jnp.zeros((16, 256), I32)
        for r in range(16):
            hit = jnp.sum(jnp.where(dest == base + r, ident + 1, 0), axis=1, keepdims=True)
            ids = jnp.where((lane & 15) == r, hit, ids)
        ids = jnp.sum(jnp.where((lane >> 4) == iota((16, 256), 0), ids, 0), axis=0, keepdims=True) - 1
        turn = jnp.where(y == 0, 1, 0) if dy < 0 else jnp.where(y == 3, -1, 0) if dy > 0 else 0
        return ids, (ids >> 4) + turn, (ids >> 2) & 3, (ids >> 1) & 1, ids & 1

    def put(k, ids, target):
        out[pl.ds(k * 64, 64), :] = jnp.where(
            (iota((64, 256), 0) == target) & (ids >= 0), 1.0, 0.0
        ).astype(BF16)

    ids, *_ = idents(0, 0)
    put(0, ids, ids)
    for k, dx in enumerate((-1, 1)):
        ids, z, layer, _, pc = idents(dx, 0)
        put(1 + k, ids, z * 16 + k * 8 + layer * 2 + pc)
    for k, dy in enumerate((-1, 1)):
        ids, z, layer, pr, _ = idents(0, dy)
        put(3 + k, ids, z * 16 + k * 8 + layer * 2 + pr)
    for k in range(4):
        ids, z, layer, _, _ = idents((k >> 1) * 2 - 1, (k & 1) * 2 - 1)
        put(5 + k, ids, z * 16 + layer)


def combine_kernel(selector, received, out):
    def add(k, start, width):
        return jnp.dot(
            selector[k * 64 : (k + 1) * 64, :],
            received[:, start : start + width],
            preferred_element_type=F32,
        )

    for k in range(8):
        out[:, k * 512 : (k + 1) * 512] = add(0, k * 512, 512)
    out[:, 4096:4224] = add(1, 4096, 128) + add(2, 4224, 128)
    out[:, 4224:4352] = add(3, 4352, 128) + add(4, 4480, 128)
    lane = iota((64, 128), 1)
    corners = jnp.zeros((64, 128), F32)
    for k in range(4):
        corners = jnp.where(lane == k, add(5 + k, 4608, 128), corners)
    out[:, 4352:4480] = corners


def unpack_kernel(whole, _left, _right, density, main, side, up, down, turned):
    for k in range(32):
        turned[k * 16 : (k + 1) * 16, :] = whole[:, k * 128 : (k + 1) * 128]
    low = iota((32, 128), 1) < 64
    lane = iota((64, 128), 1)
    low_row = iota((1, 128), 1) < 64
    lane16, row16 = iota((16, 128), 1), iota((16, 128), 0)
    rows, columns, corners = whole[:, 4096:4224], whole[:, 4224:4352], whole[:, 4352:4480]
    cell = iota((64, 128), 0)
    turn = []
    for c in range(2):
        pick = jnp.where(lane == (cell & 1) * 64 + (cell - (cell & 1)) + c, 1.0, 0.0)
        turn.append(
            lax.dot_general(
                pick, columns, (((1,), (1,)), ((), ())),
                precision=lax.Precision.HIGHEST, preferred_element_type=F32,
            )
        )
    for layer in range(4):
        base = layer * 144
        for r in range(2):
            left = turned[pl.ds(layer * 4 + r * 2, 32, stride=16), :]
            right = turned[pl.ds(layer * 4 + r * 2 + 1, 32, stride=16), :]
            at = base + r * 64
            main[pl.ds(at, 32, stride=2), :] = jnp.where(low, left, pltpu.roll(right, 64, 1))
            main[pl.ds(at + 1, 32, stride=2), :] = jnp.where(low, pltpu.roll(left, 64, 1), right)
            k = layer * 2 + r
            strip = jnp.where(lane == 0, turn[0][:, 8 + k : 9 + k], 0.0)
            strip = jnp.where(lane == 1, turn[1][:, 8 + k : 9 + k], strip)
            strip = jnp.where(lane == 126, turn[0][:, k : k + 1], strip)
            side[at : at + 64, :] = jnp.where(lane == 127, turn[1][:, k : k + 1], strip)
        block = jnp.zeros((16, 128), F32)
        for kind, first_row in ((0, 14), (1, 0)):
            k = kind * 8 + layer * 2
            a, b = rows[k : k + 1, :], rows[k + 1 : k + 2, :]
            first = jnp.where(low_row, a, pltpu.roll(b, 64, 1))
            second = jnp.where(low_row, pltpu.roll(a, 64, 1), b)
            block = jnp.where(row16 == first_row, first, block)
            block = jnp.where(row16 == first_row + 1, second, block)
        main[base + 128 : base + 144, :] = block
        block = jnp.zeros((16, 128), F32)
        for k, (r, at_lane) in enumerate(((15, 127), (15, 0), (0, 127), (0, 0))):
            value = corners[layer : layer + 1, k : k + 1]
            block = jnp.where((row16 == r) & (lane16 == at_lane), value, block)
        side[base + 128 : base + 144, :] = block
        density[layer * 128 : (layer + 1) * 128, :] = main[base : base + 128, :]
    for out, first in ((up, 288), (down, 0)):
        out[0:288, :] = main[first : first + 288, :].astype(BF16)
        second = side[first + 144 : first + 288, :]
        out[288:432, :] = (side[first : first + 144, :] + pltpu.roll(second, 4, 1)).astype(BF16)


def depth(a):
    return 3 if a < 2 else 2


def beyond(lo, hi, a, layer):
    if layer < 3:
        k = layer - 3 + depth(a)
        return (lo, 3 * a + k) if k >= 0 else None
    k = layer - 7
    return (hi, 3 * a + k) if k < depth(a) else None


def layers_kernel(temp, cond, mass, own, up, down, sems):
    copies = [pltpu.make_async_copy(a, own.at[i], sems.at[i]) for i, a in enumerate((temp, cond, mass))]
    for copy in copies:
        copy.start()
    for a, copy in enumerate(copies):
        copy.wait()
        for k in range(depth(a)):
            up[3 * a + k] = own[a, 4 - depth(a) + k].astype(BF16)
            down[3 * a + k] = own[a, k].astype(BF16)


def rows_kernel(own, lo, hi, last, first):
    lasts, firsts = [], []
    for a in range(3):
        for layer in range(10):
            if 3 <= layer < 7:
                lasts.append(own[a, layer - 3, 120:128, :])
                firsts.append(own[a, layer - 3, 0:8, :])
            elif found := beyond(lo, hi, a, layer):
                source, k = found
                lasts.append(source[k, 112:128, :].astype(F32)[8:16])
                firsts.append(source[k, 0:16, :].astype(F32)[0:8])
            else:
                lasts.append(jnp.zeros((8, 128), F32))
                firsts.append(jnp.zeros((8, 128), F32))
    last[...] = jnp.concatenate(lasts, axis=0).astype(BF16)
    first[...] = jnp.concatenate(firsts, axis=0).astype(BF16)


def gather_kernel(own, lo, hi, above, below, out, to_left, to_right):
    over, under = above[...].astype(F32), below[...].astype(F32)
    lane = iota((144, 128), 1)
    left, right = jnp.zeros((144, 128), F32), jnp.zeros((144, 128), F32)
    for a in range(3):
        for layer in range(10):
            i = a * 10 + layer
            if 3 <= layer < 7:
                source = own[a, layer - 3]
            elif found := beyond(lo, hi, a, layer):
                source = found[0][found[1]].astype(F32)
            else:
                source = jnp.zeros((128, 128), F32)
            piece = jnp.concatenate([source, under[8 * i : 8 * i + 8], over[8 * i : 8 * i + 8]], axis=0)
            out[i] = piece
            base = a * 40 + layer * 4
            here = (lane >= base) & (lane < base + 3)
            left = jnp.where(here, pltpu.roll(piece, base, 1) if base else piece, left)
            right = jnp.where(here, pltpu.roll(piece, base + 3, 1), right)
    to_left[...] = left.astype(BF16)
    to_right[...] = right.astype(BF16)


def turned_by(x, shift, axis):
    return pltpu.roll(x, shift % x.shape[axis], axis)


def around(face_row, face_col, v):
    return (
        face_row * turned_by(v, -1, 0)
        + turned_by(face_row * v, 1, 0)
        + face_col * turned_by(v, -1, 1)
        + turned_by(face_col * v, 1, 1)
    )


def operator_kernel(grids, from_left, from_right, face_layer, face_row, face_col, inverse, residual, wide):
    left, right = from_left[...].astype(F32), from_right[...].astype(F32)
    lane = iota((144, 128), 1)
    for a in range(3):
        for layer in range(10):
            i, base = a * 10 + layer, a * 40 + layer * 4
            high = turned_by(right, -base, 1) if base else right
            side = jnp.where(lane < 3, high, jnp.where(lane >= 125, turned_by(left, 125 - base, 1), 0.0))
            wide[i, :, 0:128] = grids[i]
            wide[i, :, 128:256] = side
    for layer in range(9):
        face_layer[layer] = 0.5 * (wide[10 + layer] + wide[11 + layer])
    for layer in range(1, 9):
        temp, cond, mass = (wide[a * 10 + layer] for a in range(3))
        rows = 0.5 * (cond + turned_by(cond, -1, 0))
        cols = 0.5 * (cond + turned_by(cond, -1, 1))
        face_row[layer - 1] = rows
        face_col[layer - 1] = cols
        after, before = face_layer[layer], face_layer[layer - 1]
        diagonal = mass + after + before + rows + turned_by(rows, 1, 0) + cols + turned_by(cols, 1, 1)
        share = after * wide[layer + 1] + before * wide[layer - 1] + around(rows, cols, temp)
        residual[layer - 1] = mass * temp + (share - diagonal * temp)
        inverse[layer - 1] = jnp.where(mass > 0.0, 1.0 / diagonal, 0.0)


MIDDLE = (eig_low + eig_high) / 2.0
SPREAD = (eig_high - eig_low) / 2.0
W0 = SPREAD / MIDDLE
W1 = 1.0 / (2.0 * MIDDLE / SPREAD - W0)
W2 = 1.0 / (2.0 * MIDDLE / SPREAD - W1)


def sweep_kernel(main, side, lo, hi, grids, face_layer, face_row, face_col, inverse, residual, out, d0, d1, rest):
    lane = iota((144, 128), 1)
    kept = (lane < 2) | (lane >= 126)

    def supplied(i):
        if 3 <= i <= 6:
            at = (i - 3) * 144
            return main[at : at + 144, :], side[at : at + 144, :]
        source, second = (lo, i == 2) if i < 3 else (hi, i == 8)
        at = 144 if second else 0
        beside = source[288:432, :].astype(F32)
        if second:
            beside = turned_by(beside, -4, 1)
        return source[at : at + 144, :].astype(F32), jnp.where(kept, beside, 0.0)

    for i in range(1, 9):
        start = residual[i - 1] + jnp.concatenate(supplied(i), axis=1)
        rest[i - 1] = start
        d0[i - 1] = start * inverse[i - 1] * (1.0 / MIDDLE)

    def share(i, d):
        return (
            face_layer[i] * d[i]
            + face_layer[i - 1] * d[i - 2]
            + around(face_row[i - 1], face_col[i - 1], d[i - 1])
        )

    for i in range(2, 8):
        start = rest[i - 1]
        later = start * (1.0 - 1.0 / MIDDLE) + share(i, d0)
        d1[i - 1] = W1 * W0 * d0[i - 1] + (2.0 * W1 / SPREAD) * (later * inverse[i - 1])
        rest[i - 1] = later - (W1 * W0 / MIDDLE) * start - (2.0 * W1 / SPREAD) * later
    for i in range(3, 7):
        last = rest[i - 1] + share(i, d1)
        step = d0[i - 1] + d1[i - 1] * (1.0 + W2 * W1) + (2.0 * W2 / SPREAD) * (last * inverse[i - 1])
        at = (i - 3) * 128
        out[at : at + 128, :] = grids[i, 0:128, :] + step[0:128, 0:128]


def sds(shape, dtype):
    return jax.ShapeDtypeStruct(shape, dtype)


def call(kernel, shape, args, mib=12, scratch=(), far=(), far_out=False):
    vmem, anywhere = pl.BlockSpec(memory_space=pltpu.VMEM), pl.BlockSpec(memory_space=pltpu.HBM)
    return pl.pallas_call(
        kernel,
        out_shape=shape,
        in_specs=[anywhere if i in far else vmem for i in range(len(args))],
        out_specs=jax.tree.map(lambda _: anywhere if far_out else vmem, shape),
        scratch_shapes=list(scratch),
        compiler_params=pltpu.CompilerParams(vmem_limit_bytes=mib * 2**20),
    )(*args)


def pairs(axis):
    up = [(i, i + 1) for i in range(lax.axis_size(axis) - 1)]
    return up, [(b, a) for a, b in up]


def exchange(to_next, to_last, axis):
    up, down = pairs(axis)
    return lax.ppermute(to_next, axis, up), lax.ppermute(to_last, axis, down)


def extended_grids(temp, cond, mass):
    eight, rows, edge = sds((8, 128, 128), BF16), sds((240, 128), BF16), sds((144, 128), BF16)
    own, up, down = call(
        layers_kernel,
        (sds((3, 4, 128, 128), F32), eight, eight),
        (temp, cond, mass),
        scratch=[pltpu.SemaphoreType.DMA((3,))],
        far=range(3),
    )
    lo, hi = exchange(up, down, LAYER)
    ends = call(rows_kernel, (rows, rows), (own, lo, hi))
    above, below = exchange(*ends, "row")
    wide, to_left, to_right = call(
        gather_kernel, (sds((30, 144, 128), F32), edge, edge), (own, lo, hi, above, below), mib=12
    )
    return wide, ends, exchange(to_right, to_left, COL)


def operator(wide, from_left, from_right):
    eight = sds((8, 144, 256), F32)
    return call(
        operator_kernel,
        (sds((9, 144, 256), F32), eight, eight, eight, eight),
        (wide, from_left, from_right),
        mib=12,
        scratch=[pltpu.VMEM((30, 144, 256), F32)],
    )


def shards(temp, cond, mass, toggling, baseline, panel, place, holder, tier, warming):
    row64 = pltpu.VMEM((1, 64), I32)
    message, placing, columns = call(
        message_kernel,
        (sds((64, 128), F32), sds((1024, 64), BF16), sds((64, 128), I32)),
        (temp, panel.reshape(1, 64), place, holder, tier),
        mib=60,
        scratch=[
            pltpu.VMEM((4, 128, 128), F32), row64, row64, row64,
            pltpu.VMEM((1, 16), I32), pltpu.SemaphoreType.DMA((5,)),
        ],
        far=range(5),
    )
    messages = lax.all_to_all(message.reshape(64, 1, 128), CUBE, split_axis=0, concat_axis=0, tiled=True)
    messages = messages.reshape(64, 128)
    send = call(
        power_kernel,
        sds((256, 4736), BF16),
        (messages, columns, warming, toggling[0], baseline[0], placing),
        mib=60,
        scratch=[
            pltpu.VMEM((64, 128), F32), pltpu.VMEM((64, 128), I32), pltpu.VMEM((1, 16), F32),
            pltpu.VMEM((64, 4096), BF16), pltpu.VMEM((64, 4096), BF16), pltpu.VMEM((1024, 64), BF16),
            pltpu.VMEM((256, 4736), BF16), pltpu.SemaphoreType.DMA((15,)),
        ],
        far=range(6),
        far_out=True,
    )
    received = lax.all_to_all(send.reshape(16, 16, 4736), PLANE, split_axis=0, concat_axis=0, tiled=True)
    wide, ends, beside = extended_grids(temp, cond, mass)
    selector = call(selector_kernel, sds((576, 256), BF16), (messages, *ends))
    partial = call(
        combine_kernel, sds((64, 4480), F32), (selector, received.reshape(256, 4736))
    )
    parts = lax.all_to_all(
        partial.astype(jnp.float16).reshape(4, 16, 4480), "zlo", split_axis=0, concat_axis=0, tiled=True
    )
    terms = operator(wide, *beside)
    block, strip = sds((576, 128), F32), sds((432, 128), BF16)
    density, main, side, up, down = call(
        unpack_kernel,
        (sds((512, 128), F32), block, block, strip, strip),
        (jnp.sum(parts.astype(F32), axis=0), *beside),
        scratch=[pltpu.VMEM((512, 128), F32)],
    )
    lo, hi = exchange(up, down, LAYER)
    eight = pltpu.VMEM((8, 144, 256), F32)
    guess = call(
        sweep_kernel,
        sds((512, 128), F32),
        (main, side, lo, hi, wide, *terms),
        mib=12,
        scratch=[eight, eight, eight],
    )
    return guess.reshape(4, 128, 128), density.reshape(4, 128, 128)


def solution(mesh):
    fine = Mesh(mesh.devices.reshape(4, 4, 4, 4, 2), ("row", "zlo", "y", "zhi", "core"))
    grid = P(LAYER, "row", COL)
    slot = ("row", "zlo", "y", "zhi", "core")
    return jax.shard_map(
        shards,
        mesh=fine,
        in_specs=(
            grid,
            grid,
            grid,
            P(slot, None, None),
            P(slot, None, None),
            P(slot, None, None),
            P(slot, None),
            P(slot, None),
            P(slot, None),
            P(slot, None),
        ),
        out_specs=(grid, grid),
        check_vma=False,
    )
```

```python
import jax
import jax.numpy as jnp
from jax import lax
from jax.experimental import pallas as pl
from jax.experimental.pallas import tpu as pltpu
from jax.sharding import Mesh
from jax.sharding import PartitionSpec as P

eig_low = 0.1
eig_high = 2.0

LAYER = ("zhi", "core")
COL = ("zlo", "y")
CUBE = ("row", "zlo", "y")
PLANE = ("row", "y")

F32, BF16, I32 = jnp.float32, jnp.bfloat16, jnp.int32


def iota(shape, dim):
    return lax.broadcasted_iota(I32, shape, dim)


def as_column(row):
    n = row.shape[1]
    return jnp.sum(jnp.where(iota((n, n), 0) == iota((n, n), 1), row, 0), axis=1, keepdims=True)


def slot_rows(panel, place, holder, tier):
    layer = jnp.sum(jnp.where(iota((16, 64), 0) == holder, as_column(tier), 0), axis=0, keepdims=True)
    pos = layer * 4 + place
    ident = ((panel >> 2) & 3) * 16 + pos
    column = (panel >> 4) * 4 + (panel & 3)
    same = (as_column(column) == column) & (iota((64, 64), 0) < iota((64, 64), 1))
    rank = jnp.sum(same.astype(I32), axis=0, keepdims=True)
    return pos, ident, column * 16 + rank


def place_slots(panel, pos, dest, holder, placing, columns):
    x, y, rank = panel >> 4, panel & 3, dest & 15
    lower, right = (pos >> 1) & 1, pos & 1
    next_x = x + lower * 2 - 1
    next_y = (y + right * 2 + 3) & 3
    inside = (next_x >= 0) & (next_x <= 3)
    targets = (
        dest,
        jnp.where(inside, (next_x * 4 + y) * 16 + rank, -1),
        (x * 4 + next_y) * 16 + rank,
        jnp.where(inside, (next_x * 4 + next_y) * 16 + rank, -1),
    )
    for k, target in enumerate(targets):
        placing[pl.ds(k * 256, 256), :] = jnp.where(iota((256, 64), 0) == target, 1.0, 0.0).astype(BF16)
    lane = iota((64, 128), 1)
    columns[...] = jnp.where(
        lane == 0, as_column(panel), jnp.where(lane == 1, as_column(pos), as_column(holder))
    )


def message_kernel(
    temp, cond, mass, panel, place, holder, tier, out, placing, columns, own, last, first,
    panel_v, place_v, holder_v, tier_v, sems,
):
    pairs = [(panel, panel_v), (place, place_v), (holder, holder_v), (tier, tier_v)]
    pairs += [(grid, own.at[a]) for a, grid in enumerate((temp, cond, mass))]
    copies = [pltpu.make_async_copy(a, b, sems.at[i]) for i, (a, b) in enumerate(pairs)]
    for copy in copies:
        copy.start()
    for copy in copies[:4]:
        copy.wait()
    panel_row, holder_row = panel_v[...], holder_v[...]
    pos, ident, dest = slot_rows(panel_row, place_v[...], holder_row, tier_v[...])
    place_slots(panel_row, pos, dest, holder_row, placing, columns)
    code = (dest * 64 + ident).astype(F32)
    for copy in copies[4:]:
        copy.wait()
    grids = own[...].reshape(12, 128, 128)
    last[...] = grids[:, 120:128, :].reshape(96, 128).astype(BF16)
    first[...] = grids[:, 0:8, :].reshape(96, 128).astype(BF16)
    sums = jnp.sum(own[0].reshape(8, 64, 128), axis=1)
    lane = iota((8, 128), 1)
    first = jnp.sum(jnp.where(lane < 64, sums, 0.0), axis=1, keepdims=True)
    second = jnp.sum(jnp.where(lane < 64, 0.0, sums), axis=1, keepdims=True)
    at = iota((8, 128), 0) * 2
    means = jnp.where(lane == at, first, jnp.where(lane == at + 1, second, 0.0))
    means = jnp.sum(means, axis=0, keepdims=True) * (1.0 / 4096.0)
    row = jnp.where(iota((1, 128), 1) < 64, means, jnp.concatenate([code, code], axis=1))
    out[...] = jnp.broadcast_to(row, (64, 128))


def power_kernel(
    far_messages, far_columns, far_warming, far_toggling, far_baseline, far_placing, _above, _below, out,
    messages, columns, warming, toggling, baseline, placing, sent, sems,
):
    pairs = [
        (far_messages, messages),
        (far_columns, columns),
        (far_warming, warming),
        (far_toggling, toggling),
        (far_baseline, baseline),
        (far_placing, placing),
    ]
    loads = [pltpu.make_async_copy(a, b, sems.at[9 + i]) for i, (a, b) in enumerate(pairs)]
    for load in loads:
        load.start()
    loads[0].wait()
    loads[1].wait()
    tile, pos, holder = (columns[:, k : k + 1] for k in range(3))
    lower, right = (pos >> 1) & 1, pos & 1
    pick = jnp.where(iota((64, 64), 1) == tile, 1.0, 0.0)
    means = jnp.dot(pick, messages[...], precision=lax.Precision.HIGHEST, preferred_element_type=F32)
    lane = iota((64, 128), 1)
    slot_mean = jnp.sum(jnp.where(lane == pos, means, 0.0), axis=1, keepdims=True)
    member = iota((64, 16), 1) == holder
    total = jnp.sum(jnp.where(member, slot_mean, 0.0), axis=0, keepdims=True)
    count = jnp.sum(jnp.where(member, 1.0, 0.0), axis=0, keepdims=True)
    loads[2].wait()
    leak = jnp.exp(warming[...] * (total / count))
    factor = jnp.sum(jnp.where(member, leak, 0.0), axis=1, keepdims=True)

    def place(kind, values):
        at = placing[kind * 256 : (kind + 1) * 256, :]
        return jnp.dot(at, values.astype(BF16), preferred_element_type=F32).astype(BF16)

    copies = []

    def send(start, width):
        at = pl.ds(start, width)
        copy = pltpu.make_async_copy(sent.at[:, at], out.at[:, at], sems.at[len(copies)])
        copy.start()
        copies.append(copy)

    for load in loads[3:]:
        load.wait()
    edge = ((lane & 63) >> 1) == right * 31
    sides = jnp.zeros((64, 128), F32)
    width = 512
    for k in range(8):
        at = pl.ds(k * width, width)
        power = (toggling[:, at].astype(F32) + factor * baseline[:, at].astype(F32)).astype(BF16)
        sent[:, at] = place(0, power)
        send(k * width, width)
        power = power.astype(F32)
        for t in range(4):
            piece = power[:, t * 128 : (t + 1) * 128]
            shift = 2 * (4 * k + t)
            kept = jnp.where(edge, piece, 0.0)
            sides = sides + (pltpu.roll(kept, shift, 1) if shift else kept)
            if k == 0 and t == 0:
                top = piece
    rows = jnp.where(lower == 0, top, piece)
    sides = jnp.where(right == 0, sides, pltpu.roll(sides, 66, 1))
    corner = jnp.sum(jnp.where(lane == lower * 64 + right * 63, rows, 0.0), axis=1, keepdims=True)
    quarter = (1 - lower) * 2 + 1 - right
    both = jnp.concatenate([jnp.where(lower == 1, rows, 0.0), jnp.where(lower == 0, rows, 0.0)], axis=1)
    sent[:, 4096:4352] = place(1, both)
    both = jnp.concatenate([jnp.where(right == 1, sides, 0.0), jnp.where(right == 0, sides, 0.0)], axis=1)
    sent[:, 4352:4608] = place(2, both)
    sent[:, 4608:4736] = place(3, jnp.where(lane == quarter, corner, 0.0))
    send(4096, 640)
    for copy in copies:
        copy.wait()


def selector_kernel(messages, _to_left, _to_right, out):
    x, y = lax.axis_index("row"), lax.axis_index("y")
    plane = lax.axis_index("zlo")
    code = jnp.concatenate([messages[pl.ds(r * 16 + plane * 4, 4), :] for r in range(4)], axis=0)
    code = jnp.where(iota((16, 128), 1) < 64, -1.0, code).astype(I32)
    dest, ident = code >> 6, code & 63
    lane = iota((16, 256), 1)

    def idents(dx, dy):
        base = ((x + dx) * 4 + ((y + dy + 4) & 3)) * 16
        ids = jnp.zeros((16, 256), I32)
        for r in range(16):
            hit = jnp.sum(jnp.where(dest == base + r, ident + 1, 0), axis=1, keepdims=True)
            ids = jnp.where((lane & 15) == r, hit, ids)
        ids = jnp.sum(jnp.where((lane >> 4) == iota((16, 256), 0), ids, 0), axis=0, keepdims=True) - 1
        turn = jnp.where(y == 0, 1, 0) if dy < 0 else jnp.where(y == 3, -1, 0) if dy > 0 else 0
        return ids, (ids >> 4) + turn, (ids >> 2) & 3, (ids >> 1) & 1, ids & 1

    def put(k, ids, target):
        out[pl.ds(k * 64, 64), :] = jnp.where(
            (iota((64, 256), 0) == target) & (ids >= 0), 1.0, 0.0
        ).astype(BF16)

    ids, *_ = idents(0, 0)
    put(0, ids, ids)
    for k, dx in enumerate((-1, 1)):
        ids, z, layer, _, pc = idents(dx, 0)
        put(1 + k, ids, z * 16 + k * 8 + layer * 2 + pc)
    for k, dy in enumerate((-1, 1)):
        ids, z, layer, pr, _ = idents(0, dy)
        put(3 + k, ids, z * 16 + k * 8 + layer * 2 + pr)
    for k in range(4):
        ids, z, layer, _, _ = idents((k >> 1) * 2 - 1, (k & 1) * 2 - 1)
        put(5 + k, ids, z * 16 + layer)


def combine_kernel(selector, received, out):
    def add(k, start, width):
        return jnp.dot(
            selector[k * 64 : (k + 1) * 64, :],
            received[:, start : start + width],
            preferred_element_type=F32,
        )

    for k in range(8):
        out[:, k * 512 : (k + 1) * 512] = add(0, k * 512, 512)
    out[:, 4096:4224] = add(1, 4096, 128) + add(2, 4224, 128)
    out[:, 4224:4352] = add(3, 4352, 128) + add(4, 4480, 128)
    lane = iota((64, 128), 1)
    corners = jnp.zeros((64, 128), F32)
    for k in range(4):
        corners = jnp.where(lane == k, add(5 + k, 4608, 128), corners)
    out[:, 4352:4480] = corners


def unpack_kernel(whole, _left, _right, density, main, side, up, down, turned):
    for k in range(32):
        turned[k * 16 : (k + 1) * 16, :] = whole[:, k * 128 : (k + 1) * 128]
    low = iota((32, 128), 1) < 64
    lane = iota((64, 128), 1)
    low_row = iota((1, 128), 1) < 64
    lane16, row16 = iota((16, 128), 1), iota((16, 128), 0)
    rows, columns, corners = whole[:, 4096:4224], whole[:, 4224:4352], whole[:, 4352:4480]
    cell = iota((64, 128), 0)
    turn = []
    for c in range(2):
        pick = jnp.where(lane == (cell & 1) * 64 + (cell - (cell & 1)) + c, 1.0, 0.0)
        turn.append(
            lax.dot_general(
                pick, columns, (((1,), (1,)), ((), ())),
                precision=lax.Precision.HIGHEST, preferred_element_type=F32,
            )
        )
    for layer in range(4):
        base = layer * 144
        for r in range(2):
            left = turned[pl.ds(layer * 4 + r * 2, 32, stride=16), :]
            right = turned[pl.ds(layer * 4 + r * 2 + 1, 32, stride=16), :]
            at = base + r * 64
            main[pl.ds(at, 32, stride=2), :] = jnp.where(low, left, pltpu.roll(right, 64, 1))
            main[pl.ds(at + 1, 32, stride=2), :] = jnp.where(low, pltpu.roll(left, 64, 1), right)
            k = layer * 2 + r
            strip = jnp.where(lane == 0, turn[0][:, 8 + k : 9 + k], 0.0)
            strip = jnp.where(lane == 1, turn[1][:, 8 + k : 9 + k], strip)
            strip = jnp.where(lane == 126, turn[0][:, k : k + 1], strip)
            side[at : at + 64, :] = jnp.where(lane == 127, turn[1][:, k : k + 1], strip)
        block = jnp.zeros((16, 128), F32)
        for kind, first_row in ((0, 14), (1, 0)):
            k = kind * 8 + layer * 2
            a, b = rows[k : k + 1, :], rows[k + 1 : k + 2, :]
            first = jnp.where(low_row, a, pltpu.roll(b, 64, 1))
            second = jnp.where(low_row, pltpu.roll(a, 64, 1), b)
            block = jnp.where(row16 == first_row, first, block)
            block = jnp.where(row16 == first_row + 1, second, block)
        main[base + 128 : base + 144, :] = block
        block = jnp.zeros((16, 128), F32)
        for k, (r, at_lane) in enumerate(((15, 127), (15, 0), (0, 127), (0, 0))):
            value = corners[layer : layer + 1, k : k + 1]
            block = jnp.where((row16 == r) & (lane16 == at_lane), value, block)
        side[base + 128 : base + 144, :] = block
        density[layer * 128 : (layer + 1) * 128, :] = main[base : base + 128, :]
    for out, first in ((up, 288), (down, 0)):
        out[0:288, :] = main[first : first + 288, :].astype(BF16)
        second = side[first + 144 : first + 288, :]
        out[288:432, :] = (side[first : first + 144, :] + pltpu.roll(second, 4, 1)).astype(BF16)


def depth(a):
    return 3 if a < 2 else 2


def beyond(lo, hi, a, layer):
    if layer < 3:
        k = layer - 3 + depth(a)
        return (lo, 3 * a + k) if k >= 0 else None
    k = layer - 7
    return (hi, 3 * a + k) if k < depth(a) else None


def with_rows(own, above, below, a, layer):
    at = (a * 4 + layer) * 8
    return jnp.concatenate([own[a, layer], below[at : at + 8], above[at : at + 8]], axis=0)


def layers_kernel(own, above, below, up, down):
    over, under = above[...].astype(F32), below[...].astype(F32)
    for a in range(3):
        for k in range(depth(a)):
            up[3 * a + k] = with_rows(own, over, under, a, 4 - depth(a) + k).astype(BF16)
            down[3 * a + k] = with_rows(own, over, under, a, k).astype(BF16)


def gather_kernel(own, lo, hi, above, below, out, to_left, to_right):
    over, under = above[...].astype(F32), below[...].astype(F32)
    lane = iota((144, 128), 1)
    left, right = jnp.zeros((144, 128), F32), jnp.zeros((144, 128), F32)
    for a in range(3):
        for layer in range(10):
            i = a * 10 + layer
            if 3 <= layer < 7:
                piece = with_rows(own, over, under, a, layer - 3)
            elif found := beyond(lo, hi, a, layer):
                piece = found[0][found[1]].astype(F32)
            else:
                piece = jnp.zeros((144, 128), F32)
            out[i] = piece
            base = a * 40 + layer * 4
            here = (lane >= base) & (lane < base + 3)
            left = jnp.where(here, pltpu.roll(piece, base, 1) if base else piece, left)
            right = jnp.where(here, pltpu.roll(piece, base + 3, 1), right)
    to_left[...] = left.astype(BF16)
    to_right[...] = right.astype(BF16)


def turned_by(x, shift, axis):
    return pltpu.roll(x, shift % x.shape[axis], axis)


def around(face_row, face_col, v):
    return (
        face_row * turned_by(v, -1, 0)
        + turned_by(face_row * v, 1, 0)
        + face_col * turned_by(v, -1, 1)
        + turned_by(face_col * v, 1, 1)
    )


def operator_kernel(grids, from_left, from_right, face_layer, face_row, face_col, inverse, residual, wide):
    left, right = from_left[...].astype(F32), from_right[...].astype(F32)
    lane = iota((144, 128), 1)
    for a in range(3):
        for layer in range(10):
            i, base = a * 10 + layer, a * 40 + layer * 4
            high = turned_by(right, -base, 1) if base else right
            side = jnp.where(lane < 3, high, jnp.where(lane >= 125, turned_by(left, 125 - base, 1), 0.0))
            wide[i, :, 0:128] = grids[i]
            wide[i, :, 128:256] = side
    for layer in range(9):
        face_layer[layer] = 0.5 * (wide[10 + layer] + wide[11 + layer])
    for layer in range(1, 9):
        temp, cond, mass = (wide[a * 10 + layer] for a in range(3))
        rows = 0.5 * (cond + turned_by(cond, -1, 0))
        cols = 0.5 * (cond + turned_by(cond, -1, 1))
        face_row[layer - 1] = rows
        face_col[layer - 1] = cols
        after, before = face_layer[layer], face_layer[layer - 1]
        diagonal = mass + after + before + rows + turned_by(rows, 1, 0) + cols + turned_by(cols, 1, 1)
        share = after * wide[layer + 1] + before * wide[layer - 1] + around(rows, cols, temp)
        residual[layer - 1] = mass * temp + (share - diagonal * temp)
        inverse[layer - 1] = jnp.where(mass > 0.0, 1.0 / diagonal, 0.0)


MIDDLE = (eig_low + eig_high) / 2.0
SPREAD = (eig_high - eig_low) / 2.0
W0 = SPREAD / MIDDLE
W1 = 1.0 / (2.0 * MIDDLE / SPREAD - W0)
W2 = 1.0 / (2.0 * MIDDLE / SPREAD - W1)


def sweep_kernel(main, side, lo, hi, grids, face_layer, face_row, face_col, inverse, residual, out, d0, d1, rest):
    lane = iota((144, 128), 1)
    kept = (lane < 2) | (lane >= 126)

    def supplied(i):
        if 3 <= i <= 6:
            at = (i - 3) * 144
            return main[at : at + 144, :], side[at : at + 144, :]
        source, second = (lo, i == 2) if i < 3 else (hi, i == 8)
        at = 144 if second else 0
        beside = source[288:432, :].astype(F32)
        if second:
            beside = turned_by(beside, -4, 1)
        return source[at : at + 144, :].astype(F32), jnp.where(kept, beside, 0.0)

    for i in range(1, 9):
        start = residual[i - 1] + jnp.concatenate(supplied(i), axis=1)
        rest[i - 1] = start
        d0[i - 1] = start * inverse[i - 1] * (1.0 / MIDDLE)

    def share(i, d):
        return (
            face_layer[i] * d[i]
            + face_layer[i - 1] * d[i - 2]
            + around(face_row[i - 1], face_col[i - 1], d[i - 1])
        )

    for i in range(2, 8):
        start = rest[i - 1]
        later = start * (1.0 - 1.0 / MIDDLE) + share(i, d0)
        d1[i - 1] = W1 * W0 * d0[i - 1] + (2.0 * W1 / SPREAD) * (later * inverse[i - 1])
        rest[i - 1] = later - (W1 * W0 / MIDDLE) * start - (2.0 * W1 / SPREAD) * later
    for i in range(3, 7):
        last = rest[i - 1] + share(i, d1)
        step = d0[i - 1] + d1[i - 1] * (1.0 + W2 * W1) + (2.0 * W2 / SPREAD) * (last * inverse[i - 1])
        at = (i - 3) * 128
        out[at : at + 128, :] = grids[i, 0:128, :] + step[0:128, 0:128]


def sds(shape, dtype):
    return jax.ShapeDtypeStruct(shape, dtype)


def call(kernel, shape, args, mib=12, scratch=(), far=(), far_out=False):
    vmem, anywhere = pl.BlockSpec(memory_space=pltpu.VMEM), pl.BlockSpec(memory_space=pltpu.HBM)
    return pl.pallas_call(
        kernel,
        out_shape=shape,
        in_specs=[anywhere if i in far else vmem for i in range(len(args))],
        out_specs=jax.tree.map(lambda _: anywhere if far_out else vmem, shape),
        scratch_shapes=list(scratch),
        compiler_params=pltpu.CompilerParams(vmem_limit_bytes=mib * 2**20),
    )(*args)


def pairs(axis):
    up = [(i, i + 1) for i in range(lax.axis_size(axis) - 1)]
    return up, [(b, a) for a, b in up]


def exchange(to_next, to_last, axis):
    up, down = pairs(axis)
    return lax.ppermute(to_next, axis, up), lax.ppermute(to_last, axis, down)


def extended_grids(own, above, below):
    eight, edge = sds((8, 144, 128), BF16), sds((144, 128), BF16)
    lo, hi = exchange(*call(layers_kernel, (eight, eight), (own, above, below)), LAYER)
    wide, *edges = call(
        gather_kernel, (sds((30, 144, 128), F32), edge, edge), (own, lo, hi, above, below)
    )
    to_left, to_right = edges
    return wide, edges, exchange(to_right, to_left, COL)


def operator(wide, from_left, from_right):
    eight = sds((8, 144, 256), F32)
    return call(
        operator_kernel,
        (sds((9, 144, 256), F32), eight, eight, eight, eight),
        (wide, from_left, from_right),
        mib=12,
        scratch=[pltpu.VMEM((30, 144, 256), F32)],
    )


def shards(temp, cond, mass, toggling, baseline, panel, place, holder, tier, warming):
    row64 = pltpu.VMEM((1, 64), I32)
    ends = sds((96, 128), BF16)
    message, placing, columns, own, last, first = call(
        message_kernel,
        (
            sds((64, 128), F32), sds((1024, 64), BF16), sds((64, 128), I32),
            sds((3, 4, 128, 128), F32), ends, ends,
        ),
        (temp, cond, mass, panel.reshape(1, 64), place, holder, tier),
        mib=60,
        scratch=[row64, row64, row64, pltpu.VMEM((1, 16), I32), pltpu.SemaphoreType.DMA((7,))],
        far=range(7),
    )
    above, below = exchange(last, first, "row")
    messages = lax.all_to_all(message.reshape(64, 1, 128), CUBE, split_axis=0, concat_axis=0, tiled=True)
    messages = messages.reshape(64, 128)
    send = call(
        power_kernel,
        sds((256, 4736), BF16),
        (messages, columns, warming, toggling[0], baseline[0], placing, above, below),
        mib=60,
        scratch=[
            pltpu.VMEM((64, 128), F32), pltpu.VMEM((64, 128), I32), pltpu.VMEM((1, 16), F32),
            pltpu.VMEM((64, 4096), BF16), pltpu.VMEM((64, 4096), BF16), pltpu.VMEM((1024, 64), BF16),
            pltpu.VMEM((256, 4736), BF16), pltpu.SemaphoreType.DMA((15,)),
        ],
        far=range(8),
        far_out=True,
    )
    received = lax.all_to_all(send.reshape(16, 16, 4736), PLANE, split_axis=0, concat_axis=0, tiled=True)
    wide, edges, beside = extended_grids(own, above, below)
    selector = call(selector_kernel, sds((576, 256), BF16), (messages, *edges))
    partial = call(
        combine_kernel, sds((64, 4480), F32), (selector, received.reshape(256, 4736))
    )
    parts = lax.all_to_all(
        partial.astype(jnp.float16).reshape(4, 16, 4480), "zlo", split_axis=0, concat_axis=0, tiled=True
    )
    terms = operator(wide, *beside)
    block, strip = sds((576, 128), F32), sds((432, 128), BF16)
    density, main, side, up, down = call(
        unpack_kernel,
        (sds((512, 128), F32), block, block, strip, strip),
        (jnp.sum(parts.astype(F32), axis=0), *beside),
        scratch=[pltpu.VMEM((512, 128), F32)],
    )
    lo, hi = exchange(up, down, LAYER)
    eight = pltpu.VMEM((8, 144, 256), F32)
    guess = call(
        sweep_kernel,
        sds((512, 128), F32),
        (main, side, lo, hi, wide, *terms),
        mib=12,
        scratch=[eight, eight, eight],
    )
    return guess.reshape(4, 128, 128), density.reshape(4, 128, 128)


def solution(mesh):
    fine = Mesh(mesh.devices.reshape(4, 4, 4, 4, 2), ("row", "zlo", "y", "zhi", "core"))
    grid = P(LAYER, "row", COL)
    slot = ("row", "zlo", "y", "zhi", "core")
    return jax.shard_map(
        shards,
        mesh=fine,
        in_specs=(
            grid,
            grid,
            grid,
            P(slot, None, None),
            P(slot, None, None),
            P(slot, None, None),
            P(slot, None),
            P(slot, None),
            P(slot, None),
            P(slot, None),
        ),
        out_specs=(grid, grid),
        check_vma=False,
    )
```

```python
import jax
import jax.numpy as jnp
from jax import lax
from jax.experimental import pallas as pl
from jax.experimental.pallas import tpu as pltpu
from jax.sharding import Mesh
from jax.sharding import PartitionSpec as P

eig_low = 0.1
eig_high = 2.0

LAYER = ("zhi", "core")
COL = ("zlo", "y")
CUBE = ("row", "zlo", "y")
PLANE = ("row", "y")

F32, BF16, I32 = jnp.float32, jnp.bfloat16, jnp.int32


def iota(shape, dim):
    return lax.broadcasted_iota(I32, shape, dim)


def as_column(row):
    n = row.shape[1]
    return jnp.sum(jnp.where(iota((n, n), 0) == iota((n, n), 1), row, 0), axis=1, keepdims=True)


def slot_rows(panel, place, holder, tier):
    layer = jnp.sum(jnp.where(iota((16, 64), 0) == holder, as_column(tier), 0), axis=0, keepdims=True)
    pos = layer * 4 + place
    ident = ((panel >> 2) & 3) * 16 + pos
    column = (panel >> 4) * 4 + (panel & 3)
    same = (as_column(column) == column) & (iota((64, 64), 0) < iota((64, 64), 1))
    rank = jnp.sum(same.astype(I32), axis=0, keepdims=True)
    return pos, ident, column * 16 + rank


def place_slots(panel, pos, dest, holder, placing, columns):
    x, y, rank = panel >> 4, panel & 3, dest & 15
    lower, right = (pos >> 1) & 1, pos & 1
    next_x = x + lower * 2 - 1
    next_y = (y + right * 2 + 3) & 3
    inside = (next_x >= 0) & (next_x <= 3)
    targets = (
        dest,
        jnp.where(inside, (next_x * 4 + y) * 16 + rank, -1),
        (x * 4 + next_y) * 16 + rank,
        jnp.where(inside, (next_x * 4 + next_y) * 16 + rank, -1),
    )
    for k, target in enumerate(targets):
        placing[pl.ds(k * 256, 256), :] = jnp.where(iota((256, 64), 0) == target, 1.0, 0.0).astype(BF16)
    lane = iota((64, 128), 1)
    columns[...] = jnp.where(
        lane == 0, as_column(panel), jnp.where(lane == 1, as_column(pos), as_column(holder))
    )


def message_kernel(temp, panel, place, holder, tier, out, placing, columns, temp_v, panel_v, place_v, holder_v, tier_v, sems):
    pairs = [(panel, panel_v), (place, place_v), (holder, holder_v), (tier, tier_v), (temp, temp_v)]
    copies = [pltpu.make_async_copy(a, b, sems.at[i]) for i, (a, b) in enumerate(pairs)]
    for copy in copies:
        copy.start()
    for copy in copies[:4]:
        copy.wait()
    panel_row, holder_row = panel_v[...], holder_v[...]
    pos, ident, dest = slot_rows(panel_row, place_v[...], holder_row, tier_v[...])
    place_slots(panel_row, pos, dest, holder_row, placing, columns)
    code = (dest * 64 + ident).astype(F32)
    copies[4].wait()
    sums = jnp.sum(temp_v[...].reshape(8, 64, 128), axis=1)
    lane = iota((8, 128), 1)
    first = jnp.sum(jnp.where(lane < 64, sums, 0.0), axis=1, keepdims=True)
    second = jnp.sum(jnp.where(lane < 64, 0.0, sums), axis=1, keepdims=True)
    at = iota((8, 128), 0) * 2
    means = jnp.where(lane == at, first, jnp.where(lane == at + 1, second, 0.0))
    means = jnp.sum(means, axis=0, keepdims=True) * (1.0 / 4096.0)
    row = jnp.where(iota((1, 128), 1) < 64, means, jnp.concatenate([code, code], axis=1))
    out[...] = jnp.broadcast_to(row, (64, 128))


def power_kernel(
    far_messages, far_columns, far_warming, far_toggling, far_baseline, far_placing, out,
    messages, columns, warming, toggling, baseline, placing, sent, sems,
):
    pairs = [
        (far_messages, messages),
        (far_columns, columns),
        (far_warming, warming),
        (far_toggling, toggling),
        (far_baseline, baseline),
        (far_placing, placing),
    ]
    loads = [pltpu.make_async_copy(a, b, sems.at[9 + i]) for i, (a, b) in enumerate(pairs)]
    for load in loads:
        load.start()
    loads[0].wait()
    loads[1].wait()
    tile, pos, holder = (columns[:, k : k + 1] for k in range(3))
    lower, right = (pos >> 1) & 1, pos & 1
    pick = jnp.where(iota((64, 64), 1) == tile, 1.0, 0.0)
    means = jnp.dot(pick, messages[...], precision=lax.Precision.HIGHEST, preferred_element_type=F32)
    lane = iota((64, 128), 1)
    slot_mean = jnp.sum(jnp.where(lane == pos, means, 0.0), axis=1, keepdims=True)
    member = iota((64, 16), 1) == holder
    total = jnp.sum(jnp.where(member, slot_mean, 0.0), axis=0, keepdims=True)
    count = jnp.sum(jnp.where(member, 1.0, 0.0), axis=0, keepdims=True)
    loads[2].wait()
    leak = jnp.exp(warming[...] * (total / count))
    factor = jnp.sum(jnp.where(member, leak, 0.0), axis=1, keepdims=True)

    def place(kind, values):
        at = placing[kind * 256 : (kind + 1) * 256, :]
        return jnp.dot(at, values.astype(BF16), preferred_element_type=F32).astype(BF16)

    copies = []

    def send(start, width):
        at = pl.ds(start, width)
        copy = pltpu.make_async_copy(sent.at[:, at], out.at[:, at], sems.at[len(copies)])
        copy.start()
        copies.append(copy)

    for load in loads[3:]:
        load.wait()
    edge = ((lane & 63) >> 1) == right * 31
    sides = jnp.zeros((64, 128), F32)
    width = 512
    for k in range(8):
        at = pl.ds(k * width, width)
        power = (toggling[:, at].astype(F32) + factor * baseline[:, at].astype(F32)).astype(BF16)
        sent[:, at] = place(0, power)
        send(k * width, width)
        power = power.astype(F32)
        for t in range(4):
            piece = power[:, t * 128 : (t + 1) * 128]
            shift = 2 * (4 * k + t)
            kept = jnp.where(edge, piece, 0.0)
            sides = sides + (pltpu.roll(kept, shift, 1) if shift else kept)
            if k == 0 and t == 0:
                top = piece
    rows = jnp.where(lower == 0, top, piece)
    sides = jnp.where(right == 0, sides, pltpu.roll(sides, 66, 1))
    corner = jnp.sum(jnp.where(lane == lower * 64 + right * 63, rows, 0.0), axis=1, keepdims=True)
    quarter = (1 - lower) * 2 + 1 - right
    both = jnp.concatenate([jnp.where(lower == 1, rows, 0.0), jnp.where(lower == 0, rows, 0.0)], axis=1)
    sent[:, 4096:4352] = place(1, both)
    both = jnp.concatenate([jnp.where(right == 1, sides, 0.0), jnp.where(right == 0, sides, 0.0)], axis=1)
    sent[:, 4352:4608] = place(2, both)
    sent[:, 4608:4736] = place(3, jnp.where(lane == quarter, corner, 0.0))
    send(4096, 640)
    for copy in copies:
        copy.wait()


def selector_kernel(messages, out):
    x, y = lax.axis_index("row"), lax.axis_index("y")
    plane = lax.axis_index("zlo")
    code = jnp.concatenate([messages[pl.ds(r * 16 + plane * 4, 4), :] for r in range(4)], axis=0)
    code = jnp.where(iota((16, 128), 1) < 64, -1.0, code).astype(I32)
    dest, ident = code >> 6, code & 63
    lane = iota((16, 256), 1)

    def idents(dx, dy):
        base = ((x + dx) * 4 + ((y + dy + 4) & 3)) * 16
        ids = jnp.zeros((16, 256), I32)
        for r in range(16):
            hit = jnp.sum(jnp.where(dest == base + r, ident + 1, 0), axis=1, keepdims=True)
            ids = jnp.where((lane & 15) == r, hit, ids)
        ids = jnp.sum(jnp.where((lane >> 4) == iota((16, 256), 0), ids, 0), axis=0, keepdims=True) - 1
        turn = jnp.where(y == 0, 1, 0) if dy < 0 else jnp.where(y == 3, -1, 0) if dy > 0 else 0
        return ids, (ids >> 4) + turn, (ids >> 2) & 3, (ids >> 1) & 1, ids & 1

    def put(k, ids, target):
        out[pl.ds(k * 64, 64), :] = jnp.where(
            (iota((64, 256), 0) == target) & (ids >= 0), 1.0, 0.0
        ).astype(BF16)

    ids, *_ = idents(0, 0)
    put(0, ids, ids)
    for k, dx in enumerate((-1, 1)):
        ids, z, layer, _, pc = idents(dx, 0)
        put(1 + k, ids, z * 16 + k * 8 + layer * 2 + pc)
    for k, dy in enumerate((-1, 1)):
        ids, z, layer, pr, _ = idents(0, dy)
        put(3 + k, ids, z * 16 + k * 8 + layer * 2 + pr)
    for k in range(4):
        ids, z, layer, _, _ = idents((k >> 1) * 2 - 1, (k & 1) * 2 - 1)
        put(5 + k, ids, z * 16 + layer)


def combine_kernel(selector, received, _to_left, _to_right, out):
    def add(k, start, width):
        return jnp.dot(
            selector[k * 64 : (k + 1) * 64, :],
            received[:, start : start + width],
            preferred_element_type=F32,
        )

    for k in range(8):
        out[:, k * 512 : (k + 1) * 512] = add(0, k * 512, 512)
    out[:, 4096:4224] = add(1, 4096, 128) + add(2, 4224, 128)
    out[:, 4224:4352] = add(3, 4352, 128) + add(4, 4480, 128)
    lane = iota((64, 128), 1)
    corners = jnp.zeros((64, 128), F32)
    for k in range(4):
        corners = jnp.where(lane == k, add(5 + k, 4608, 128), corners)
    out[:, 4352:4480] = corners


def unpack_kernel(whole, _left, _right, density, main, side, far, near, turned):
    for k in range(32):
        turned[k * 16 : (k + 1) * 16, :] = whole[:, k * 128 : (k + 1) * 128]
    low = iota((32, 128), 1) < 64
    lane = iota((64, 128), 1)
    low_row = iota((1, 128), 1) < 64
    lane16, row16 = iota((16, 128), 1), iota((16, 128), 0)
    rows, columns, corners = whole[:, 4096:4224], whole[:, 4224:4352], whole[:, 4352:4480]
    cell = iota((64, 128), 0)
    turn = []
    for c in range(2):
        pick = jnp.where(lane == (cell & 1) * 64 + (cell - (cell & 1)) + c, 1.0, 0.0)
        turn.append(
            lax.dot_general(
                pick, columns, (((1,), (1,)), ((), ())),
                precision=lax.Precision.HIGHEST, preferred_element_type=F32,
            )
        )
    for layer in range(4):
        base = layer * 144
        for r in range(2):
            left = turned[pl.ds(layer * 4 + r * 2, 32, stride=16), :]
            right = turned[pl.ds(layer * 4 + r * 2 + 1, 32, stride=16), :]
            at = base + r * 64
            main[pl.ds(at, 32, stride=2), :] = jnp.where(low, left, pltpu.roll(right, 64, 1))
            main[pl.ds(at + 1, 32, stride=2), :] = jnp.where(low, pltpu.roll(left, 64, 1), right)
            k = layer * 2 + r
            strip = jnp.where(lane == 0, turn[0][:, 8 + k : 9 + k], 0.0)
            strip = jnp.where(lane == 1, turn[1][:, 8 + k : 9 + k], strip)
            strip = jnp.where(lane == 126, turn[0][:, k : k + 1], strip)
            side[at : at + 64, :] = jnp.where(lane == 127, turn[1][:, k : k + 1], strip)
        block = jnp.zeros((16, 128), F32)
        for kind, first_row in ((0, 14), (1, 0)):
            k = kind * 8 + layer * 2
            a, b = rows[k : k + 1, :], rows[k + 1 : k + 2, :]
            first = jnp.where(low_row, a, pltpu.roll(b, 64, 1))
            second = jnp.where(low_row, pltpu.roll(a, 64, 1), b)
            block = jnp.where(row16 == first_row, first, block)
            block = jnp.where(row16 == first_row + 1, second, block)
        main[base + 128 : base + 144, :] = block
        block = jnp.zeros((16, 128), F32)
        for k, (r, at_lane) in enumerate(((15, 127), (15, 0), (0, 127), (0, 0))):
            value = corners[layer : layer + 1, k : k + 1]
            block = jnp.where((row16 == r) & (lane16 == at_lane), value, block)
        side[base + 128 : base + 144, :] = block
        density[layer * 128 : (layer + 1) * 128, :] = main[base : base + 128, :]
    upper = jnp.where(lax.axis_index("core") == 1, 288, 0)
    for out, first in ((far, upper), (near, 288 - upper)):
        first = pl.multiple_of(first, 144)
        out[0:288, :] = main[pl.ds(first, 288), :].astype(BF16)
        second = side[pl.ds(first + 144, 144), :]
        out[288:432, :] = (side[pl.ds(first, 144), :] + pltpu.roll(second, 4, 1)).astype(BF16)


def depth(a):
    return 3 if a < 2 else 2


def beyond(a, layer):
    k = layer - 3 + depth(a) if layer < 3 else layer - 7
    return 3 * a + k if 0 <= k < depth(a) else None


def from_layer(far, near, a, layer, at):
    k = beyond(a, layer)
    if k is None:
        return None
    same, other = (near, far) if layer < 3 else (far, near)
    upper = lax.axis_index("core") == 1
    return jnp.where(upper, same[k, at, :].astype(F32), other[k, at, :].astype(F32))


def layers_kernel(temp, cond, mass, own, far, near, sems):
    upper = lax.axis_index("core") == 1
    copies = [pltpu.make_async_copy(a, own.at[i], sems.at[i]) for i, a in enumerate((temp, cond, mass))]
    for copy in copies:
        copy.start()
    for a, copy in enumerate(copies):
        copy.wait()
        for k in range(depth(a)):
            last, first = own[a, 4 - depth(a) + k], own[a, k]
            far[3 * a + k] = jnp.where(upper, last, first).astype(BF16)
            near[3 * a + k] = jnp.where(upper, first, last).astype(BF16)


def rows_kernel(own, far, near, last, first):
    lasts, firsts = [], []
    for a in range(3):
        for layer in range(10):
            if 3 <= layer < 7:
                lasts.append(own[a, layer - 3, 120:128, :])
                firsts.append(own[a, layer - 3, 0:8, :])
            else:
                zeros = jnp.zeros((8, 128), F32)
                ends = from_layer(far, near, a, layer, slice(112, 128))
                lasts.append(zeros if ends is None else ends[8:16])
                ends = from_layer(far, near, a, layer, slice(0, 16))
                firsts.append(zeros if ends is None else ends[0:8])
    last[...] = jnp.concatenate(lasts, axis=0).astype(BF16)
    first[...] = jnp.concatenate(firsts, axis=0).astype(BF16)


def gather_kernel(own, far, near, above, below, out, to_left, to_right):
    over, under = above[...].astype(F32), below[...].astype(F32)
    lane = iota((144, 128), 1)
    left, right = jnp.zeros((144, 128), F32), jnp.zeros((144, 128), F32)
    for a in range(3):
        for layer in range(10):
            i = a * 10 + layer
            if 3 <= layer < 7:
                source = own[a, layer - 3]
            else:
                source = from_layer(far, near, a, layer, slice(0, 128))
                source = jnp.zeros((128, 128), F32) if source is None else source
            piece = jnp.concatenate([source, under[8 * i : 8 * i + 8], over[8 * i : 8 * i + 8]], axis=0)
            out[i] = piece
            base = a * 40 + layer * 4
            here = (lane >= base) & (lane < base + 3)
            left = jnp.where(here, pltpu.roll(piece, base, 1) if base else piece, left)
            right = jnp.where(here, pltpu.roll(piece, base + 3, 1), right)
    to_left[...] = left.astype(BF16)
    to_right[...] = right.astype(BF16)


def turned_by(x, shift, axis):
    return pltpu.roll(x, shift % x.shape[axis], axis)


def around(face_row, face_col, v):
    return (
        face_row * turned_by(v, -1, 0)
        + turned_by(face_row * v, 1, 0)
        + face_col * turned_by(v, -1, 1)
        + turned_by(face_col * v, 1, 1)
    )


def operator_kernel(grids, from_left, from_right, face_layer, face_row, face_col, inverse, residual, wide):
    left, right = from_left[...].astype(F32), from_right[...].astype(F32)
    lane = iota((144, 128), 1)
    for a in range(3):
        for layer in range(10):
            i, base = a * 10 + layer, a * 40 + layer * 4
            high = turned_by(right, -base, 1) if base else right
            side = jnp.where(lane < 3, high, jnp.where(lane >= 125, turned_by(left, 125 - base, 1), 0.0))
            wide[i, :, 0:128] = grids[i]
            wide[i, :, 128:256] = side
    for layer in range(9):
        face_layer[layer] = 0.5 * (wide[10 + layer] + wide[11 + layer])
    for layer in range(1, 9):
        temp, cond, mass = (wide[a * 10 + layer] for a in range(3))
        rows = 0.5 * (cond + turned_by(cond, -1, 0))
        cols = 0.5 * (cond + turned_by(cond, -1, 1))
        face_row[layer - 1] = rows
        face_col[layer - 1] = cols
        after, before = face_layer[layer], face_layer[layer - 1]
        diagonal = mass + after + before + rows + turned_by(rows, 1, 0) + cols + turned_by(cols, 1, 1)
        share = after * wide[layer + 1] + before * wide[layer - 1] + around(rows, cols, temp)
        residual[layer - 1] = mass * temp + (share - diagonal * temp)
        inverse[layer - 1] = jnp.where(mass > 0.0, 1.0 / diagonal, 0.0)


MIDDLE = (eig_low + eig_high) / 2.0
SPREAD = (eig_high - eig_low) / 2.0
W0 = SPREAD / MIDDLE
W1 = 1.0 / (2.0 * MIDDLE / SPREAD - W0)
W2 = 1.0 / (2.0 * MIDDLE / SPREAD - W1)


def sweep_kernel(main, side, far, near, grids, face_layer, face_row, face_col, inverse, residual, out, d0, d1, rest):
    lane = iota((144, 128), 1)
    kept = (lane < 2) | (lane >= 126)
    upper = lax.axis_index("core") == 1

    def supplied(i):
        if 3 <= i <= 6:
            at = (i - 3) * 144
            return main[at : at + 144, :], side[at : at + 144, :]
        second = i in (2, 8)
        at = 144 if second else 0
        same, other = (near, far) if i < 3 else (far, near)

        def rows(at):
            return jnp.where(
                upper, same[at : at + 144, :].astype(F32), other[at : at + 144, :].astype(F32)
            )

        beside = turned_by(rows(288), -4, 1) if second else rows(288)
        return rows(at), jnp.where(kept, beside, 0.0)

    for i in range(1, 9):
        start = residual[i - 1] + jnp.concatenate(supplied(i), axis=1)
        rest[i - 1] = start
        d0[i - 1] = start * inverse[i - 1] * (1.0 / MIDDLE)

    def share(i, d):
        return (
            face_layer[i] * d[i]
            + face_layer[i - 1] * d[i - 2]
            + around(face_row[i - 1], face_col[i - 1], d[i - 1])
        )

    for i in range(2, 8):
        start = rest[i - 1]
        later = start * (1.0 - 1.0 / MIDDLE) + share(i, d0)
        d1[i - 1] = W1 * W0 * d0[i - 1] + (2.0 * W1 / SPREAD) * (later * inverse[i - 1])
        rest[i - 1] = later - (W1 * W0 / MIDDLE) * start - (2.0 * W1 / SPREAD) * later
    for i in range(3, 7):
        last = rest[i - 1] + share(i, d1)
        step = d0[i - 1] + d1[i - 1] * (1.0 + W2 * W1) + (2.0 * W2 / SPREAD) * (last * inverse[i - 1])
        at = (i - 3) * 128
        out[at : at + 128, :] = grids[i, 0:128, :] + step[0:128, 0:128]


def sds(shape, dtype):
    return jax.ShapeDtypeStruct(shape, dtype)


def call(kernel, shape, args, mib=16, scratch=(), far=(), far_out=False):
    vmem, anywhere = pl.BlockSpec(memory_space=pltpu.VMEM), pl.BlockSpec(memory_space=pltpu.HBM)
    return pl.pallas_call(
        kernel,
        out_shape=shape,
        in_specs=[anywhere if i in far else vmem for i in range(len(args))],
        out_specs=jax.tree.map(lambda _: anywhere if far_out else vmem, shape),
        scratch_shapes=list(scratch),
        compiler_params=pltpu.CompilerParams(vmem_limit_bytes=mib * 2**20),
    )(*args)


def pairs(axis):
    up = [(i, i + 1) for i in range(lax.axis_size(axis) - 1)]
    return up, [(b, a) for a, b in up]


def exchange(to_next, to_last, axis):
    up, down = pairs(axis)
    return lax.ppermute(to_next, axis, up), lax.ppermute(to_last, axis, down)


def swap_layers(far, near):
    apart = [(i, i + 1) for i in range(1, lax.axis_size(LAYER) - 1, 2)]
    return (
        lax.ppermute(far, LAYER, apart + [(b, a) for a, b in apart]),
        lax.ppermute(near, "core", [(0, 1), (1, 0)]),
    )


def extended_grids(temp, cond, mass):
    eight, rows, edge = sds((8, 128, 128), BF16), sds((240, 128), BF16), sds((144, 128), BF16)
    own, far, near = call(
        layers_kernel,
        (sds((3, 4, 128, 128), F32), eight, eight),
        (temp, cond, mass),
        scratch=[pltpu.SemaphoreType.DMA((3,))],
        far=range(3),
    )
    far, near = swap_layers(far, near)
    above, below = exchange(*call(rows_kernel, (rows, rows), (own, far, near)), "row")
    wide, to_left, to_right = call(
        gather_kernel, (sds((30, 144, 128), F32), edge, edge), (own, far, near, above, below), mib=24
    )
    return wide, (to_left, to_right), exchange(to_right, to_left, COL)


def operator(wide, from_left, from_right):
    eight = sds((8, 144, 256), F32)
    return call(
        operator_kernel,
        (sds((9, 144, 256), F32), eight, eight, eight, eight),
        (wide, from_left, from_right),
        mib=32,
        scratch=[pltpu.VMEM((30, 144, 256), F32)],
    )


def shards(temp, cond, mass, toggling, baseline, panel, place, holder, tier, warming):
    row64 = pltpu.VMEM((1, 64), I32)
    message, placing, columns = call(
        message_kernel,
        (sds((64, 128), F32), sds((1024, 64), BF16), sds((64, 128), I32)),
        (temp, panel.reshape(1, 64), place, holder, tier),
        mib=60,
        scratch=[
            pltpu.VMEM((4, 128, 128), F32), row64, row64, row64,
            pltpu.VMEM((1, 16), I32), pltpu.SemaphoreType.DMA((5,)),
        ],
        far=range(5),
    )
    messages = lax.all_to_all(message.reshape(64, 1, 128), CUBE, split_axis=0, concat_axis=0, tiled=True)
    messages = messages.reshape(64, 128)
    send = call(
        power_kernel,
        sds((256, 4736), BF16),
        (messages, columns, warming, toggling[0], baseline[0], placing),
        mib=60,
        scratch=[
            pltpu.VMEM((64, 128), F32), pltpu.VMEM((64, 128), I32), pltpu.VMEM((1, 16), F32),
            pltpu.VMEM((64, 4096), BF16), pltpu.VMEM((64, 4096), BF16), pltpu.VMEM((1024, 64), BF16),
            pltpu.VMEM((256, 4736), BF16), pltpu.SemaphoreType.DMA((15,)),
        ],
        far=range(6),
        far_out=True,
    )
    received = lax.all_to_all(send.reshape(16, 16, 4736), PLANE, split_axis=0, concat_axis=0, tiled=True)
    selector = call(selector_kernel, sds((576, 256), BF16), (messages,))
    wide, edges, beside = extended_grids(temp, cond, mass)
    partial = call(
        combine_kernel, sds((64, 4480), F32), (selector, received.reshape(256, 4736), *edges)
    )
    parts = lax.all_to_all(
        partial.astype(jnp.float16).reshape(4, 16, 4480), "zlo", split_axis=0, concat_axis=0, tiled=True
    )
    terms = operator(wide, *beside)
    block, strip = sds((576, 128), F32), sds((432, 128), BF16)
    density, main, side, far, near = call(
        unpack_kernel,
        (sds((512, 128), F32), block, block, strip, strip),
        (jnp.sum(parts.astype(F32), axis=0), *beside),
        scratch=[pltpu.VMEM((512, 128), F32)],
    )
    far, near = swap_layers(far, near)
    eight = pltpu.VMEM((8, 144, 256), F32)
    guess = call(
        sweep_kernel,
        sds((512, 128), F32),
        (main, side, far, near, wide, *terms),
        mib=40,
        scratch=[eight, eight, eight],
    )
    return guess.reshape(4, 128, 128), density.reshape(4, 128, 128)


def solution(mesh):
    fine = Mesh(mesh.devices.reshape(4, 4, 4, 4, 2), ("row", "zlo", "y", "zhi", "core"))
    grid = P(LAYER, "row", COL)
    slot = ("row", "zlo", "y", "zhi", "core")
    return jax.shard_map(
        shards,
        mesh=fine,
        in_specs=(
            grid,
            grid,
            grid,
            P(slot, None, None),
            P(slot, None, None),
            P(slot, None, None),
            P(slot, None),
            P(slot, None),
            P(slot, None),
            P(slot, None),
        ),
        out_specs=(grid, grid),
        check_vma=False,
    )
```

```python
import jax
import jax.numpy as jnp
from jax import lax
from jax.experimental import pallas as pl
from jax.experimental.pallas import tpu as pltpu
from jax.sharding import Mesh
from jax.sharding import PartitionSpec as P

eig_low = 0.1
eig_high = 2.0

LAYER = ("zhi", "core")
COL = ("zlo", "y")
CUBE = ("row", "zlo", "y")
PLANE = ("row", "y")

F32, BF16, I32 = jnp.float32, jnp.bfloat16, jnp.int32


def iota(shape, dim):
    return lax.broadcasted_iota(I32, shape, dim)


def as_column(row):
    n = row.shape[1]
    return jnp.sum(jnp.where(iota((n, n), 0) == iota((n, n), 1), row, 0), axis=1, keepdims=True)


def slot_rows(panel, place, holder, tier):
    layer = jnp.sum(jnp.where(iota((16, 64), 0) == holder, as_column(tier), 0), axis=0, keepdims=True)
    pos = layer * 4 + place
    ident = ((panel >> 2) & 3) * 16 + pos
    column = (panel >> 4) * 4 + (panel & 3)
    same = (as_column(column) == column) & (iota((64, 64), 0) < iota((64, 64), 1))
    rank = jnp.sum(same.astype(I32), axis=0, keepdims=True)
    return pos, ident, column * 16 + rank


def place_slots(panel, pos, dest, holder, placing, columns):
    x, y, rank = panel >> 4, panel & 3, dest & 15
    lower, right = (pos >> 1) & 1, pos & 1
    next_x = x + lower * 2 - 1
    next_y = (y + right * 2 + 3) & 3
    inside = (next_x >= 0) & (next_x <= 3)
    targets = (
        dest,
        jnp.where(inside, (next_x * 4 + y) * 16 + rank, -1),
        (x * 4 + next_y) * 16 + rank,
        jnp.where(inside, (next_x * 4 + next_y) * 16 + rank, -1),
    )
    for k, target in enumerate(targets):
        placing[pl.ds(k * 256, 256), :] = jnp.where(iota((256, 64), 0) == target, 1.0, 0.0).astype(BF16)
    lane = iota((64, 128), 1)
    columns[...] = jnp.where(
        lane == 0, as_column(panel), jnp.where(lane == 1, as_column(pos), as_column(holder))
    )


def message_kernel(temp, panel, place, holder, tier, out, placing, columns, temp_v, panel_v, place_v, holder_v, tier_v, sems):
    pairs = [(panel, panel_v), (place, place_v), (holder, holder_v), (tier, tier_v), (temp, temp_v)]
    copies = [pltpu.make_async_copy(a, b, sems.at[i]) for i, (a, b) in enumerate(pairs)]
    for copy in copies:
        copy.start()
    for copy in copies[:4]:
        copy.wait()
    panel_row, holder_row = panel_v[...], holder_v[...]
    pos, ident, dest = slot_rows(panel_row, place_v[...], holder_row, tier_v[...])
    place_slots(panel_row, pos, dest, holder_row, placing, columns)
    code = (dest * 64 + ident).astype(F32)
    copies[4].wait()
    sums = jnp.sum(temp_v[...].reshape(8, 64, 128), axis=1)
    lane = iota((8, 128), 1)
    first = jnp.sum(jnp.where(lane < 64, sums, 0.0), axis=1, keepdims=True)
    second = jnp.sum(jnp.where(lane < 64, 0.0, sums), axis=1, keepdims=True)
    at = iota((8, 128), 0) * 2
    means = jnp.where(lane == at, first, jnp.where(lane == at + 1, second, 0.0))
    means = jnp.sum(means, axis=0, keepdims=True) * (1.0 / 4096.0)
    row = jnp.where(iota((1, 128), 1) < 64, means, jnp.concatenate([code, code], axis=1))
    out[...] = jnp.broadcast_to(row, (64, 128))


def power_kernel(
    far_messages, far_columns, far_warming, far_toggling, far_baseline, far_placing, out,
    messages, columns, warming, toggling, baseline, placing, sent, sems,
):
    pairs = [
        (far_messages, messages),
        (far_columns, columns),
        (far_warming, warming),
        (far_toggling, toggling),
        (far_baseline, baseline),
        (far_placing, placing),
    ]
    loads = [pltpu.make_async_copy(a, b, sems.at[9 + i]) for i, (a, b) in enumerate(pairs)]
    for load in loads:
        load.start()
    loads[0].wait()
    loads[1].wait()
    tile, pos, holder = (columns[:, k : k + 1] for k in range(3))
    lower, right = (pos >> 1) & 1, pos & 1
    pick = jnp.where(iota((64, 64), 1) == tile, 1.0, 0.0)
    means = jnp.dot(pick, messages[...], precision=lax.Precision.HIGHEST, preferred_element_type=F32)
    lane = iota((64, 128), 1)
    slot_mean = jnp.sum(jnp.where(lane == pos, means, 0.0), axis=1, keepdims=True)
    member = iota((64, 16), 1) == holder
    total = jnp.sum(jnp.where(member, slot_mean, 0.0), axis=0, keepdims=True)
    count = jnp.sum(jnp.where(member, 1.0, 0.0), axis=0, keepdims=True)
    loads[2].wait()
    leak = jnp.exp(warming[...] * (total / count))
    factor = jnp.sum(jnp.where(member, leak, 0.0), axis=1, keepdims=True)

    def place(kind, values):
        at = placing[kind * 256 : (kind + 1) * 256, :]
        return jnp.dot(at, values.astype(BF16), preferred_element_type=F32).astype(BF16)

    copies = []

    def send(start, width):
        at = pl.ds(start, width)
        copy = pltpu.make_async_copy(sent.at[:, at], out.at[:, at], sems.at[len(copies)])
        copy.start()
        copies.append(copy)

    for load in loads[3:]:
        load.wait()
    edge = ((lane & 63) >> 1) == right * 31
    sides = jnp.zeros((64, 128), F32)
    width = 512
    for k in range(8):
        at = pl.ds(k * width, width)
        power = (toggling[:, at].astype(F32) + factor * baseline[:, at].astype(F32)).astype(BF16)
        sent[:, at] = place(0, power)
        send(k * width, width)
        power = power.astype(F32)
        for t in range(4):
            piece = power[:, t * 128 : (t + 1) * 128]
            shift = 2 * (4 * k + t)
            kept = jnp.where(edge, piece, 0.0)
            sides = sides + (pltpu.roll(kept, shift, 1) if shift else kept)
            if k == 0 and t == 0:
                top = piece
    rows = jnp.where(lower == 0, top, piece)
    sides = jnp.where(right == 0, sides, pltpu.roll(sides, 66, 1))
    corner = jnp.sum(jnp.where(lane == lower * 64 + right * 63, rows, 0.0), axis=1, keepdims=True)
    quarter = (1 - lower) * 2 + 1 - right
    both = jnp.concatenate([jnp.where(lower == 1, rows, 0.0), jnp.where(lower == 0, rows, 0.0)], axis=1)
    sent[:, 4096:4352] = place(1, both)
    both = jnp.concatenate([jnp.where(right == 1, sides, 0.0), jnp.where(right == 0, sides, 0.0)], axis=1)
    sent[:, 4352:4608] = place(2, both)
    sent[:, 4608:4736] = place(3, jnp.where(lane == quarter, corner, 0.0))
    send(4096, 640)
    for copy in copies:
        copy.wait()


def selector_kernel(messages, out):
    x, y = lax.axis_index("row"), lax.axis_index("y")
    plane = lax.axis_index("zlo")
    code = jnp.concatenate([messages[pl.ds(r * 16 + plane * 4, 4), :] for r in range(4)], axis=0)
    code = jnp.where(iota((16, 128), 1) < 64, -1.0, code).astype(I32)
    dest, ident = code >> 6, code & 63
    lane = iota((16, 256), 1)

    def idents(dx, dy):
        base = ((x + dx) * 4 + ((y + dy + 4) & 3)) * 16
        ids = jnp.zeros((16, 256), I32)
        for r in range(16):
            hit = jnp.sum(jnp.where(dest == base + r, ident + 1, 0), axis=1, keepdims=True)
            ids = jnp.where((lane & 15) == r, hit, ids)
        ids = jnp.sum(jnp.where((lane >> 4) == iota((16, 256), 0), ids, 0), axis=0, keepdims=True) - 1
        turn = jnp.where(y == 0, 1, 0) if dy < 0 else jnp.where(y == 3, -1, 0) if dy > 0 else 0
        return ids, (ids >> 4) + turn, (ids >> 2) & 3, (ids >> 1) & 1, ids & 1

    def put(k, ids, target):
        out[pl.ds(k * 64, 64), :] = jnp.where(
            (iota((64, 256), 0) == target) & (ids >= 0), 1.0, 0.0
        ).astype(BF16)

    ids, *_ = idents(0, 0)
    put(0, ids, ids)
    for k, dx in enumerate((-1, 1)):
        ids, z, layer, _, pc = idents(dx, 0)
        put(1 + k, ids, z * 16 + k * 8 + layer * 2 + pc)
    for k, dy in enumerate((-1, 1)):
        ids, z, layer, pr, _ = idents(0, dy)
        put(3 + k, ids, z * 16 + k * 8 + layer * 2 + pr)
    for k in range(4):
        ids, z, layer, _, _ = idents((k >> 1) * 2 - 1, (k & 1) * 2 - 1)
        put(5 + k, ids, z * 16 + layer)


def combine_kernel(selector, received, _outer, _inner, out):
    def add(k, start, width):
        return jnp.dot(
            selector[k * 64 : (k + 1) * 64, :],
            received[:, start : start + width],
            preferred_element_type=F32,
        )

    for k in range(8):
        out[:, k * 512 : (k + 1) * 512] = add(0, k * 512, 512)
    out[:, 4096:4224] = add(1, 4096, 128) + add(2, 4224, 128)
    out[:, 4224:4352] = add(3, 4352, 128) + add(4, 4480, 128)
    lane = iota((64, 128), 1)
    corners = jnp.zeros((64, 128), F32)
    for k in range(4):
        corners = jnp.where(lane == k, add(5 + k, 4608, 128), corners)
    out[:, 4352:4480] = corners


def unpack_kernel(whole, _outer, _inner, density, main, side, far, near, turned):
    for k in range(32):
        turned[k * 16 : (k + 1) * 16, :] = whole[:, k * 128 : (k + 1) * 128]
    low = iota((32, 128), 1) < 64
    lane = iota((64, 128), 1)
    low_row = iota((1, 128), 1) < 64
    lane16, row16 = iota((16, 128), 1), iota((16, 128), 0)
    rows, columns, corners = whole[:, 4096:4224], whole[:, 4224:4352], whole[:, 4352:4480]
    cell = iota((64, 128), 0)
    turn = []
    for c in range(2):
        pick = jnp.where(lane == (cell & 1) * 64 + (cell - (cell & 1)) + c, 1.0, 0.0)
        turn.append(
            lax.dot_general(
                pick, columns, (((1,), (1,)), ((), ())),
                precision=lax.Precision.HIGHEST, preferred_element_type=F32,
            )
        )
    for layer in range(4):
        base = layer * 144
        for r in range(2):
            left = turned[pl.ds(layer * 4 + r * 2, 32, stride=16), :]
            right = turned[pl.ds(layer * 4 + r * 2 + 1, 32, stride=16), :]
            at = base + r * 64
            main[pl.ds(at, 32, stride=2), :] = jnp.where(low, left, pltpu.roll(right, 64, 1))
            main[pl.ds(at + 1, 32, stride=2), :] = jnp.where(low, pltpu.roll(left, 64, 1), right)
            k = layer * 2 + r
            strip = jnp.where(lane == 0, turn[0][:, 8 + k : 9 + k], 0.0)
            strip = jnp.where(lane == 1, turn[1][:, 8 + k : 9 + k], strip)
            strip = jnp.where(lane == 126, turn[0][:, k : k + 1], strip)
            side[at : at + 64, :] = jnp.where(lane == 127, turn[1][:, k : k + 1], strip)
        block = jnp.zeros((16, 128), F32)
        for kind, first_row in ((0, 14), (1, 0)):
            k = kind * 8 + layer * 2
            a, b = rows[k : k + 1, :], rows[k + 1 : k + 2, :]
            first = jnp.where(low_row, a, pltpu.roll(b, 64, 1))
            second = jnp.where(low_row, pltpu.roll(a, 64, 1), b)
            block = jnp.where(row16 == first_row, first, block)
            block = jnp.where(row16 == first_row + 1, second, block)
        main[base + 128 : base + 144, :] = block
        block = jnp.zeros((16, 128), F32)
        for k, (r, at_lane) in enumerate(((15, 127), (15, 0), (0, 127), (0, 0))):
            value = corners[layer : layer + 1, k : k + 1]
            block = jnp.where((row16 == r) & (lane16 == at_lane), value, block)
        side[base + 128 : base + 144, :] = block
        density[layer * 128 : (layer + 1) * 128, :] = main[base : base + 128, :]
    upper = jnp.where(lax.axis_index("core") == 1, 288, 0)
    for out, first in ((far, upper), (near, 288 - upper)):
        first = pl.multiple_of(first, 144)
        out[0:288, :] = main[pl.ds(first, 288), :].astype(BF16)
        second = side[pl.ds(first + 144, 144), :]
        out[288:432, :] = (side[pl.ds(first, 144), :] + pltpu.roll(second, 4, 1)).astype(BF16)


def depth(a):
    return 3 if a < 2 else 2


def beyond(a, layer):
    k = layer - 3 + depth(a) if layer < 3 else layer - 7
    return 3 * a + k if 0 <= k < depth(a) else None


def from_layer(far, near, a, layer, at):
    k = beyond(a, layer)
    if k is None:
        return None
    same, other = (near, far) if layer < 3 else (far, near)
    upper = lax.axis_index("core") == 1
    return jnp.where(upper, same[k, at, :].astype(F32), other[k, at, :].astype(F32))


def layers_kernel(temp, cond, mass, own, far, near, sems):
    upper = lax.axis_index("core") == 1
    copies = [pltpu.make_async_copy(a, own.at[i], sems.at[i]) for i, a in enumerate((temp, cond, mass))]
    for copy in copies:
        copy.start()
    for a, copy in enumerate(copies):
        copy.wait()
        for k in range(depth(a)):
            last, first = own[a, 4 - depth(a) + k], own[a, k]
            far[3 * a + k] = jnp.where(upper, last, first).astype(BF16)
            near[3 * a + k] = jnp.where(upper, first, last).astype(BF16)


def rows_kernel(own, far, near, outer, inner):
    lasts, firsts = [], []
    for a in range(3):
        for layer in range(10):
            if 3 <= layer < 7:
                lasts.append(own[a, layer - 3, 120:128, :])
                firsts.append(own[a, layer - 3, 0:8, :])
            else:
                zeros = jnp.zeros((8, 128), F32)
                ends = from_layer(far, near, a, layer, slice(112, 128))
                lasts.append(zeros if ends is None else ends[8:16])
                ends = from_layer(far, near, a, layer, slice(0, 16))
                firsts.append(zeros if ends is None else ends[0:8])
    last, first = jnp.concatenate(lasts, axis=0), jnp.concatenate(firsts, axis=0)
    odd = is_odd("row")
    outer[...] = jnp.where(odd, last, first).astype(BF16)
    inner[...] = jnp.where(odd, first, last).astype(BF16)


def gather_kernel(own, far, near, outer, inner, out, to_outer, to_inner):
    over, under = sides(is_odd("row"), outer, inner)
    lane = iota((144, 128), 1)
    left, right = jnp.zeros((144, 128), F32), jnp.zeros((144, 128), F32)
    for a in range(3):
        for layer in range(10):
            i = a * 10 + layer
            if 3 <= layer < 7:
                source = own[a, layer - 3]
            else:
                source = from_layer(far, near, a, layer, slice(0, 128))
                source = jnp.zeros((128, 128), F32) if source is None else source
            piece = jnp.concatenate([source, under[8 * i : 8 * i + 8], over[8 * i : 8 * i + 8]], axis=0)
            out[i] = piece
            base = a * 40 + layer * 4
            here = (lane >= base) & (lane < base + 3)
            left = jnp.where(here, pltpu.roll(piece, base, 1) if base else piece, left)
            right = jnp.where(here, pltpu.roll(piece, base + 3, 1), right)
    odd = is_odd("y")
    to_outer[...] = jnp.where(odd, right, left).astype(BF16)
    to_inner[...] = jnp.where(odd, left, right).astype(BF16)


def turned_by(x, shift, axis):
    return pltpu.roll(x, shift % x.shape[axis], axis)


def around(face_row, face_col, v):
    return (
        face_row * turned_by(v, -1, 0)
        + turned_by(face_row * v, 1, 0)
        + face_col * turned_by(v, -1, 1)
        + turned_by(face_col * v, 1, 1)
    )


def operator_kernel(grids, outer, inner, face_layer, face_row, face_col, inverse, residual, wide):
    left, right = sides(is_odd("y"), outer, inner)
    lane = iota((144, 128), 1)
    for a in range(3):
        for layer in range(10):
            i, base = a * 10 + layer, a * 40 + layer * 4
            high = turned_by(right, -base, 1) if base else right
            side = jnp.where(lane < 3, high, jnp.where(lane >= 125, turned_by(left, 125 - base, 1), 0.0))
            wide[i, :, 0:128] = grids[i]
            wide[i, :, 128:256] = side
    for layer in range(9):
        face_layer[layer] = 0.5 * (wide[10 + layer] + wide[11 + layer])
    for layer in range(1, 9):
        temp, cond, mass = (wide[a * 10 + layer] for a in range(3))
        rows = 0.5 * (cond + turned_by(cond, -1, 0))
        cols = 0.5 * (cond + turned_by(cond, -1, 1))
        face_row[layer - 1] = rows
        face_col[layer - 1] = cols
        after, before = face_layer[layer], face_layer[layer - 1]
        diagonal = mass + after + before + rows + turned_by(rows, 1, 0) + cols + turned_by(cols, 1, 1)
        share = after * wide[layer + 1] + before * wide[layer - 1] + around(rows, cols, temp)
        residual[layer - 1] = mass * temp + (share - diagonal * temp)
        inverse[layer - 1] = jnp.where(mass > 0.0, 1.0 / diagonal, 0.0)


MIDDLE = (eig_low + eig_high) / 2.0
SPREAD = (eig_high - eig_low) / 2.0
W0 = SPREAD / MIDDLE
W1 = 1.0 / (2.0 * MIDDLE / SPREAD - W0)
W2 = 1.0 / (2.0 * MIDDLE / SPREAD - W1)


def sweep_kernel(main, side, far, near, grids, face_layer, face_row, face_col, inverse, residual, out, d0, d1, rest):
    lane = iota((144, 128), 1)
    kept = (lane < 2) | (lane >= 126)
    upper = lax.axis_index("core") == 1

    def supplied(i):
        if 3 <= i <= 6:
            at = (i - 3) * 144
            return main[at : at + 144, :], side[at : at + 144, :]
        second = i in (2, 8)
        at = 144 if second else 0
        same, other = (near, far) if i < 3 else (far, near)

        def rows(at):
            return jnp.where(
                upper, same[at : at + 144, :].astype(F32), other[at : at + 144, :].astype(F32)
            )

        beside = turned_by(rows(288), -4, 1) if second else rows(288)
        return rows(at), jnp.where(kept, beside, 0.0)

    for i in range(1, 9):
        start = residual[i - 1] + jnp.concatenate(supplied(i), axis=1)
        rest[i - 1] = start
        d0[i - 1] = start * inverse[i - 1] * (1.0 / MIDDLE)

    def share(i, d):
        return (
            face_layer[i] * d[i]
            + face_layer[i - 1] * d[i - 2]
            + around(face_row[i - 1], face_col[i - 1], d[i - 1])
        )

    for i in range(2, 8):
        start = rest[i - 1]
        later = start * (1.0 - 1.0 / MIDDLE) + share(i, d0)
        d1[i - 1] = W1 * W0 * d0[i - 1] + (2.0 * W1 / SPREAD) * (later * inverse[i - 1])
        rest[i - 1] = later - (W1 * W0 / MIDDLE) * start - (2.0 * W1 / SPREAD) * later
    for i in range(3, 7):
        last = rest[i - 1] + share(i, d1)
        step = d0[i - 1] + d1[i - 1] * (1.0 + W2 * W1) + (2.0 * W2 / SPREAD) * (last * inverse[i - 1])
        at = (i - 3) * 128
        out[at : at + 128, :] = grids[i, 0:128, :] + step[0:128, 0:128]


def sds(shape, dtype):
    return jax.ShapeDtypeStruct(shape, dtype)


def call(kernel, shape, args, mib=16, scratch=(), far=(), far_out=False):
    vmem, anywhere = pl.BlockSpec(memory_space=pltpu.VMEM), pl.BlockSpec(memory_space=pltpu.HBM)
    return pl.pallas_call(
        kernel,
        out_shape=shape,
        in_specs=[anywhere if i in far else vmem for i in range(len(args))],
        out_specs=jax.tree.map(lambda _: anywhere if far_out else vmem, shape),
        scratch_shapes=list(scratch),
        compiler_params=pltpu.CompilerParams(vmem_limit_bytes=mib * 2**20),
    )(*args)


def swap_sides(to_outer, to_inner, axis):
    count = lax.axis_size(axis)

    def swapped(data, first):
        apart = [(i, i + 1) for i in range(first, count - 1, 2)]
        return lax.ppermute(data, axis, apart + [(b, a) for a, b in apart])

    return swapped(to_outer, 1), swapped(to_inner, 0)


def is_odd(axis):
    return (lax.axis_index(axis) & 1) == 1


def sides(odd, outer, inner):
    outer, inner = outer[...].astype(F32), inner[...].astype(F32)
    return jnp.where(odd, inner, outer), jnp.where(odd, outer, inner)


def swap_layers(far, near):
    apart = [(i, i + 1) for i in range(1, lax.axis_size(LAYER) - 1, 2)]
    return (
        lax.ppermute(far, LAYER, apart + [(b, a) for a, b in apart]),
        lax.ppermute(near, "core", [(0, 1), (1, 0)]),
    )


def extended_grids(temp, cond, mass):
    eight, rows, edge = sds((8, 128, 128), BF16), sds((240, 128), BF16), sds((144, 128), BF16)
    own, far, near = call(
        layers_kernel,
        (sds((3, 4, 128, 128), F32), eight, eight),
        (temp, cond, mass),
        scratch=[pltpu.SemaphoreType.DMA((3,))],
        far=range(3),
    )
    far, near = swap_layers(far, near)
    beside = swap_sides(*call(rows_kernel, (rows, rows), (own, far, near)), "row")
    wide, *edges = call(
        gather_kernel, (sds((30, 144, 128), F32), edge, edge), (own, far, near, *beside), mib=24
    )
    return wide, edges, swap_sides(*edges, COL)


def operator(wide, outer, inner):
    eight = sds((8, 144, 256), F32)
    return call(
        operator_kernel,
        (sds((9, 144, 256), F32), eight, eight, eight, eight),
        (wide, outer, inner),
        mib=32,
        scratch=[pltpu.VMEM((30, 144, 256), F32)],
    )


def shards(temp, cond, mass, toggling, baseline, panel, place, holder, tier, warming):
    row64 = pltpu.VMEM((1, 64), I32)
    message, placing, columns = call(
        message_kernel,
        (sds((64, 128), F32), sds((1024, 64), BF16), sds((64, 128), I32)),
        (temp, panel.reshape(1, 64), place, holder, tier),
        mib=60,
        scratch=[
            pltpu.VMEM((4, 128, 128), F32), row64, row64, row64,
            pltpu.VMEM((1, 16), I32), pltpu.SemaphoreType.DMA((5,)),
        ],
        far=range(5),
    )
    messages = lax.all_to_all(message.reshape(64, 1, 128), CUBE, split_axis=0, concat_axis=0, tiled=True)
    messages = messages.reshape(64, 128)
    send = call(
        power_kernel,
        sds((256, 4736), BF16),
        (messages, columns, warming, toggling[0], baseline[0], placing),
        mib=60,
        scratch=[
            pltpu.VMEM((64, 128), F32), pltpu.VMEM((64, 128), I32), pltpu.VMEM((1, 16), F32),
            pltpu.VMEM((64, 4096), BF16), pltpu.VMEM((64, 4096), BF16), pltpu.VMEM((1024, 64), BF16),
            pltpu.VMEM((256, 4736), BF16), pltpu.SemaphoreType.DMA((15,)),
        ],
        far=range(6),
        far_out=True,
    )
    received = lax.all_to_all(send.reshape(16, 16, 4736), PLANE, split_axis=0, concat_axis=0, tiled=True)
    selector = call(selector_kernel, sds((576, 256), BF16), (messages,))
    wide, edges, beside = extended_grids(temp, cond, mass)
    partial = call(
        combine_kernel, sds((64, 4480), F32), (selector, received.reshape(256, 4736), *edges)
    )
    parts = lax.all_to_all(
        partial.astype(jnp.float16).reshape(4, 16, 4480), "zlo", split_axis=0, concat_axis=0, tiled=True
    )
    terms = operator(wide, *beside)
    block, strip = sds((576, 128), F32), sds((432, 128), BF16)
    density, main, side, far, near = call(
        unpack_kernel,
        (sds((512, 128), F32), block, block, strip, strip),
        (jnp.sum(parts.astype(F32), axis=0), *beside),
        scratch=[pltpu.VMEM((512, 128), F32)],
    )
    far, near = swap_layers(far, near)
    eight = pltpu.VMEM((8, 144, 256), F32)
    guess = call(
        sweep_kernel,
        sds((512, 128), F32),
        (main, side, far, near, wide, *terms),
        mib=40,
        scratch=[eight, eight, eight],
    )
    return guess.reshape(4, 128, 128), density.reshape(4, 128, 128)


def solution(mesh):
    fine = Mesh(mesh.devices.reshape(4, 4, 4, 4, 2), ("row", "zlo", "y", "zhi", "core"))
    grid = P(LAYER, "row", COL)
    slot = ("row", "zlo", "y", "zhi", "core")
    return jax.shard_map(
        shards,
        mesh=fine,
        in_specs=(
            grid,
            grid,
            grid,
            P(slot, None, None),
            P(slot, None, None),
            P(slot, None, None),
            P(slot, None),
            P(slot, None),
            P(slot, None),
            P(slot, None),
        ),
        out_specs=(grid, grid),
        check_vma=False,
    )
```

```python
import jax
import jax.numpy as jnp
from jax import lax
from jax.experimental import pallas as pl
from jax.experimental.pallas import tpu as pltpu
from jax.sharding import Mesh
from jax.sharding import PartitionSpec as P

eig_low = 0.1
eig_high = 2.0

LAYER = ("zhi", "core")
COL = ("zlo", "y")
CUBE = ("row", "zlo", "y")
PLANE = ("row", "y")

F32, BF16, I32 = jnp.float32, jnp.bfloat16, jnp.int32


def iota(shape, dim):
    return lax.broadcasted_iota(I32, shape, dim)


def as_column(row):
    n = row.shape[1]
    return jnp.sum(jnp.where(iota((n, n), 0) == iota((n, n), 1), row, 0), axis=1, keepdims=True)


def slot_rows(panel, place, holder, tier):
    layer = jnp.sum(jnp.where(iota((16, 64), 0) == holder, as_column(tier), 0), axis=0, keepdims=True)
    pos = layer * 4 + place
    ident = ((panel >> 2) & 3) * 16 + pos
    column = (panel >> 4) * 4 + (panel & 3)
    same = (as_column(column) == column) & (iota((64, 64), 0) < iota((64, 64), 1))
    rank = jnp.sum(same.astype(I32), axis=0, keepdims=True)
    return pos, ident, column * 16 + rank


def place_slots(panel, pos, dest, holder, placing, columns):
    x, y, rank = panel >> 4, panel & 3, dest & 15
    lower, right = (pos >> 1) & 1, pos & 1
    next_x = x + lower * 2 - 1
    next_y = (y + right * 2 + 3) & 3
    inside = (next_x >= 0) & (next_x <= 3)
    targets = (
        dest,
        jnp.where(inside, (next_x * 4 + y) * 16 + rank, -1),
        (x * 4 + next_y) * 16 + rank,
        jnp.where(inside, (next_x * 4 + next_y) * 16 + rank, -1),
    )
    for k, target in enumerate(targets):
        placing[pl.ds(k * 256, 256), :] = jnp.where(iota((256, 64), 0) == target, 1.0, 0.0).astype(BF16)
    lane = iota((64, 128), 1)
    columns[...] = jnp.where(
        lane == 0, as_column(panel), jnp.where(lane == 1, as_column(pos), as_column(holder))
    )


def message_kernel(temp, panel, place, holder, tier, out, placing, columns, temp_v, panel_v, place_v, holder_v, tier_v, sems):
    pairs = [(panel, panel_v), (place, place_v), (holder, holder_v), (tier, tier_v), (temp, temp_v)]
    copies = [pltpu.make_async_copy(a, b, sems.at[i]) for i, (a, b) in enumerate(pairs)]
    for copy in copies:
        copy.start()
    for copy in copies[:4]:
        copy.wait()
    panel_row, holder_row = panel_v[...], holder_v[...]
    pos, ident, dest = slot_rows(panel_row, place_v[...], holder_row, tier_v[...])
    place_slots(panel_row, pos, dest, holder_row, placing, columns)
    code = (dest * 64 + ident).astype(F32)
    copies[4].wait()
    sums = jnp.sum(temp_v[...].reshape(8, 64, 128), axis=1)
    lane = iota((8, 128), 1)
    first = jnp.sum(jnp.where(lane < 64, sums, 0.0), axis=1, keepdims=True)
    second = jnp.sum(jnp.where(lane < 64, 0.0, sums), axis=1, keepdims=True)
    at = iota((8, 128), 0) * 2
    means = jnp.where(lane == at, first, jnp.where(lane == at + 1, second, 0.0))
    means = jnp.sum(means, axis=0, keepdims=True) * (1.0 / 4096.0)
    row = jnp.where(iota((1, 128), 1) < 64, means, jnp.concatenate([code, code], axis=1))
    out[...] = jnp.broadcast_to(row, (64, 128))


def power_kernel(
    far_messages, far_columns, far_warming, far_toggling, far_baseline, far_placing, out,
    messages, columns, warming, toggling, baseline, placing, sent, sems,
):
    pairs = [
        (far_messages, messages),
        (far_columns, columns),
        (far_warming, warming),
        (far_toggling, toggling),
        (far_baseline, baseline),
        (far_placing, placing),
    ]
    loads = [pltpu.make_async_copy(a, b, sems.at[9 + i]) for i, (a, b) in enumerate(pairs)]
    for load in loads:
        load.start()
    loads[0].wait()
    loads[1].wait()
    tile, pos, holder = (columns[:, k : k + 1] for k in range(3))
    lower, right = (pos >> 1) & 1, pos & 1
    pick = jnp.where(iota((64, 64), 1) == tile, 1.0, 0.0)
    means = jnp.dot(pick, messages[...], precision=lax.Precision.HIGHEST, preferred_element_type=F32)
    lane = iota((64, 128), 1)
    slot_mean = jnp.sum(jnp.where(lane == pos, means, 0.0), axis=1, keepdims=True)
    member = iota((64, 16), 1) == holder
    total = jnp.sum(jnp.where(member, slot_mean, 0.0), axis=0, keepdims=True)
    count = jnp.sum(jnp.where(member, 1.0, 0.0), axis=0, keepdims=True)
    loads[2].wait()
    leak = jnp.exp(warming[...] * (total / count))
    factor = jnp.sum(jnp.where(member, leak, 0.0), axis=1, keepdims=True)

    def place(kind, values):
        at = placing[kind * 256 : (kind + 1) * 256, :]
        return jnp.dot(at, values.astype(BF16), preferred_element_type=F32).astype(BF16)

    copies = []

    def send(start, width):
        at = pl.ds(start, width)
        copy = pltpu.make_async_copy(sent.at[:, at], out.at[:, at], sems.at[len(copies)])
        copy.start()
        copies.append(copy)

    for load in loads[3:]:
        load.wait()
    edge = ((lane & 63) >> 1) == right * 31
    sides = jnp.zeros((64, 128), F32)
    width = 512
    for k in range(8):
        at = pl.ds(k * width, width)
        power = (toggling[:, at].astype(F32) + factor * baseline[:, at].astype(F32)).astype(BF16)
        sent[:, at] = place(0, power)
        send(k * width, width)
        power = power.astype(F32)
        for t in range(4):
            piece = power[:, t * 128 : (t + 1) * 128]
            shift = 2 * (4 * k + t)
            kept = jnp.where(edge, piece, 0.0)
            sides = sides + (pltpu.roll(kept, shift, 1) if shift else kept)
            if k == 0 and t == 0:
                top = piece
    rows = jnp.where(lower == 0, top, piece)
    sides = jnp.where(right == 0, sides, pltpu.roll(sides, 66, 1))
    corner = jnp.sum(jnp.where(lane == lower * 64 + right * 63, rows, 0.0), axis=1, keepdims=True)
    quarter = (1 - lower) * 2 + 1 - right
    both = jnp.concatenate([jnp.where(lower == 1, rows, 0.0), jnp.where(lower == 0, rows, 0.0)], axis=1)
    sent[:, 4096:4352] = place(1, both)
    both = jnp.concatenate([jnp.where(right == 1, sides, 0.0), jnp.where(right == 0, sides, 0.0)], axis=1)
    sent[:, 4352:4608] = place(2, both)
    sent[:, 4608:4736] = place(3, jnp.where(lane == quarter, corner, 0.0))
    send(4096, 640)
    for copy in copies:
        copy.wait()


def selector_kernel(messages, out):
    x, y = lax.axis_index("row"), lax.axis_index("y")
    plane = lax.axis_index("zlo")
    code = jnp.concatenate([messages[pl.ds(r * 16 + plane * 4, 4), :] for r in range(4)], axis=0)
    code = jnp.where(iota((16, 128), 1) < 64, -1.0, code).astype(I32)
    dest, ident = code >> 6, code & 63
    lane = iota((16, 256), 1)

    def idents(dx, dy):
        base = ((x + dx) * 4 + ((y + dy + 4) & 3)) * 16
        ids = jnp.zeros((16, 256), I32)
        for r in range(16):
            hit = jnp.sum(jnp.where(dest == base + r, ident + 1, 0), axis=1, keepdims=True)
            ids = jnp.where((lane & 15) == r, hit, ids)
        ids = jnp.sum(jnp.where((lane >> 4) == iota((16, 256), 0), ids, 0), axis=0, keepdims=True) - 1
        turn = jnp.where(y == 0, 1, 0) if dy < 0 else jnp.where(y == 3, -1, 0) if dy > 0 else 0
        return ids, (ids >> 4) + turn, (ids >> 2) & 3, (ids >> 1) & 1, ids & 1

    def put(k, ids, target):
        out[pl.ds(k * 64, 64), :] = jnp.where(
            (iota((64, 256), 0) == target) & (ids >= 0), 1.0, 0.0
        ).astype(BF16)

    ids, *_ = idents(0, 0)
    put(0, ids, ids)
    for k, dx in enumerate((-1, 1)):
        ids, z, layer, _, pc = idents(dx, 0)
        put(1 + k, ids, z * 16 + k * 8 + layer * 2 + pc)
    for k, dy in enumerate((-1, 1)):
        ids, z, layer, pr, _ = idents(0, dy)
        put(3 + k, ids, z * 16 + k * 8 + layer * 2 + pr)
    for k in range(4):
        ids, z, layer, _, _ = idents((k >> 1) * 2 - 1, (k & 1) * 2 - 1)
        put(5 + k, ids, z * 16 + layer)


def combine_kernel(selector, received, _outer, _inner, out):
    def add(k, start, width):
        return jnp.dot(
            selector[k * 64 : (k + 1) * 64, :],
            received[:, start : start + width],
            preferred_element_type=F32,
        )

    for k in range(8):
        out[:, k * 512 : (k + 1) * 512] = add(0, k * 512, 512)
    out[:, 4096:4224] = add(1, 4096, 128) + add(2, 4224, 128)
    out[:, 4224:4352] = add(3, 4352, 128) + add(4, 4480, 128)
    lane = iota((64, 128), 1)
    corners = jnp.zeros((64, 128), F32)
    for k in range(4):
        corners = jnp.where(lane == k, add(5 + k, 4608, 128), corners)
    out[:, 4352:4480] = corners


def unpack_kernel(whole, _outer, _inner, density, main, side, far, near, turned):
    for k in range(32):
        turned[k * 16 : (k + 1) * 16, :] = whole[:, k * 128 : (k + 1) * 128]
    low = iota((32, 128), 1) < 64
    lane = iota((64, 128), 1)
    low_row = iota((1, 128), 1) < 64
    lane16, row16 = iota((16, 128), 1), iota((16, 128), 0)
    rows, columns, corners = whole[:, 4096:4224], whole[:, 4224:4352], whole[:, 4352:4480]
    cell = iota((64, 128), 0)
    turn = []
    for c in range(2):
        pick = jnp.where(lane == (cell & 1) * 64 + (cell - (cell & 1)) + c, 1.0, 0.0)
        turn.append(
            lax.dot_general(
                pick, columns, (((1,), (1,)), ((), ())),
                precision=lax.Precision.HIGHEST, preferred_element_type=F32,
            )
        )
    for layer in range(4):
        base = layer * 144
        for r in range(2):
            left = turned[pl.ds(layer * 4 + r * 2, 32, stride=16), :]
            right = turned[pl.ds(layer * 4 + r * 2 + 1, 32, stride=16), :]
            at = base + r * 64
            main[pl.ds(at, 32, stride=2), :] = jnp.where(low, left, pltpu.roll(right, 64, 1))
            main[pl.ds(at + 1, 32, stride=2), :] = jnp.where(low, pltpu.roll(left, 64, 1), right)
            k = layer * 2 + r
            strip = jnp.where(lane == 0, turn[0][:, 8 + k : 9 + k], 0.0)
            strip = jnp.where(lane == 1, turn[1][:, 8 + k : 9 + k], strip)
            strip = jnp.where(lane == 126, turn[0][:, k : k + 1], strip)
            side[at : at + 64, :] = jnp.where(lane == 127, turn[1][:, k : k + 1], strip)
        block = jnp.zeros((16, 128), F32)
        for kind, first_row in ((0, 14), (1, 0)):
            k = kind * 8 + layer * 2
            a, b = rows[k : k + 1, :], rows[k + 1 : k + 2, :]
            first = jnp.where(low_row, a, pltpu.roll(b, 64, 1))
            second = jnp.where(low_row, pltpu.roll(a, 64, 1), b)
            block = jnp.where(row16 == first_row, first, block)
            block = jnp.where(row16 == first_row + 1, second, block)
        main[base + 128 : base + 144, :] = block
        block = jnp.zeros((16, 128), F32)
        for k, (r, at_lane) in enumerate(((15, 127), (15, 0), (0, 127), (0, 0))):
            value = corners[layer : layer + 1, k : k + 1]
            block = jnp.where((row16 == r) & (lane16 == at_lane), value, block)
        side[base + 128 : base + 144, :] = block
        density[layer * 128 : (layer + 1) * 128, :] = main[base : base + 128, :]
    upper = jnp.where(lax.axis_index("core") == 1, 288, 0)
    lane8 = iota((8, 128), 1)
    for out, first in ((far, upper), (near, 288 - upper)):
        nearest = pl.multiple_of(jnp.where(first == 0, 0, 432), 144)
        first = pl.multiple_of(first, 144)
        out[0:128, :] = main[pl.ds(first, 128), :].astype(BF16)
        out[128:256, :] = main[pl.ds(first + 144, 128), :].astype(BF16)
        out[256:272, :] = main[pl.ds(nearest + 128, 16), :].astype(BF16)
        folded = jnp.zeros((8, 128), F32)
        for k in range(16):
            piece = pltpu.roll(side[pl.ds(nearest + 8 * k, 8), :], 4 * k + 2, 1)
            folded = jnp.where(lane8 >> 2 == k, piece, folded)
        out[272:288, :] = jnp.concatenate([folded, jnp.zeros((8, 128), F32)], axis=0).astype(BF16)


def depth(a):
    return 3 if a < 2 else 2


def beyond(a, layer):
    k = layer - 3 + depth(a) if layer < 3 else layer - 7
    return 3 * a + k if 0 <= k < depth(a) else None


def from_layer(far, near, a, layer, at):
    k = beyond(a, layer)
    if k is None:
        return None
    same, other = (near, far) if layer < 3 else (far, near)
    upper = lax.axis_index("core") == 1
    return jnp.where(upper, same[k, at, :].astype(F32), other[k, at, :].astype(F32))


def layers_kernel(temp, cond, mass, own, far, near, sems):
    upper = lax.axis_index("core") == 1
    copies = [pltpu.make_async_copy(a, own.at[i], sems.at[i]) for i, a in enumerate((temp, cond, mass))]
    for copy in copies:
        copy.start()
    for a, copy in enumerate(copies):
        copy.wait()
        for k in range(depth(a)):
            last, first = own[a, 4 - depth(a) + k], own[a, k]
            far[3 * a + k] = jnp.where(upper, last, first).astype(BF16)
            near[3 * a + k] = jnp.where(upper, first, last).astype(BF16)


def rows_kernel(own, far, near, outer, inner):
    lasts, firsts = [], []
    for a in range(3):
        for layer in range(10):
            if 3 <= layer < 7:
                lasts.append(own[a, layer - 3, 120:128, :])
                firsts.append(own[a, layer - 3, 0:8, :])
            else:
                zeros = jnp.zeros((8, 128), F32)
                ends = from_layer(far, near, a, layer, slice(112, 128))
                lasts.append(zeros if ends is None else ends[8:16])
                ends = from_layer(far, near, a, layer, slice(0, 16))
                firsts.append(zeros if ends is None else ends[0:8])
    last, first = jnp.concatenate(lasts, axis=0), jnp.concatenate(firsts, axis=0)
    odd = is_odd("row")
    outer[...] = jnp.where(odd, last, first).astype(BF16)
    inner[...] = jnp.where(odd, first, last).astype(BF16)


def gather_kernel(own, far, near, outer, inner, out, to_outer, to_inner):
    over, under = sides(is_odd("row"), outer, inner)
    lane = iota((144, 128), 1)
    left, right = jnp.zeros((144, 128), F32), jnp.zeros((144, 128), F32)
    for a in range(3):
        for layer in range(10):
            i = a * 10 + layer
            if 3 <= layer < 7:
                source = own[a, layer - 3]
            else:
                source = from_layer(far, near, a, layer, slice(0, 128))
                source = jnp.zeros((128, 128), F32) if source is None else source
            piece = jnp.concatenate([source, under[8 * i : 8 * i + 8], over[8 * i : 8 * i + 8]], axis=0)
            out[i] = piece
            base = a * 40 + layer * 4
            here = (lane >= base) & (lane < base + 3)
            left = jnp.where(here, pltpu.roll(piece, base, 1) if base else piece, left)
            right = jnp.where(here, pltpu.roll(piece, base + 3, 1), right)
    odd = is_odd("y")
    to_outer[...] = jnp.where(odd, right, left).astype(BF16)
    to_inner[...] = jnp.where(odd, left, right).astype(BF16)


def turned_by(x, shift, axis):
    return pltpu.roll(x, shift % x.shape[axis], axis)


def around(face_row, face_col, v):
    return (
        face_row * turned_by(v, -1, 0)
        + turned_by(face_row * v, 1, 0)
        + face_col * turned_by(v, -1, 1)
        + turned_by(face_col * v, 1, 1)
    )


def operator_kernel(grids, outer, inner, face_layer, face_row, face_col, inverse, residual, wide):
    left, right = sides(is_odd("y"), outer, inner)
    lane = iota((144, 128), 1)
    for a in range(3):
        for layer in range(10):
            i, base = a * 10 + layer, a * 40 + layer * 4
            high = turned_by(right, -base, 1) if base else right
            side = jnp.where(lane < 3, high, jnp.where(lane >= 125, turned_by(left, 125 - base, 1), 0.0))
            wide[i, :, 0:128] = grids[i]
            wide[i, :, 128:256] = side
    for layer in range(9):
        face_layer[layer] = 0.5 * (wide[10 + layer] + wide[11 + layer])
    for layer in range(1, 9):
        temp, cond, mass = (wide[a * 10 + layer] for a in range(3))
        rows = 0.5 * (cond + turned_by(cond, -1, 0))
        cols = 0.5 * (cond + turned_by(cond, -1, 1))
        face_row[layer - 1] = rows
        face_col[layer - 1] = cols
        after, before = face_layer[layer], face_layer[layer - 1]
        diagonal = mass + after + before + rows + turned_by(rows, 1, 0) + cols + turned_by(cols, 1, 1)
        share = after * wide[layer + 1] + before * wide[layer - 1] + around(rows, cols, temp)
        residual[layer - 1] = mass * temp + (share - diagonal * temp)
        inverse[layer - 1] = jnp.where(mass > 0.0, 1.0 / diagonal, 0.0)


MIDDLE = (eig_low + eig_high) / 2.0
SPREAD = (eig_high - eig_low) / 2.0
W0 = SPREAD / MIDDLE
W1 = 1.0 / (2.0 * MIDDLE / SPREAD - W0)
W2 = 1.0 / (2.0 * MIDDLE / SPREAD - W1)


def sweep_kernel(main, side, far, near, grids, face_layer, face_row, face_col, inverse, residual, out, d0, d1, rest):
    lane = iota((8, 128), 1)
    kept = (lane < 2) | (lane >= 126)
    upper = lax.axis_index("core") == 1

    def supplied(i):
        if 3 <= i <= 6:
            at = (i - 3) * 144
            return main[at : at + 144, :], side[at : at + 144, :]
        at = 128 if i in (2, 8) else 0
        same, other = (near, far) if i < 3 else (far, near)

        def rows(at, size):
            return jnp.where(
                upper, same[at : at + size, :].astype(F32), other[at : at + size, :].astype(F32)
            )

        ends = jnp.zeros((16, 128), F32)
        if i in (1, 8):
            return jnp.concatenate([rows(at, 128), ends], axis=0), jnp.zeros((144, 128), F32)
        folded = rows(272, 16)[0:8]
        beside = [jnp.where(kept, turned_by(folded, -4 * k - 2, 1), 0.0) for k in range(16)]
        return (
            jnp.concatenate([rows(at, 128), rows(256, 16)], axis=0),
            jnp.concatenate([*beside, ends], axis=0),
        )

    for i in range(1, 9):
        start = residual[i - 1] + jnp.concatenate(supplied(i), axis=1)
        rest[i - 1] = start
        d0[i - 1] = start * inverse[i - 1] * (1.0 / MIDDLE)

    def share(i, d):
        return (
            face_layer[i] * d[i]
            + face_layer[i - 1] * d[i - 2]
            + around(face_row[i - 1], face_col[i - 1], d[i - 1])
        )

    for i in range(2, 8):
        start = rest[i - 1]
        later = start * (1.0 - 1.0 / MIDDLE) + share(i, d0)
        d1[i - 1] = W1 * W0 * d0[i - 1] + (2.0 * W1 / SPREAD) * (later * inverse[i - 1])
        rest[i - 1] = later - (W1 * W0 / MIDDLE) * start - (2.0 * W1 / SPREAD) * later
    for i in range(3, 7):
        last = rest[i - 1] + share(i, d1)
        step = d0[i - 1] + d1[i - 1] * (1.0 + W2 * W1) + (2.0 * W2 / SPREAD) * (last * inverse[i - 1])
        at = (i - 3) * 128
        out[at : at + 128, :] = grids[i, 0:128, :] + step[0:128, 0:128]


def sds(shape, dtype):
    return jax.ShapeDtypeStruct(shape, dtype)


def call(kernel, shape, args, mib=16, scratch=(), far=(), far_out=False):
    vmem, anywhere = pl.BlockSpec(memory_space=pltpu.VMEM), pl.BlockSpec(memory_space=pltpu.HBM)
    return pl.pallas_call(
        kernel,
        out_shape=shape,
        in_specs=[anywhere if i in far else vmem for i in range(len(args))],
        out_specs=jax.tree.map(lambda _: anywhere if far_out else vmem, shape),
        scratch_shapes=list(scratch),
        compiler_params=pltpu.CompilerParams(vmem_limit_bytes=mib * 2**20),
    )(*args)


def swap_sides(to_outer, to_inner, axis):
    count = lax.axis_size(axis)

    def swapped(data, first):
        apart = [(i, i + 1) for i in range(first, count - 1, 2)]
        return lax.ppermute(data, axis, apart + [(b, a) for a, b in apart])

    return swapped(to_outer, 1), swapped(to_inner, 0)


def is_odd(axis):
    return (lax.axis_index(axis) & 1) == 1


def sides(odd, outer, inner):
    outer, inner = outer[...].astype(F32), inner[...].astype(F32)
    return jnp.where(odd, inner, outer), jnp.where(odd, outer, inner)


def swap_layers(far, near):
    apart = [(i, i + 1) for i in range(1, lax.axis_size(LAYER) - 1, 2)]
    return (
        lax.ppermute(far, LAYER, apart + [(b, a) for a, b in apart]),
        lax.ppermute(near, "core", [(0, 1), (1, 0)]),
    )


def extended_grids(temp, cond, mass):
    eight, rows, edge = sds((8, 128, 128), BF16), sds((240, 128), BF16), sds((144, 128), BF16)
    own, far, near = call(
        layers_kernel,
        (sds((3, 4, 128, 128), F32), eight, eight),
        (temp, cond, mass),
        scratch=[pltpu.SemaphoreType.DMA((3,))],
        far=range(3),
    )
    far, near = swap_layers(far, near)
    beside = swap_sides(*call(rows_kernel, (rows, rows), (own, far, near)), "row")
    wide, *edges = call(
        gather_kernel, (sds((30, 144, 128), F32), edge, edge), (own, far, near, *beside), mib=24
    )
    return wide, edges, swap_sides(*edges, COL)


def operator(wide, outer, inner):
    eight = sds((8, 144, 256), F32)
    return call(
        operator_kernel,
        (sds((9, 144, 256), F32), eight, eight, eight, eight),
        (wide, outer, inner),
        mib=32,
        scratch=[pltpu.VMEM((30, 144, 256), F32)],
    )


def shards(temp, cond, mass, toggling, baseline, panel, place, holder, tier, warming):
    row64 = pltpu.VMEM((1, 64), I32)
    message, placing, columns = call(
        message_kernel,
        (sds((64, 128), F32), sds((1024, 64), BF16), sds((64, 128), I32)),
        (temp, panel.reshape(1, 64), place, holder, tier),
        mib=60,
        scratch=[
            pltpu.VMEM((4, 128, 128), F32), row64, row64, row64,
            pltpu.VMEM((1, 16), I32), pltpu.SemaphoreType.DMA((5,)),
        ],
        far=range(5),
    )
    messages = lax.all_to_all(message.reshape(64, 1, 128), CUBE, split_axis=0, concat_axis=0, tiled=True)
    messages = messages.reshape(64, 128)
    send = call(
        power_kernel,
        sds((256, 4736), BF16),
        (messages, columns, warming, toggling[0], baseline[0], placing),
        mib=60,
        scratch=[
            pltpu.VMEM((64, 128), F32), pltpu.VMEM((64, 128), I32), pltpu.VMEM((1, 16), F32),
            pltpu.VMEM((64, 4096), BF16), pltpu.VMEM((64, 4096), BF16), pltpu.VMEM((1024, 64), BF16),
            pltpu.VMEM((256, 4736), BF16), pltpu.SemaphoreType.DMA((15,)),
        ],
        far=range(6),
        far_out=True,
    )
    received = lax.all_to_all(send.reshape(16, 16, 4736), PLANE, split_axis=0, concat_axis=0, tiled=True)
    selector = call(selector_kernel, sds((576, 256), BF16), (messages,))
    wide, edges, beside = extended_grids(temp, cond, mass)
    partial = call(
        combine_kernel, sds((64, 4480), F32), (selector, received.reshape(256, 4736), *edges)
    )
    parts = lax.all_to_all(
        partial.astype(jnp.float16).reshape(4, 16, 4480), "zlo", split_axis=0, concat_axis=0, tiled=True
    )
    terms = operator(wide, *beside)
    block, strip = sds((576, 128), F32), sds((288, 128), BF16)
    density, main, side, far, near = call(
        unpack_kernel,
        (sds((512, 128), F32), block, block, strip, strip),
        (jnp.sum(parts.astype(F32), axis=0), *beside),
        scratch=[pltpu.VMEM((512, 128), F32)],
    )
    far, near = swap_layers(far, near)
    eight = pltpu.VMEM((8, 144, 256), F32)
    guess = call(
        sweep_kernel,
        sds((512, 128), F32),
        (main, side, far, near, wide, *terms),
        mib=40,
        scratch=[eight, eight, eight],
    )
    return guess.reshape(4, 128, 128), density.reshape(4, 128, 128)


def solution(mesh):
    fine = Mesh(mesh.devices.reshape(4, 4, 4, 4, 2), ("row", "zlo", "y", "zhi", "core"))
    grid = P(LAYER, "row", COL)
    slot = ("row", "zlo", "y", "zhi", "core")
    return jax.shard_map(
        shards,
        mesh=fine,
        in_specs=(
            grid,
            grid,
            grid,
            P(slot, None, None),
            P(slot, None, None),
            P(slot, None, None),
            P(slot, None),
            P(slot, None),
            P(slot, None),
            P(slot, None),
        ),
        out_specs=(grid, grid),
        check_vma=False,
    )
```

```python
import jax
import jax.numpy as jnp
from jax import lax
from jax.experimental import pallas as pl
from jax.experimental.pallas import tpu as pltpu
from jax.sharding import Mesh
from jax.sharding import PartitionSpec as P

eig_low = 0.1
eig_high = 2.0

LAYER = ("zhi", "core")
COL = ("zlo", "y")
CUBE = ("row", "zlo", "y")
PLANE = ("row", "y")

F32, BF16, I32 = jnp.float32, jnp.bfloat16, jnp.int32


def iota(shape, dim):
    return lax.broadcasted_iota(I32, shape, dim)


def as_column(row):
    n = row.shape[1]
    return jnp.sum(jnp.where(iota((n, n), 0) == iota((n, n), 1), row, 0), axis=1, keepdims=True)


def slot_rows(panel, place, holder, tier):
    layer = jnp.sum(jnp.where(iota((16, 64), 0) == holder, as_column(tier), 0), axis=0, keepdims=True)
    pos = layer * 4 + place
    ident = ((panel >> 2) & 3) * 16 + pos
    column = (panel >> 4) * 4 + (panel & 3)
    same = (as_column(column) == column) & (iota((64, 64), 0) < iota((64, 64), 1))
    rank = jnp.sum(same.astype(I32), axis=0, keepdims=True)
    return pos, ident, column * 16 + rank


def place_slots(panel, pos, dest, holder, placing, columns):
    x, y, rank = panel >> 4, panel & 3, dest & 15
    lower, right = (pos >> 1) & 1, pos & 1
    next_x = x + lower * 2 - 1
    next_y = (y + right * 2 + 3) & 3
    inside = (next_x >= 0) & (next_x <= 3)
    targets = (
        dest,
        jnp.where(inside, (next_x * 4 + y) * 16 + rank, -1),
        (x * 4 + next_y) * 16 + rank,
        jnp.where(inside, (next_x * 4 + next_y) * 16 + rank, -1),
    )
    for k, target in enumerate(targets):
        placing[pl.ds(k * 256, 256), :] = jnp.where(iota((256, 64), 0) == target, 1.0, 0.0).astype(BF16)
    lane = iota((64, 128), 1)
    columns[...] = jnp.where(
        lane == 0, as_column(panel), jnp.where(lane == 1, as_column(pos), as_column(holder))
    )


def message_kernel(temp, panel, place, holder, tier, out, placing, columns, temp_v, panel_v, place_v, holder_v, tier_v, sems):
    pairs = [(panel, panel_v), (place, place_v), (holder, holder_v), (tier, tier_v), (temp, temp_v)]
    copies = [pltpu.make_async_copy(a, b, sems.at[i]) for i, (a, b) in enumerate(pairs)]
    for copy in copies:
        copy.start()
    for copy in copies[:4]:
        copy.wait()
    panel_row, holder_row = panel_v[...], holder_v[...]
    pos, ident, dest = slot_rows(panel_row, place_v[...], holder_row, tier_v[...])
    place_slots(panel_row, pos, dest, holder_row, placing, columns)
    code = (dest * 64 + ident).astype(F32)
    copies[4].wait()
    sums = jnp.sum(temp_v[...].reshape(8, 64, 128), axis=1)
    lane = iota((8, 128), 1)
    first = jnp.sum(jnp.where(lane < 64, sums, 0.0), axis=1, keepdims=True)
    second = jnp.sum(jnp.where(lane < 64, 0.0, sums), axis=1, keepdims=True)
    at = iota((8, 128), 0) * 2
    means = jnp.where(lane == at, first, jnp.where(lane == at + 1, second, 0.0))
    means = jnp.sum(means, axis=0, keepdims=True) * (1.0 / 4096.0)
    row = jnp.where(iota((1, 128), 1) < 64, means, jnp.concatenate([code, code], axis=1))
    out[...] = jnp.broadcast_to(row, (64, 128))


def power_kernel(
    far_messages, far_columns, far_warming, far_toggling, far_baseline, far_placing, out,
    messages, columns, warming, toggling, baseline, placing, sent, sems,
):
    pairs = [
        (far_messages, messages),
        (far_columns, columns),
        (far_warming, warming),
        (far_toggling, toggling),
        (far_baseline, baseline),
        (far_placing, placing),
    ]
    loads = [pltpu.make_async_copy(a, b, sems.at[9 + i]) for i, (a, b) in enumerate(pairs)]
    for load in loads:
        load.start()
    loads[0].wait()
    loads[1].wait()
    tile, pos, holder = (columns[:, k : k + 1] for k in range(3))
    lower, right = (pos >> 1) & 1, pos & 1
    pick = jnp.where(iota((64, 64), 1) == tile, 1.0, 0.0)
    means = jnp.dot(pick, messages[...], precision=lax.Precision.HIGHEST, preferred_element_type=F32)
    lane = iota((64, 128), 1)
    slot_mean = jnp.sum(jnp.where(lane == pos, means, 0.0), axis=1, keepdims=True)
    member = iota((64, 16), 1) == holder
    total = jnp.sum(jnp.where(member, slot_mean, 0.0), axis=0, keepdims=True)
    count = jnp.sum(jnp.where(member, 1.0, 0.0), axis=0, keepdims=True)
    loads[2].wait()
    leak = jnp.exp(warming[...] * (total / count))
    factor = jnp.sum(jnp.where(member, leak, 0.0), axis=1, keepdims=True)

    def place(kind, values):
        at = placing[kind * 256 : (kind + 1) * 256, :]
        return jnp.dot(at, values.astype(BF16), preferred_element_type=F32).astype(BF16)

    copies = []

    def send(start, width):
        at = pl.ds(start, width)
        copy = pltpu.make_async_copy(sent.at[:, at], out.at[:, at], sems.at[len(copies)])
        copy.start()
        copies.append(copy)

    for load in loads[3:]:
        load.wait()
    edge = ((lane & 63) >> 1) == right * 31
    sides = jnp.zeros((64, 128), F32)
    width = 512
    for k in range(8):
        at = pl.ds(k * width, width)
        power = (toggling[:, at].astype(F32) + factor * baseline[:, at].astype(F32)).astype(BF16)
        sent[:, at] = place(0, power)
        send(k * width, width)
        power = power.astype(F32)
        for t in range(4):
            piece = power[:, t * 128 : (t + 1) * 128]
            shift = 2 * (4 * k + t)
            kept = jnp.where(edge, piece, 0.0)
            sides = sides + (pltpu.roll(kept, shift, 1) if shift else kept)
            if k == 0 and t == 0:
                top = piece
    rows = jnp.where(lower == 0, top, piece)
    sides = jnp.where(right == 0, sides, pltpu.roll(sides, 66, 1))
    corner = jnp.sum(jnp.where(lane == lower * 64 + right * 63, rows, 0.0), axis=1, keepdims=True)
    quarter = (1 - lower) * 2 + 1 - right
    both = jnp.concatenate([jnp.where(lower == 1, rows, 0.0), jnp.where(lower == 0, rows, 0.0)], axis=1)
    sent[:, 4096:4352] = place(1, both)
    both = jnp.concatenate([jnp.where(right == 1, sides, 0.0), jnp.where(right == 0, sides, 0.0)], axis=1)
    sent[:, 4352:4608] = place(2, both)
    sent[:, 4608:4736] = place(3, jnp.where(lane == quarter, corner, 0.0))
    send(4096, 640)
    for copy in copies:
        copy.wait()


def selector_kernel(messages, out):
    x, y = lax.axis_index("row"), lax.axis_index("y")
    plane = lax.axis_index("zlo")
    code = jnp.concatenate([messages[pl.ds(r * 16 + plane * 4, 4), :] for r in range(4)], axis=0)
    code = jnp.where(iota((16, 128), 1) < 64, -1.0, code).astype(I32)
    dest, ident = code >> 6, code & 63
    lane = iota((16, 256), 1)

    def idents(dx, dy):
        base = ((x + dx) * 4 + ((y + dy + 4) & 3)) * 16
        ids = jnp.zeros((16, 256), I32)
        for r in range(16):
            hit = jnp.sum(jnp.where(dest == base + r, ident + 1, 0), axis=1, keepdims=True)
            ids = jnp.where((lane & 15) == r, hit, ids)
        ids = jnp.sum(jnp.where((lane >> 4) == iota((16, 256), 0), ids, 0), axis=0, keepdims=True) - 1
        turn = jnp.where(y == 0, 1, 0) if dy < 0 else jnp.where(y == 3, -1, 0) if dy > 0 else 0
        return ids, (ids >> 4) + turn, (ids >> 2) & 3, (ids >> 1) & 1, ids & 1

    def put(k, ids, target):
        out[pl.ds(k * 64, 64), :] = jnp.where(
            (iota((64, 256), 0) == target) & (ids >= 0), 1.0, 0.0
        ).astype(BF16)

    ids, *_ = idents(0, 0)
    put(0, ids, ids)
    for k, dx in enumerate((-1, 1)):
        ids, z, layer, _, pc = idents(dx, 0)
        put(1 + k, ids, z * 16 + k * 8 + layer * 2 + pc)
    for k, dy in enumerate((-1, 1)):
        ids, z, layer, pr, _ = idents(0, dy)
        put(3 + k, ids, z * 16 + k * 8 + layer * 2 + pr)
    for k in range(4):
        ids, z, layer, _, _ = idents((k >> 1) * 2 - 1, (k & 1) * 2 - 1)
        put(5 + k, ids, z * 16 + layer)


def combine_kernel(selector, received, _outer, _inner, out):
    def add(k, start, width):
        return jnp.dot(
            selector[k * 64 : (k + 1) * 64, :],
            received[:, start : start + width],
            preferred_element_type=F32,
        )

    for k in range(8):
        out[:, k * 512 : (k + 1) * 512] = add(0, k * 512, 512)
    out[:, 4096:4224] = add(1, 4096, 128) + add(2, 4224, 128)
    out[:, 4224:4352] = add(3, 4352, 128) + add(4, 4480, 128)
    lane = iota((64, 128), 1)
    corners = jnp.zeros((64, 128), F32)
    for k in range(4):
        corners = jnp.where(lane == k, add(5 + k, 4608, 128), corners)
    out[:, 4352:4480] = corners


def unpack_kernel(whole, _outer, _inner, density, main, side, far, near, turned):
    for k in range(32):
        turned[k * 16 : (k + 1) * 16, :] = whole[:, k * 128 : (k + 1) * 128]
    low = iota((32, 128), 1) < 64
    lane = iota((64, 128), 1)
    low_row = iota((1, 128), 1) < 64
    lane16, row16 = iota((16, 128), 1), iota((16, 128), 0)
    rows, columns, corners = whole[:, 4096:4224], whole[:, 4224:4352], whole[:, 4352:4480]
    cell = iota((64, 128), 0)
    turn = []
    for c in range(2):
        pick = jnp.where(lane == (cell & 1) * 64 + (cell - (cell & 1)) + c, 1.0, 0.0)
        turn.append(
            lax.dot_general(
                pick, columns, (((1,), (1,)), ((), ())),
                precision=lax.Precision.HIGHEST, preferred_element_type=F32,
            )
        )
    for layer in range(4):
        base = layer * 144
        for r in range(2):
            left = turned[pl.ds(layer * 4 + r * 2, 32, stride=16), :]
            right = turned[pl.ds(layer * 4 + r * 2 + 1, 32, stride=16), :]
            at = base + r * 64
            main[pl.ds(at, 32, stride=2), :] = jnp.where(low, left, pltpu.roll(right, 64, 1))
            main[pl.ds(at + 1, 32, stride=2), :] = jnp.where(low, pltpu.roll(left, 64, 1), right)
            k = layer * 2 + r
            strip = jnp.where(lane == 0, turn[0][:, 8 + k : 9 + k], 0.0)
            strip = jnp.where(lane == 1, turn[1][:, 8 + k : 9 + k], strip)
            strip = jnp.where(lane == 126, turn[0][:, k : k + 1], strip)
            side[at : at + 64, :] = jnp.where(lane == 127, turn[1][:, k : k + 1], strip)
        block = jnp.zeros((16, 128), F32)
        for kind, first_row in ((0, 14), (1, 0)):
            k = kind * 8 + layer * 2
            a, b = rows[k : k + 1, :], rows[k + 1 : k + 2, :]
            first = jnp.where(low_row, a, pltpu.roll(b, 64, 1))
            second = jnp.where(low_row, pltpu.roll(a, 64, 1), b)
            block = jnp.where(row16 == first_row, first, block)
            block = jnp.where(row16 == first_row + 1, second, block)
        main[base + 128 : base + 144, :] = block
        block = jnp.zeros((16, 128), F32)
        for k, (r, at_lane) in enumerate(((15, 127), (15, 0), (0, 127), (0, 0))):
            value = corners[layer : layer + 1, k : k + 1]
            block = jnp.where((row16 == r) & (lane16 == at_lane), value, block)
        side[base + 128 : base + 144, :] = block
        density[layer * 128 : (layer + 1) * 128, :] = main[base : base + 128, :]
    upper = jnp.where(lax.axis_index("core") == 1, 288, 0)
    lane8 = iota((8, 128), 1)
    for out, first in ((far, upper), (near, 288 - upper)):
        nearest = pl.multiple_of(jnp.where(first == 0, 0, 432), 144)
        first = pl.multiple_of(first, 144)
        out[0:128, :] = main[pl.ds(first, 128), :].astype(BF16)
        out[128:256, :] = main[pl.ds(first + 144, 128), :].astype(BF16)
        out[256:272, :] = main[pl.ds(nearest + 128, 16), :].astype(BF16)
        folded = jnp.zeros((8, 128), F32)
        for k in range(16):
            piece = pltpu.roll(side[pl.ds(nearest + 8 * k, 8), :], 4 * k + 2, 1)
            folded = jnp.where(lane8 >> 2 == k, piece, folded)
        out[272:288, :] = jnp.concatenate([folded, jnp.zeros((8, 128), F32)], axis=0).astype(BF16)


def depth(a):
    return 3 if a < 2 else 2


def beyond(a, layer):
    k = layer - 3 + depth(a) if layer < 3 else layer - 7
    return 3 * a + k if 0 <= k < depth(a) else None


def from_layer(far, near, a, layer, at):
    k = beyond(a, layer)
    if k is None:
        return None
    same, other = (near, far) if layer < 3 else (far, near)
    upper = lax.axis_index("core") == 1
    return jnp.where(upper, same[k, at, :].astype(F32), other[k, at, :].astype(F32))


def layers_kernel(temp, cond, mass, own, far, near, sems):
    upper = lax.axis_index("core") == 1
    copies = [pltpu.make_async_copy(a, own.at[i], sems.at[i]) for i, a in enumerate((temp, cond, mass))]
    for copy in copies:
        copy.start()
    for a, copy in enumerate(copies):
        copy.wait()
        for k in range(depth(a)):
            last, first = own[a, 4 - depth(a) + k], own[a, k]
            far[3 * a + k] = jnp.where(upper, last, first).astype(BF16)
            near[3 * a + k] = jnp.where(upper, first, last).astype(BF16)


def rows_kernel(own, far, near, outer, inner):
    lasts, firsts = [], []
    for a in range(3):
        for layer in range(10):
            if 3 <= layer < 7:
                lasts.append(own[a, layer - 3, 120:128, :])
                firsts.append(own[a, layer - 3, 0:8, :])
            else:
                zeros = jnp.zeros((8, 128), F32)
                ends = from_layer(far, near, a, layer, slice(112, 128))
                lasts.append(zeros if ends is None else ends[8:16])
                ends = from_layer(far, near, a, layer, slice(0, 16))
                firsts.append(zeros if ends is None else ends[0:8])
    last, first = jnp.concatenate(lasts, axis=0), jnp.concatenate(firsts, axis=0)
    odd = is_odd("row")
    outer[...] = jnp.where(odd, last, first).astype(BF16)
    inner[...] = jnp.where(odd, first, last).astype(BF16)


def gather_kernel(own, far, near, outer, inner, out, to_outer, to_inner):
    over, under = sides(is_odd("row"), outer, inner)
    lane = iota((144, 128), 1)
    left, right = jnp.zeros((144, 128), F32), jnp.zeros((144, 128), F32)
    for a in range(3):
        for layer in range(10):
            i = a * 10 + layer
            if 3 <= layer < 7:
                source = own[a, layer - 3]
            else:
                source = from_layer(far, near, a, layer, slice(0, 128))
                source = jnp.zeros((128, 128), F32) if source is None else source
            piece = jnp.concatenate([source, under[8 * i : 8 * i + 8], over[8 * i : 8 * i + 8]], axis=0)
            out[i] = piece
            base = a * 40 + layer * 4
            here = (lane >= base) & (lane < base + 3)
            left = jnp.where(here, pltpu.roll(piece, base, 1) if base else piece, left)
            right = jnp.where(here, pltpu.roll(piece, base + 3, 1), right)
    odd = is_odd("y")
    to_outer[...] = jnp.where(odd, right, left).astype(BF16)
    to_inner[...] = jnp.where(odd, left, right).astype(BF16)


def turned_by(x, shift, axis):
    return pltpu.roll(x, shift % x.shape[axis], axis)


def around(face_row, face_col, v):
    return (
        face_row * turned_by(v, -1, 0)
        + turned_by(face_row * v, 1, 0)
        + face_col * turned_by(v, -1, 1)
        + turned_by(face_col * v, 1, 1)
    )


def operator_kernel(grids, outer, inner, face_layer, face_row, face_col, inverse, residual, wide):
    left, right = sides(is_odd("y"), outer, inner)
    lane = iota((144, 128), 1)
    for a in range(3):
        for layer in range(10):
            i, base = a * 10 + layer, a * 40 + layer * 4
            high = turned_by(right, -base, 1) if base else right
            side = jnp.where(lane < 3, high, jnp.where(lane >= 125, turned_by(left, 125 - base, 1), 0.0))
            wide[i, :, 0:128] = grids[i]
            wide[i, :, 128:256] = side
    for layer in range(9):
        face_layer[layer] = 0.5 * (wide[10 + layer] + wide[11 + layer])
    for layer in range(1, 9):
        temp, cond, mass = (wide[a * 10 + layer] for a in range(3))
        rows = 0.5 * (cond + turned_by(cond, -1, 0))
        cols = 0.5 * (cond + turned_by(cond, -1, 1))
        face_row[layer - 1] = rows
        face_col[layer - 1] = cols
        after, before = face_layer[layer], face_layer[layer - 1]
        diagonal = mass + after + before + rows + turned_by(rows, 1, 0) + cols + turned_by(cols, 1, 1)
        share = after * wide[layer + 1] + before * wide[layer - 1] + around(rows, cols, temp)
        residual[layer - 1] = mass * temp + (share - diagonal * temp)
        inverse[layer - 1] = jnp.where(mass > 0.0, 1.0 / diagonal, 0.0)


MIDDLE = (eig_low + eig_high) / 2.0
SPREAD = (eig_high - eig_low) / 2.0
W0 = SPREAD / MIDDLE
W1 = 1.0 / (2.0 * MIDDLE / SPREAD - W0)
W2 = 1.0 / (2.0 * MIDDLE / SPREAD - W1)


def sweep_kernel(main, side, far, near, grids, face_layer, face_row, face_col, inverse, residual, out, d0, d1, rest):
    lane = iota((8, 128), 1)
    kept = (lane < 2) | (lane >= 126)
    upper = lax.axis_index("core") == 1

    def supplied(i):
        if 3 <= i <= 6:
            at = (i - 3) * 144
            return main[at : at + 144, :], side[at : at + 144, :]
        at = 128 if i in (2, 8) else 0
        same, other = (near, far) if i < 3 else (far, near)

        def rows(at, size):
            return jnp.where(
                upper, same[at : at + size, :].astype(F32), other[at : at + size, :].astype(F32)
            )

        ends = jnp.zeros((16, 128), F32)
        if i in (1, 8):
            return jnp.concatenate([rows(at, 128), ends], axis=0), jnp.zeros((144, 128), F32)
        folded = rows(272, 16)[0:8]
        beside = [jnp.where(kept, turned_by(folded, -4 * k - 2, 1), 0.0) for k in range(16)]
        return (
            jnp.concatenate([rows(at, 128), rows(256, 16)], axis=0),
            jnp.concatenate([*beside, ends], axis=0),
        )

    for i in range(1, 9):
        start = residual[i - 1] + jnp.concatenate(supplied(i), axis=1)
        rest[i - 1] = start
        d0[i - 1] = start * inverse[i - 1] * (1.0 / MIDDLE)

    def share(i, d):
        return (
            face_layer[i] * d[i]
            + face_layer[i - 1] * d[i - 2]
            + around(face_row[i - 1], face_col[i - 1], d[i - 1])
        )

    for i in range(2, 8):
        start = rest[i - 1]
        later = start * (1.0 - 1.0 / MIDDLE) + share(i, d0)
        d1[i - 1] = W1 * W0 * d0[i - 1] + (2.0 * W1 / SPREAD) * (later * inverse[i - 1])
        rest[i - 1] = later - (W1 * W0 / MIDDLE) * start - (2.0 * W1 / SPREAD) * later
    for i in range(3, 7):
        last = rest[i - 1] + share(i, d1)
        step = d0[i - 1] + d1[i - 1] * (1.0 + W2 * W1) + (2.0 * W2 / SPREAD) * (last * inverse[i - 1])
        at = (i - 3) * 128
        out[at : at + 128, :] = grids[i, 0:128, :] + step[0:128, 0:128]


def sds(shape, dtype):
    return jax.ShapeDtypeStruct(shape, dtype)


def call(kernel, shape, args, mib=16, scratch=(), far=(), far_out=False):
    vmem, anywhere = pl.BlockSpec(memory_space=pltpu.VMEM), pl.BlockSpec(memory_space=pltpu.HBM)
    return pl.pallas_call(
        kernel,
        out_shape=shape,
        in_specs=[anywhere if i in far else vmem for i in range(len(args))],
        out_specs=jax.tree.map(lambda _: anywhere if far_out else vmem, shape),
        scratch_shapes=list(scratch),
        compiler_params=pltpu.CompilerParams(vmem_limit_bytes=mib * 2**20),
    )(*args)


def swap_sides(to_outer, to_inner, axis):
    count = lax.axis_size(axis)

    def swapped(data, first):
        apart = [(i, i + 1) for i in range(first, count - 1, 2)]
        return lax.ppermute(data, axis, apart + [(b, a) for a, b in apart])

    return swapped(to_outer, 1), swapped(to_inner, 0)


def is_odd(axis):
    return (lax.axis_index(axis) & 1) == 1


def sides(odd, outer, inner):
    outer, inner = outer[...].astype(F32), inner[...].astype(F32)
    return jnp.where(odd, inner, outer), jnp.where(odd, outer, inner)


def swap_layers(far, near):
    apart = [(i, i + 1) for i in range(1, lax.axis_size(LAYER) - 1, 2)]
    return (
        lax.ppermute(far, LAYER, apart + [(b, a) for a, b in apart]),
        lax.ppermute(near, "core", [(0, 1), (1, 0)]),
    )


def extended_grids(temp, cond, mass):
    eight, rows, edge = sds((8, 128, 128), BF16), sds((240, 128), BF16), sds((144, 128), BF16)
    own, far, near = call(
        layers_kernel,
        (sds((3, 4, 128, 128), F32), eight, eight),
        (temp, cond, mass),
        scratch=[pltpu.SemaphoreType.DMA((3,))],
        far=range(3),
    )
    far, near = swap_layers(far, near)
    beside = swap_sides(*call(rows_kernel, (rows, rows), (own, far, near)), "row")
    wide, *edges = call(
        gather_kernel, (sds((30, 144, 128), F32), edge, edge), (own, far, near, *beside), mib=24
    )
    return wide, edges, swap_sides(*edges, COL)


def operator(wide, outer, inner):
    eight = sds((8, 144, 256), F32)
    return call(
        operator_kernel,
        (sds((9, 144, 256), F32), eight, eight, eight, eight),
        (wide, outer, inner),
        mib=32,
        scratch=[pltpu.VMEM((30, 144, 256), F32)],
    )


def shards(temp, cond, mass, toggling, baseline, panel, place, holder, tier, warming):
    row64 = pltpu.VMEM((1, 64), I32)
    message, placing, columns = call(
        message_kernel,
        (sds((64, 128), F32), sds((1024, 64), BF16), sds((64, 128), I32)),
        (temp, panel.reshape(1, 64), place, holder, tier),
        mib=60,
        scratch=[
            pltpu.VMEM((4, 128, 128), F32), row64, row64, row64,
            pltpu.VMEM((1, 16), I32), pltpu.SemaphoreType.DMA((5,)),
        ],
        far=range(5),
    )
    messages = lax.all_to_all(message.reshape(64, 1, 128), CUBE, split_axis=0, concat_axis=0, tiled=True)
    messages = messages.reshape(64, 128)
    send = call(
        power_kernel,
        sds((256, 4736), BF16),
        (messages, columns, warming, toggling[0], baseline[0], placing),
        mib=60,
        scratch=[
            pltpu.VMEM((64, 128), F32), pltpu.VMEM((64, 128), I32), pltpu.VMEM((1, 16), F32),
            pltpu.VMEM((64, 4096), BF16), pltpu.VMEM((64, 4096), BF16), pltpu.VMEM((1024, 64), BF16),
            pltpu.VMEM((256, 4736), BF16), pltpu.SemaphoreType.DMA((15,)),
        ],
        far=range(6),
        far_out=True,
    )
    received = lax.all_to_all(send.reshape(16, 16, 4736), PLANE, split_axis=0, concat_axis=0, tiled=True)
    selector = call(selector_kernel, sds((576, 256), BF16), (messages,))
    wide, edges, beside = extended_grids(temp, cond, mass)
    partial = call(
        combine_kernel, sds((64, 4480), F32), (selector, received.reshape(256, 4736), *edges)
    )
    parts = lax.all_to_all(
        partial.astype(jnp.float16).reshape(4, 16, 4480), "zlo", split_axis=0, concat_axis=0, tiled=True
    )
    terms = operator(wide, *beside)
    block, strip = sds((576, 128), F32), sds((288, 128), BF16)
    density, main, side, far, near = call(
        unpack_kernel,
        (sds((512, 128), F32), block, block, strip, strip),
        (jnp.sum(parts.astype(F32), axis=0), *beside),
        scratch=[pltpu.VMEM((528, 128), F32)],
    )
    far, near = swap_layers(far, near)
    eight = pltpu.VMEM((8, 144, 256), F32)
    guess = call(
        sweep_kernel,
        sds((512, 128), F32),
        (main, side, far, near, wide, *terms),
        mib=40,
        scratch=[eight, eight, eight],
    )
    return guess.reshape(4, 128, 128), density.reshape(4, 128, 128)


def solution(mesh):
    fine = Mesh(mesh.devices.reshape(4, 4, 4, 4, 2), ("row", "zlo", "y", "zhi", "core"))
    grid = P(LAYER, "row", COL)
    slot = ("row", "zlo", "y", "zhi", "core")
    return jax.shard_map(
        shards,
        mesh=fine,
        in_specs=(
            grid,
            grid,
            grid,
            P(slot, None, None),
            P(slot, None, None),
            P(slot, None, None),
            P(slot, None),
            P(slot, None),
            P(slot, None),
            P(slot, None),
        ),
        out_specs=(grid, grid),
        check_vma=False,
    )
```

```python
import jax
import jax.numpy as jnp
from jax import lax
from jax.experimental import pallas as pl
from jax.experimental.pallas import tpu as pltpu
from jax.sharding import Mesh
from jax.sharding import PartitionSpec as P

eig_low = 0.1
eig_high = 2.0

LAYER = ("zhi", "core")
COL = ("zlo", "y")
CUBE = ("row", "zlo", "y")
PLANE = ("row", "y")

F32, BF16, I32 = jnp.float32, jnp.bfloat16, jnp.int32


def iota(shape, dim):
    return lax.broadcasted_iota(I32, shape, dim)


def as_column(row):
    n = row.shape[1]
    return jnp.sum(jnp.where(iota((n, n), 0) == iota((n, n), 1), row, 0), axis=1, keepdims=True)


def slot_rows(panel, place, holder, tier):
    layer = jnp.sum(jnp.where(iota((16, 64), 0) == holder, as_column(tier), 0), axis=0, keepdims=True)
    pos = layer * 4 + place
    ident = ((panel >> 2) & 3) * 16 + pos
    column = (panel >> 4) * 4 + (panel & 3)
    same = (as_column(column) == column) & (iota((64, 64), 0) < iota((64, 64), 1))
    rank = jnp.sum(same.astype(I32), axis=0, keepdims=True)
    return pos, ident, column * 16 + rank


def place_slots(panel, pos, dest, holder, placing, columns):
    x, y, rank = panel >> 4, panel & 3, dest & 15
    lower, right = (pos >> 1) & 1, pos & 1
    next_x = x + lower * 2 - 1
    next_y = (y + right * 2 + 3) & 3
    inside = (next_x >= 0) & (next_x <= 3)
    targets = (
        dest,
        jnp.where(inside, (next_x * 4 + y) * 16 + rank, -1),
        (x * 4 + next_y) * 16 + rank,
        jnp.where(inside, (next_x * 4 + next_y) * 16 + rank, -1),
    )
    for k, target in enumerate(targets):
        placing[pl.ds(k * 256, 256), :] = jnp.where(iota((256, 64), 0) == target, 1.0, 0.0).astype(BF16)
    lane = iota((64, 128), 1)
    columns[...] = jnp.where(
        lane == 0, as_column(panel), jnp.where(lane == 1, as_column(pos), as_column(holder))
    )


def message_kernel(temp, panel, place, holder, tier, out, placing, columns, temp_v, panel_v, place_v, holder_v, tier_v, sems):
    pairs = [(panel, panel_v), (place, place_v), (holder, holder_v), (tier, tier_v), (temp, temp_v)]
    copies = [pltpu.make_async_copy(a, b, sems.at[i]) for i, (a, b) in enumerate(pairs)]
    for copy in copies:
        copy.start()
    for copy in copies[:4]:
        copy.wait()
    panel_row, holder_row = panel_v[...], holder_v[...]
    pos, ident, dest = slot_rows(panel_row, place_v[...], holder_row, tier_v[...])
    place_slots(panel_row, pos, dest, holder_row, placing, columns)
    code = (dest * 64 + ident).astype(F32)
    copies[4].wait()
    sums = jnp.sum(temp_v[...].reshape(8, 64, 128), axis=1)
    lane = iota((8, 128), 1)
    first = jnp.sum(jnp.where(lane < 64, sums, 0.0), axis=1, keepdims=True)
    second = jnp.sum(jnp.where(lane < 64, 0.0, sums), axis=1, keepdims=True)
    at = iota((8, 128), 0) * 2
    means = jnp.where(lane == at, first, jnp.where(lane == at + 1, second, 0.0))
    means = jnp.sum(means, axis=0, keepdims=True) * (1.0 / 4096.0)
    row = jnp.where(iota((1, 128), 1) < 64, means, jnp.concatenate([code, code], axis=1))
    out[...] = jnp.broadcast_to(row, (64, 128))


def power_kernel(
    far_messages, far_columns, far_warming, far_toggling, far_baseline, far_placing, out,
    messages, columns, warming, toggling, baseline, placing, sent, sems,
):
    pairs = [
        (far_messages, messages),
        (far_columns, columns),
        (far_warming, warming),
        (far_toggling, toggling),
        (far_baseline, baseline),
        (far_placing, placing),
    ]
    loads = [pltpu.make_async_copy(a, b, sems.at[9 + i]) for i, (a, b) in enumerate(pairs)]
    for load in loads:
        load.start()
    loads[0].wait()
    loads[1].wait()
    tile, pos, holder = (columns[:, k : k + 1] for k in range(3))
    lower, right = (pos >> 1) & 1, pos & 1
    pick = jnp.where(iota((64, 64), 1) == tile, 1.0, 0.0)
    means = jnp.dot(pick, messages[...], precision=lax.Precision.HIGHEST, preferred_element_type=F32)
    lane = iota((64, 128), 1)
    slot_mean = jnp.sum(jnp.where(lane == pos, means, 0.0), axis=1, keepdims=True)
    member = iota((64, 16), 1) == holder
    total = jnp.sum(jnp.where(member, slot_mean, 0.0), axis=0, keepdims=True)
    count = jnp.sum(jnp.where(member, 1.0, 0.0), axis=0, keepdims=True)
    loads[2].wait()
    leak = jnp.exp(warming[...] * (total / count))
    factor = jnp.sum(jnp.where(member, leak, 0.0), axis=1, keepdims=True)

    def place(kind, values):
        at = placing[kind * 256 : (kind + 1) * 256, :]
        return jnp.dot(at, values.astype(BF16), preferred_element_type=F32).astype(BF16)

    copies = []

    def send(start, width):
        at = pl.ds(start, width)
        copy = pltpu.make_async_copy(sent.at[:, at], out.at[:, at], sems.at[len(copies)])
        copy.start()
        copies.append(copy)

    for load in loads[3:]:
        load.wait()
    edge = ((lane & 63) >> 1) == right * 31
    sides = jnp.zeros((64, 128), F32)
    width = 512
    for k in range(8):
        at = pl.ds(k * width, width)
        power = (toggling[:, at].astype(F32) + factor * baseline[:, at].astype(F32)).astype(BF16)
        sent[:, at] = place(0, power)
        send(k * width, width)
        power = power.astype(F32)
        for t in range(4):
            piece = power[:, t * 128 : (t + 1) * 128]
            shift = 2 * (4 * k + t)
            kept = jnp.where(edge, piece, 0.0)
            sides = sides + (pltpu.roll(kept, shift, 1) if shift else kept)
            if k == 0 and t == 0:
                top = piece
    rows = jnp.where(lower == 0, top, piece)
    sides = jnp.where(right == 0, sides, pltpu.roll(sides, 66, 1))
    corner = jnp.sum(jnp.where(lane == lower * 64 + right * 63, rows, 0.0), axis=1, keepdims=True)
    quarter = (1 - lower) * 2 + 1 - right
    both = jnp.concatenate([jnp.where(lower == 1, rows, 0.0), jnp.where(lower == 0, rows, 0.0)], axis=1)
    sent[:, 4096:4352] = place(1, both)
    both = jnp.concatenate([jnp.where(right == 1, sides, 0.0), jnp.where(right == 0, sides, 0.0)], axis=1)
    sent[:, 4352:4608] = place(2, both)
    sent[:, 4608:4736] = place(3, jnp.where(lane == quarter, corner, 0.0))
    send(4096, 640)
    for copy in copies:
        copy.wait()


def selector_kernel(messages, _outer, _inner, out):
    x, y = lax.axis_index("row"), lax.axis_index("y")
    plane = lax.axis_index("zlo")
    code = jnp.concatenate([messages[pl.ds(r * 16 + plane * 4, 4), :] for r in range(4)], axis=0)
    code = jnp.where(iota((16, 128), 1) < 64, -1.0, code).astype(I32)
    dest, ident = code >> 6, code & 63
    lane = iota((16, 256), 1)

    def idents(dx, dy):
        base = ((x + dx) * 4 + ((y + dy + 4) & 3)) * 16
        ids = jnp.zeros((16, 256), I32)
        for r in range(16):
            hit = jnp.sum(jnp.where(dest == base + r, ident + 1, 0), axis=1, keepdims=True)
            ids = jnp.where((lane & 15) == r, hit, ids)
        ids = jnp.sum(jnp.where((lane >> 4) == iota((16, 256), 0), ids, 0), axis=0, keepdims=True) - 1
        turn = jnp.where(y == 0, 1, 0) if dy < 0 else jnp.where(y == 3, -1, 0) if dy > 0 else 0
        return ids, (ids >> 4) + turn, (ids >> 2) & 3, (ids >> 1) & 1, ids & 1

    def put(k, ids, target):
        out[pl.ds(k * 64, 64), :] = jnp.where(
            (iota((64, 256), 0) == target) & (ids >= 0), 1.0, 0.0
        ).astype(BF16)

    ids, *_ = idents(0, 0)
    put(0, ids, ids)
    for k, dx in enumerate((-1, 1)):
        ids, z, layer, _, pc = idents(dx, 0)
        put(1 + k, ids, z * 16 + k * 8 + layer * 2 + pc)
    for k, dy in enumerate((-1, 1)):
        ids, z, layer, pr, _ = idents(0, dy)
        put(3 + k, ids, z * 16 + k * 8 + layer * 2 + pr)
    for k in range(4):
        ids, z, layer, _, _ = idents((k >> 1) * 2 - 1, (k & 1) * 2 - 1)
        put(5 + k, ids, z * 16 + layer)


def combine_kernel(selector, received, out):
    def add(k, start, width):
        return jnp.dot(
            selector[k * 64 : (k + 1) * 64, :],
            received[:, start : start + width],
            preferred_element_type=F32,
        )

    for k in range(8):
        out[:, k * 512 : (k + 1) * 512] = add(0, k * 512, 512)
    out[:, 4096:4224] = add(1, 4096, 128) + add(2, 4224, 128)
    out[:, 4224:4352] = add(3, 4352, 128) + add(4, 4480, 128)
    lane = iota((64, 128), 1)
    corners = jnp.zeros((64, 128), F32)
    for k in range(4):
        corners = jnp.where(lane == k, add(5 + k, 4608, 128), corners)
    out[:, 4352:4480] = corners


def unpack_kernel(whole, _outer, _inner, density, main, side, far, near, turned):
    for k in range(32):
        turned[k * 16 : (k + 1) * 16, :] = whole[:, k * 128 : (k + 1) * 128]
    low = iota((32, 128), 1) < 64
    lane = iota((64, 128), 1)
    low_row = iota((1, 128), 1) < 64
    lane16, row16 = iota((16, 128), 1), iota((16, 128), 0)
    rows, columns, corners = whole[:, 4096:4224], whole[:, 4224:4352], whole[:, 4352:4480]
    cell = iota((64, 128), 0)
    turn = []
    for c in range(2):
        pick = jnp.where(lane == (cell & 1) * 64 + (cell - (cell & 1)) + c, 1.0, 0.0)
        turn.append(
            lax.dot_general(
                pick, columns, (((1,), (1,)), ((), ())),
                precision=lax.Precision.HIGHEST, preferred_element_type=F32,
            )
        )
    for layer in range(4):
        base = layer * 144
        for r in range(2):
            left = turned[pl.ds(layer * 4 + r * 2, 32, stride=16), :]
            right = turned[pl.ds(layer * 4 + r * 2 + 1, 32, stride=16), :]
            at = base + r * 64
            main[pl.ds(at, 32, stride=2), :] = jnp.where(low, left, pltpu.roll(right, 64, 1))
            main[pl.ds(at + 1, 32, stride=2), :] = jnp.where(low, pltpu.roll(left, 64, 1), right)
            k = layer * 2 + r
            strip = jnp.where(lane == 0, turn[0][:, 8 + k : 9 + k], 0.0)
            strip = jnp.where(lane == 1, turn[1][:, 8 + k : 9 + k], strip)
            strip = jnp.where(lane == 126, turn[0][:, k : k + 1], strip)
            side[at : at + 64, :] = jnp.where(lane == 127, turn[1][:, k : k + 1], strip)
        block = jnp.zeros((16, 128), F32)
        for kind, first_row in ((0, 14), (1, 0)):
            k = kind * 8 + layer * 2
            a, b = rows[k : k + 1, :], rows[k + 1 : k + 2, :]
            first = jnp.where(low_row, a, pltpu.roll(b, 64, 1))
            second = jnp.where(low_row, pltpu.roll(a, 64, 1), b)
            block = jnp.where(row16 == first_row, first, block)
            block = jnp.where(row16 == first_row + 1, second, block)
        main[base + 128 : base + 144, :] = block
        block = jnp.zeros((16, 128), F32)
        for k, (r, at_lane) in enumerate(((15, 127), (15, 0), (0, 127), (0, 0))):
            value = corners[layer : layer + 1, k : k + 1]
            block = jnp.where((row16 == r) & (lane16 == at_lane), value, block)
        side[base + 128 : base + 144, :] = block
        density[layer * 128 : (layer + 1) * 128, :] = main[base : base + 128, :]
    upper = jnp.where(lax.axis_index("core") == 1, 288, 0)
    lane8 = iota((8, 128), 1)
    for out, first in ((far, upper), (near, 288 - upper)):
        nearest = pl.multiple_of(jnp.where(first == 0, 0, 432), 144)
        first = pl.multiple_of(first, 144)
        out[0:128, :] = main[pl.ds(first, 128), :].astype(BF16)
        out[128:256, :] = main[pl.ds(first + 144, 128), :].astype(BF16)
        out[256:272, :] = main[pl.ds(nearest + 128, 16), :].astype(BF16)
        folded = jnp.zeros((8, 128), F32)
        for k in range(16):
            piece = pltpu.roll(side[pl.ds(nearest + 8 * k, 8), :], 4 * k + 2, 1)
            folded = jnp.where(lane8 >> 2 == k, piece, folded)
        out[272:288, :] = jnp.concatenate([folded, jnp.zeros((8, 128), F32)], axis=0).astype(BF16)


def depth(a):
    return 3 if a < 2 else 2


def beyond(a, layer):
    k = layer - 3 + depth(a) if layer < 3 else layer - 7
    return 3 * a + k if 0 <= k < depth(a) else None


def from_layer(far, near, a, layer, at):
    k = beyond(a, layer)
    if k is None:
        return None
    same, other = (near, far) if layer < 3 else (far, near)
    upper = lax.axis_index("core") == 1
    return jnp.where(upper, same[k, at, :].astype(F32), other[k, at, :].astype(F32))


def layers_kernel(temp, cond, mass, own, far, near, sems):
    upper = lax.axis_index("core") == 1
    copies = [pltpu.make_async_copy(a, own.at[i], sems.at[i]) for i, a in enumerate((temp, cond, mass))]
    for copy in copies:
        copy.start()
    for a, copy in enumerate(copies):
        copy.wait()
        for k in range(depth(a)):
            last, first = own[a, 4 - depth(a) + k], own[a, k]
            far[3 * a + k] = jnp.where(upper, last, first).astype(BF16)
            near[3 * a + k] = jnp.where(upper, first, last).astype(BF16)


def rows_kernel(own, far, near, outer, inner):
    lasts, firsts = [], []
    for a in range(3):
        for layer in range(10):
            if 3 <= layer < 7:
                lasts.append(own[a, layer - 3, 120:128, :])
                firsts.append(own[a, layer - 3, 0:8, :])
            else:
                zeros = jnp.zeros((8, 128), F32)
                ends = from_layer(far, near, a, layer, slice(112, 128))
                lasts.append(zeros if ends is None else ends[8:16])
                ends = from_layer(far, near, a, layer, slice(0, 16))
                firsts.append(zeros if ends is None else ends[0:8])
    last, first = jnp.concatenate(lasts, axis=0), jnp.concatenate(firsts, axis=0)
    odd = is_odd("row")
    outer[...] = jnp.where(odd, last, first).astype(BF16)
    inner[...] = jnp.where(odd, first, last).astype(BF16)


def gather_kernel(own, far, near, outer, inner, out, to_outer, to_inner):
    over, under = sides(is_odd("row"), outer, inner)
    lane = iota((144, 128), 1)
    left, right = jnp.zeros((144, 128), F32), jnp.zeros((144, 128), F32)
    for a in range(3):
        for layer in range(10):
            i = a * 10 + layer
            if 3 <= layer < 7:
                source = own[a, layer - 3]
            else:
                source = from_layer(far, near, a, layer, slice(0, 128))
                source = jnp.zeros((128, 128), F32) if source is None else source
            piece = jnp.concatenate([source, under[8 * i : 8 * i + 8], over[8 * i : 8 * i + 8]], axis=0)
            out[i] = piece
            base = a * 40 + layer * 4
            here = (lane >= base) & (lane < base + 3)
            left = jnp.where(here, pltpu.roll(piece, base, 1) if base else piece, left)
            right = jnp.where(here, pltpu.roll(piece, base + 3, 1), right)
    odd = is_odd("y")
    to_outer[...] = jnp.where(odd, right, left).astype(BF16)
    to_inner[...] = jnp.where(odd, left, right).astype(BF16)


def turned_by(x, shift, axis):
    return pltpu.roll(x, shift % x.shape[axis], axis)


def around(face_row, face_col, v):
    return (
        face_row * turned_by(v, -1, 0)
        + turned_by(face_row * v, 1, 0)
        + face_col * turned_by(v, -1, 1)
        + turned_by(face_col * v, 1, 1)
    )


def operator_kernel(grids, outer, inner, face_layer, face_row, face_col, inverse, residual, wide):
    left, right = sides(is_odd("y"), outer, inner)
    lane = iota((144, 128), 1)
    for a in range(3):
        for layer in range(10):
            i, base = a * 10 + layer, a * 40 + layer * 4
            high = turned_by(right, -base, 1) if base else right
            side = jnp.where(lane < 3, high, jnp.where(lane >= 125, turned_by(left, 125 - base, 1), 0.0))
            wide[i, :, 0:128] = grids[i]
            wide[i, :, 128:256] = side
    for layer in range(9):
        face_layer[layer] = 0.5 * (wide[10 + layer] + wide[11 + layer])
    for layer in range(1, 9):
        temp, cond, mass = (wide[a * 10 + layer] for a in range(3))
        rows = 0.5 * (cond + turned_by(cond, -1, 0))
        cols = 0.5 * (cond + turned_by(cond, -1, 1))
        face_row[layer - 1] = rows
        face_col[layer - 1] = cols
        after, before = face_layer[layer], face_layer[layer - 1]
        diagonal = mass + after + before + rows + turned_by(rows, 1, 0) + cols + turned_by(cols, 1, 1)
        share = after * wide[layer + 1] + before * wide[layer - 1] + around(rows, cols, temp)
        residual[layer - 1] = mass * temp + (share - diagonal * temp)
        inverse[layer - 1] = jnp.where(mass > 0.0, 1.0 / diagonal, 0.0)


MIDDLE = (eig_low + eig_high) / 2.0
SPREAD = (eig_high - eig_low) / 2.0
W0 = SPREAD / MIDDLE
W1 = 1.0 / (2.0 * MIDDLE / SPREAD - W0)
W2 = 1.0 / (2.0 * MIDDLE / SPREAD - W1)


def sweep_kernel(main, side, far, near, grids, face_layer, face_row, face_col, inverse, residual, out, d0, d1, rest):
    lane = iota((8, 128), 1)
    kept = (lane < 2) | (lane >= 126)
    upper = lax.axis_index("core") == 1

    def supplied(i):
        if 3 <= i <= 6:
            at = (i - 3) * 144
            return main[at : at + 144, :], side[at : at + 144, :]
        at = 128 if i in (2, 8) else 0
        same, other = (near, far) if i < 3 else (far, near)

        def rows(at, size):
            return jnp.where(
                upper, same[at : at + size, :].astype(F32), other[at : at + size, :].astype(F32)
            )

        ends = jnp.zeros((16, 128), F32)
        if i in (1, 8):
            return jnp.concatenate([rows(at, 128), ends], axis=0), jnp.zeros((144, 128), F32)
        folded = rows(272, 16)[0:8]
        beside = [jnp.where(kept, turned_by(folded, -4 * k - 2, 1), 0.0) for k in range(16)]
        return (
            jnp.concatenate([rows(at, 128), rows(256, 16)], axis=0),
            jnp.concatenate([*beside, ends], axis=0),
        )

    for i in range(1, 9):
        start = residual[i - 1] + jnp.concatenate(supplied(i), axis=1)
        rest[i - 1] = start
        d0[i - 1] = start * inverse[i - 1] * (1.0 / MIDDLE)

    def share(i, d):
        return (
            face_layer[i] * d[i]
            + face_layer[i - 1] * d[i - 2]
            + around(face_row[i - 1], face_col[i - 1], d[i - 1])
        )

    for i in range(2, 8):
        start = rest[i - 1]
        later = start * (1.0 - 1.0 / MIDDLE) + share(i, d0)
        d1[i - 1] = W1 * W0 * d0[i - 1] + (2.0 * W1 / SPREAD) * (later * inverse[i - 1])
        rest[i - 1] = later - (W1 * W0 / MIDDLE) * start - (2.0 * W1 / SPREAD) * later
    for i in range(3, 7):
        last = rest[i - 1] + share(i, d1)
        step = d0[i - 1] + d1[i - 1] * (1.0 + W2 * W1) + (2.0 * W2 / SPREAD) * (last * inverse[i - 1])
        at = (i - 3) * 128
        out[at : at + 128, :] = grids[i, 0:128, :] + step[0:128, 0:128]


def sds(shape, dtype):
    return jax.ShapeDtypeStruct(shape, dtype)


def call(kernel, shape, args, mib=16, scratch=(), far=(), far_out=False):
    vmem, anywhere = pl.BlockSpec(memory_space=pltpu.VMEM), pl.BlockSpec(memory_space=pltpu.HBM)
    return pl.pallas_call(
        kernel,
        out_shape=shape,
        in_specs=[anywhere if i in far else vmem for i in range(len(args))],
        out_specs=jax.tree.map(lambda _: anywhere if far_out else vmem, shape),
        scratch_shapes=list(scratch),
        compiler_params=pltpu.CompilerParams(vmem_limit_bytes=mib * 2**20),
    )(*args)


def swap_sides(to_outer, to_inner, axis):
    count = lax.axis_size(axis)

    def swapped(data, first):
        apart = [(i, i + 1) for i in range(first, count - 1, 2)]
        return lax.ppermute(data, axis, apart + [(b, a) for a, b in apart])

    return swapped(to_outer, 1), swapped(to_inner, 0)


def is_odd(axis):
    return (lax.axis_index(axis) & 1) == 1


def sides(odd, outer, inner):
    outer, inner = outer[...].astype(F32), inner[...].astype(F32)
    return jnp.where(odd, inner, outer), jnp.where(odd, outer, inner)


def swap_layers(far, near):
    apart = [(i, i + 1) for i in range(1, lax.axis_size(LAYER) - 1, 2)]
    return (
        lax.ppermute(far, LAYER, apart + [(b, a) for a, b in apart]),
        lax.ppermute(near, "core", [(0, 1), (1, 0)]),
    )


def extended_grids(temp, cond, mass):
    eight, rows, edge = sds((8, 128, 128), BF16), sds((240, 128), BF16), sds((144, 128), BF16)
    own, far, near = call(
        layers_kernel,
        (sds((3, 4, 128, 128), F32), eight, eight),
        (temp, cond, mass),
        scratch=[pltpu.SemaphoreType.DMA((3,))],
        far=range(3),
    )
    far, near = swap_layers(far, near)
    beside = swap_sides(*call(rows_kernel, (rows, rows), (own, far, near)), "row")
    wide, *edges = call(
        gather_kernel, (sds((30, 144, 128), F32), edge, edge), (own, far, near, *beside), mib=24
    )
    return wide, beside, swap_sides(*edges, COL)


def operator(wide, outer, inner):
    eight = sds((8, 144, 256), F32)
    return call(
        operator_kernel,
        (sds((9, 144, 256), F32), eight, eight, eight, eight),
        (wide, outer, inner),
        mib=32,
        scratch=[pltpu.VMEM((30, 144, 256), F32)],
    )


def shards(temp, cond, mass, toggling, baseline, panel, place, holder, tier, warming):
    row64 = pltpu.VMEM((1, 64), I32)
    message, placing, columns = call(
        message_kernel,
        (sds((64, 128), F32), sds((1024, 64), BF16), sds((64, 128), I32)),
        (temp, panel.reshape(1, 64), place, holder, tier),
        mib=60,
        scratch=[
            pltpu.VMEM((4, 128, 128), F32), row64, row64, row64,
            pltpu.VMEM((1, 16), I32), pltpu.SemaphoreType.DMA((5,)),
        ],
        far=range(5),
    )
    messages = lax.all_to_all(message.reshape(64, 1, 128), CUBE, split_axis=0, concat_axis=0, tiled=True)
    messages = messages.reshape(64, 128)
    send = call(
        power_kernel,
        sds((256, 4736), BF16),
        (messages, columns, warming, toggling[0], baseline[0], placing),
        mib=60,
        scratch=[
            pltpu.VMEM((64, 128), F32), pltpu.VMEM((64, 128), I32), pltpu.VMEM((1, 16), F32),
            pltpu.VMEM((64, 4096), BF16), pltpu.VMEM((64, 4096), BF16), pltpu.VMEM((1024, 64), BF16),
            pltpu.VMEM((256, 4736), BF16), pltpu.SemaphoreType.DMA((15,)),
        ],
        far=range(6),
        far_out=True,
    )
    received = lax.all_to_all(send.reshape(16, 16, 4736), PLANE, split_axis=0, concat_axis=0, tiled=True)
    wide, rows, beside = extended_grids(temp, cond, mass)
    selector = call(selector_kernel, sds((576, 256), BF16), (messages, *rows))
    partial = call(
        combine_kernel, sds((64, 4480), F32), (selector, received.reshape(256, 4736))
    )
    parts = lax.all_to_all(
        partial.astype(jnp.float16).reshape(4, 16, 4480), "zlo", split_axis=0, concat_axis=0, tiled=True
    )
    terms = operator(wide, *beside)
    block, strip = sds((576, 128), F32), sds((288, 128), BF16)
    density, main, side, far, near = call(
        unpack_kernel,
        (sds((512, 128), F32), block, block, strip, strip),
        (jnp.sum(parts.astype(F32), axis=0), *beside),
        scratch=[pltpu.VMEM((528, 128), F32)],
    )
    far, near = swap_layers(far, near)
    eight = pltpu.VMEM((8, 144, 256), F32)
    guess = call(
        sweep_kernel,
        sds((512, 128), F32),
        (main, side, far, near, wide, *terms),
        mib=40,
        scratch=[eight, eight, eight],
    )
    return guess.reshape(4, 128, 128), density.reshape(4, 128, 128)


def solution(mesh):
    fine = Mesh(mesh.devices.reshape(4, 4, 4, 4, 2), ("row", "zlo", "y", "zhi", "core"))
    grid = P(LAYER, "row", COL)
    slot = ("row", "zlo", "y", "zhi", "core")
    return jax.shard_map(
        shards,
        mesh=fine,
        in_specs=(
            grid,
            grid,
            grid,
            P(slot, None, None),
            P(slot, None, None),
            P(slot, None, None),
            P(slot, None),
            P(slot, None),
            P(slot, None),
            P(slot, None),
        ),
        out_specs=(grid, grid),
        check_vma=False,
    )
```
